256 devices in a mesh: ctx: 16 (over x_hi, z), head: 2 (over core), exp: 8 (over y, x_lo).
Axes of the slice: x: 4 (x_hi: 2, x_lo: 2; x = x_hi * 2 + x_lo), y: 4, z: 8, core: 2. Of those that a mesh axis runs over, the one named last changes fastest.
Arguments:
- queries: bfloat16 [4096, 32, 128], P('ctx', ('head', 'exp')), may hold values from -6 to 6
- key_rows: bfloat16 [4096, 2, 128], P(('ctx', 'exp'), 'head'), may hold values from -6 to 6
- value_vector_rows: bfloat16 [4096, 2, 128], P(('ctx', 'exp'), 'head'), may hold values from -6 to 6
- grad_attn: bfloat16 [4096, 32, 128], P('ctx', ('head', 'exp')), may hold values from -6 to 6
- moe_input: bfloat16 [4096, 4096], P('exp', 'ctx'), may hold values from -6 to 6
- moe_grad: bfloat16 [4096, 4096], P('exp', 'ctx'), may hold values from -6 to 6
- expert_ids: int32 [4096, 8], P('exp'), may hold values from 0 to 127, as said below
- router_weight: float32 [4096, 8], P('exp'), may hold values from 0.02 to 0.5
- gate_weight: bfloat16 [8, 4096, 1536], P('exp', 'ctx'), may hold values from -0.09375 to 0.09375
- up_weight: bfloat16 [8, 4096, 1536], P('exp', 'ctx'), may hold values from -0.09375 to 0.09375
- down_weight: bfloat16 [8, 1536, 4096], P('exp', None, 'ctx'), may hold values from -0.15625 to 0.15625
Outputs:
- grad_query: bfloat16 [4096, 32, 128], P('ctx', ('head', 'exp'))
- grad_key: bfloat16 [4096, 2, 128], P(('ctx', 'exp'), 'head')
- grad_value: bfloat16 [4096, 2, 128], P(('ctx', 'exp'), 'head')
- grad_input: bfloat16 [4096, 4096], P('exp', ('ctx', 'head'))
- grad_gate: bfloat16 [8, 4096, 1536], P('exp', 'ctx', 'head')
- grad_up: bfloat16 [8, 4096, 1536], P('exp', 'ctx', 'head')
- grad_down: bfloat16 [8, 1536, 4096], P('exp', 'head', 'ctx')
The draws below stay inside these ranges and needn't reach their ends.
Inputs may be any that keep to these rules, and one draw needn't show every extreme that they name: `expert_ids`: each row names 8 different experts. In each aligned block of 512 rows every expert below 8 is named by at most 48 rows, and some expert below 8 is named by exactly 48 rows in every block.
All inputs are finite; a program needn't handle non-finite values.
Results may differ from the reference program's by a relative error of at most 0.0083.
Values may be sent and summed in bfloat16 or wider, within the bound.
No kernel may reach another device: no remote copies, remote signals or barrier semaphores. Data moves between devices by JAX's collectives and lax.ppermute only.
A program may use at most 128 MiB of HBM per device.

```python
import math
import jax
import jax.numpy as jnp
from jax import lax

D = 4096
FF = 1536
QUERY_HEADS = 32
KEY_VALUE_HEADS = 2
HEAD_SIZE = 128
EXPERTS = 128
TOPK = 8
CAP = 48
TOK = 256
SEQUENCE_LENGTH = 4096
BLK = 512
W_EXP = 8


def draw_queries(key, part):
    key = jax.random.fold_in(key, 1)
    primary_random_key, secondary_random_key = jax.random.split(key)
    scale_factors = jnp.exp(jax.random.uniform(secondary_random_key, (SEQUENCE_LENGTH, QUERY_HEADS, 1), minval=math.log(0.4), maxval=math.log(2.0)))
    sampled_draws = jax.random.normal(primary_random_key, (SEQUENCE_LENGTH, QUERY_HEADS, HEAD_SIZE)) * scale_factors
    return jnp.clip(sampled_draws, -6.0, 6.0).astype(jnp.bfloat16)


def draw_key_rows(key, part):
    key = jax.random.fold_in(key, 2)
    primary_random_key, secondary_random_key = jax.random.split(key)
    scale_factors = jnp.exp(jax.random.uniform(secondary_random_key, (SEQUENCE_LENGTH, KEY_VALUE_HEADS, 1), minval=math.log(0.5), maxval=math.log(1.5)))
    sampled_draws = jax.random.normal(primary_random_key, (SEQUENCE_LENGTH, KEY_VALUE_HEADS, HEAD_SIZE)) * scale_factors
    return jnp.clip(sampled_draws, -6.0, 6.0).astype(jnp.bfloat16)


def draw_expert_ids(key, part):
    key = jax.random.fold_in(key, 3)
    subkeys = jax.random.split(key, 5)
    blocks = SEQUENCE_LENGTH // BLK
    counts = jax.random.randint(subkeys[0], (blocks, W_EXP), CAP // 4, CAP + 1)
    labels = jnp.arange(W_EXP)
    always_full = jax.random.randint(subkeys[1], (), 0, W_EXP)
    block_full = jax.random.randint(subkeys[2], (blocks,), 0, W_EXP)
    full_mask = (labels[None, :] == always_full) | (labels[None, :] == block_full[:, None])
    counts = jnp.where(full_mask, CAP, counts)
    orders = jax.vmap(lambda sub: jax.random.permutation(sub, BLK))(jax.random.split(subkeys[3], blocks * W_EXP))
    orders = orders.reshape(blocks, W_EXP, BLK)
    chosen = orders < counts[:, :, None]
    chosen = jnp.transpose(chosen, (0, 2, 1)).reshape(SEQUENCE_LENGTH, W_EXP)
    scores = jax.random.randint(subkeys[4], (SEQUENCE_LENGTH, EXPERTS), 0, 2 ** 20) * 256 + jnp.arange(EXPERTS)[None, :]
    window = jnp.where(chosen, 2 ** 29 + labels[None, :], -1 - labels[None, :])
    scores = scores.at[:, :W_EXP].set(window)
    top_scores, picked = lax.top_k(scores, TOPK)
    return picked.astype(jnp.int32)


def shard_levels(rng, dims, shards, least, largest):
    def one(axis_at, blocks):
        heights = jax.random.uniform(jax.random.fold_in(jax.random.fold_in(rng, 6), axis_at), (blocks,), jnp.float32, least / len(shards), largest / len(shards))
        return jnp.repeat(jnp.exp(heights), dims[axis_at] // blocks).reshape((-1,) + (1,) * (len(dims) - axis_at - 1))

    loudness = one(*shards[0])
    for cut in shards[1:]:
        loudness = loudness * one(*cut)
    return loudness


def centred(own_key, dims, deviation, limit, cuts=(), held_as=jnp.bfloat16):
    level = shard_levels(own_key, dims, cuts, -0.22, 0.18) if cuts else 1.0
    array = jax.random.normal(own_key, dims, jnp.float32) * deviation * level
    return jnp.minimum(jnp.maximum(array, -limit), limit).astype(held_as)


def setup_inputs(seed: int = 0) -> dict:
    splits = jax.random.split(jax.random.key(seed), 12)
    return {
        "queries": draw_queries(jax.random.fold_in(splits[11], 71), 0),
        "key_rows": draw_key_rows(jax.random.fold_in(splits[11], 71), 0),
        "value_vector_rows": centred(splits[2], (SEQUENCE_LENGTH, KEY_VALUE_HEADS, HEAD_SIZE), 1.0, 6.0, ((0, 128), (1, 2))),
        "grad_attn": centred(splits[3], (SEQUENCE_LENGTH, QUERY_HEADS, HEAD_SIZE), 1.0, 6.0, ((0, 16), (1, 16))),
        "moe_input": centred(splits[4], (SEQUENCE_LENGTH, D), 1.0, 6.0, ((0, 8), (1, 16))),
        "moe_grad": centred(splits[5], (SEQUENCE_LENGTH, D), 1.0, 6.0, ((0, 8), (1, 16))),
        "expert_ids": draw_expert_ids(jax.random.fold_in(splits[11], 71), 0),
        "router_weight": jnp.clip(0.02 + 0.48 * jax.random.uniform(splits[7], (SEQUENCE_LENGTH, TOPK), jnp.float32) ** shard_levels(splits[7], (SEQUENCE_LENGTH, TOPK), ((0, 8),), -0.2, 0.2), 0.02, 0.5),
        "gate_weight": centred(splits[8], (W_EXP, D, FF), D ** -0.5, 0.09375, ((0, 8), (1, 16))),
        "up_weight": centred(splits[9], (W_EXP, D, FF), D ** -0.5, 0.09375, ((0, 8), (1, 16))),
        "down_weight": centred(splits[10], (W_EXP, FF, D), FF ** -0.5, 0.15625, ((0, 8), (2, 16))),
    }


def reference(queries, key_rows, value_vector_rows, grad_attn, moe_input, moe_grad, expert_ids, router_weight, gate_weight, up_weight, down_weight):
    inv_root = HEAD_SIZE ** -0.5
    query_group_count = QUERY_HEADS // KEY_VALUE_HEADS
    keys_full = jnp.repeat(key_rows, query_group_count, axis=1).astype(jnp.float32)
    values_full = jnp.repeat(value_vector_rows, query_group_count, axis=1).astype(jnp.float32)
    key_pos = jnp.arange(SEQUENCE_LENGTH)

    def attend(running, block_index):
        key_gradient_rows, value_gradient_rows = running
        row_start = block_index * TOK
        query_part = lax.dynamic_slice_in_dim(queries, row_start, TOK, 0).astype(jnp.float32)
        grad_part = lax.dynamic_slice_in_dim(grad_attn, row_start, TOK, 0).astype(jnp.float32)
        query_pos = row_start + jnp.arange(TOK)
        allowed = key_pos[None, :] <= query_pos[:, None]
        scores = jnp.einsum("phd,thd->hpt", query_part, keys_full) * inv_root
        scores = jnp.where(allowed[None], scores, -jnp.inf)
        probs_full = jax.nn.softmax(scores, axis=-1)
        probs_low = probs_full.astype(jnp.bfloat16)
        attn_out = jnp.einsum("hpt,thd->phd", probs_low.astype(jnp.float32), values_full)
        row_delta = jnp.sum(grad_part * attn_out, axis=-1)
        grad_prob = jnp.einsum("phd,thd->hpt", grad_part, values_full)
        dscore = (probs_full * (grad_prob - jnp.transpose(row_delta)[:, :, None])).astype(jnp.bfloat16)
        dscore_wide = dscore.astype(jnp.float32)
        grad_q = (jnp.einsum("hpt,thd->phd", dscore_wide, keys_full) * inv_root).astype(jnp.bfloat16)
        key_gradient_terms = jnp.einsum("hpt,phd->thd", dscore_wide, query_part)
        value_gradient_terms = jnp.einsum("hpt,phd->thd", probs_low.astype(jnp.float32), grad_part)
        key_gradient_rows = key_gradient_rows + key_gradient_terms.reshape(SEQUENCE_LENGTH, KEY_VALUE_HEADS, query_group_count, HEAD_SIZE).sum(axis=2)
        value_gradient_rows = value_gradient_rows + value_gradient_terms.reshape(SEQUENCE_LENGTH, KEY_VALUE_HEADS, query_group_count, HEAD_SIZE).sum(axis=2)
        return (key_gradient_rows, value_gradient_rows), grad_q

    empty_key_value = jnp.zeros((SEQUENCE_LENGTH, KEY_VALUE_HEADS, HEAD_SIZE), jnp.float32)
    (key_gradient_rows, value_gradient_rows), grad_blocks = lax.scan(attend, (empty_key_value, empty_key_value), jnp.arange(SEQUENCE_LENGTH // TOK))
    grad_query = grad_blocks.reshape(SEQUENCE_LENGTH, QUERY_HEADS, HEAD_SIZE)
    grad_key = (key_gradient_rows * inv_root).astype(jnp.bfloat16)
    grad_value = value_gradient_rows.astype(jnp.bfloat16)

    blocks = SEQUENCE_LENGTH // BLK
    slot_ids = jnp.arange(CAP)

    def expert_step(grad_total, packed):
        expert, gate_mat, up_mat, down_mat = packed
        matches = expert_ids == expert
        in_expert = jnp.any(matches, axis=1)
        weight_row = jnp.sum(jnp.where(matches, router_weight, 0.0), axis=1)
        member = in_expert.reshape(blocks, BLK).astype(jnp.int32)
        slot_rank = jnp.cumsum(member, axis=1) - member
        slot_hit = (member[:, :, None] == 1) & (slot_rank[:, :, None] == slot_ids[None, None, :])
        row_token = jnp.sum(jnp.where(slot_hit, jnp.arange(BLK)[None, :, None], 0), axis=1)
        row_token = (row_token + (jnp.arange(blocks) * BLK)[:, None]).reshape(-1)
        row_valid = jnp.any(slot_hit, axis=1).reshape(-1)
        input_rows = moe_input[row_token]
        scaled = weight_row[row_token][:, None] * moe_grad[row_token].astype(jnp.float32)
        grad_rows = jnp.where(row_valid[:, None], scaled, 0.0).astype(jnp.bfloat16)
        gate_val = jnp.dot(input_rows, gate_mat, preferred_element_type=jnp.float32)
        up_val = jnp.dot(input_rows, up_mat, preferred_element_type=jnp.float32)
        back_val = jnp.dot(grad_rows, down_mat.T, preferred_element_type=jnp.float32)
        sigmoid_gate = jax.nn.sigmoid(gate_val)
        hidden = (gate_val * sigmoid_gate * up_val).astype(jnp.bfloat16)
        d_up = (back_val * gate_val * sigmoid_gate).astype(jnp.bfloat16)
        d_gate = (back_val * up_val * sigmoid_gate * (1.0 + gate_val * (1.0 - sigmoid_gate))).astype(jnp.bfloat16)
        new_gate = jnp.dot(input_rows.T, d_gate, preferred_element_type=jnp.float32).astype(jnp.bfloat16)
        new_up = jnp.dot(input_rows.T, d_up, preferred_element_type=jnp.float32).astype(jnp.bfloat16)
        new_down = jnp.dot(hidden.T, grad_rows, preferred_element_type=jnp.float32).astype(jnp.bfloat16)
        contrib = (jnp.dot(d_gate, gate_mat.T, preferred_element_type=jnp.float32) + jnp.dot(d_up, up_mat.T, preferred_element_type=jnp.float32)).astype(jnp.bfloat16)
        grad_total = grad_total.at[row_token].add(jnp.where(row_valid[:, None], contrib.astype(jnp.float32), 0.0))
        return grad_total, (new_gate, new_up, new_down)

    start_total = jnp.zeros((SEQUENCE_LENGTH, D), jnp.float32)
    grad_total, (grad_gate, grad_up, grad_down) = lax.scan(expert_step, start_total, (jnp.arange(W_EXP).astype(jnp.int32), gate_weight, up_weight, down_weight))
    grad_input = grad_total.astype(jnp.bfloat16)
    return grad_query, grad_key, grad_value, grad_input, grad_gate, grad_up, grad_down
```

```python
import jax
import jax.numpy as jnp
from jax import lax
from jax.sharding import PartitionSpec as P

CAP = 48
BF = jnp.bfloat16
F32 = jnp.float32


def activate(gate_val, up_val, back_val):
    sigmoid_gate = jax.nn.sigmoid(gate_val)
    hidden = (gate_val * sigmoid_gate * up_val).astype(BF)
    d_up = (back_val * gate_val * sigmoid_gate).astype(BF)
    d_gate = (back_val * up_val * sigmoid_gate * (1.0 + gate_val * (1.0 - sigmoid_gate))).astype(BF)
    return (hidden, d_gate, d_up)


def spread(block, axis):
    n = lax.axis_size(axis)
    copies = jnp.broadcast_to(block[None], (n,) + block.shape)
    return lax.all_to_all(copies, axis, 0, 0, tiled=True)


def gather_sum(parts, axis):
    return jnp.sum(lax.all_to_all(parts, axis, 0, 0, tiled=True).astype(F32), axis=0)


def attention(queries, key_rows, value_vector_rows, grad_attn):
    tok_rows = queries.shape[0]
    head_dim = queries.shape[2]
    inv_root = head_dim ** (-0.5)
    ctx_size, exp_size = lax.axis_size("ctx"), lax.axis_size("exp")
    own = key_rows.shape[0]
    pair = jnp.concatenate([key_rows[:, 0, :], value_vector_rows[:, 0, :]], axis=1)
    everyone = spread(spread(pair, "ctx"), "exp")
    flat = everyone.reshape(-1, 2 * head_dim)
    key_flat, value_flat = flat[:, :head_dim], flat[:, head_dim:]
    place = jnp.arange(flat.shape[0])
    key_pos = (
        (place // own) % ctx_size * (own * exp_size) + place // (own * ctx_size) * own + place % own
    )
    query_pos = lax.axis_index("ctx") * tok_rows + jnp.arange(tok_rows)
    allowed = key_pos[None, :] <= query_pos[:, None]
    scores = (
        jnp.einsum("phd,td->hpt", queries, key_flat, preferred_element_type=F32) * inv_root
    )
    scores = jnp.where(allowed[None], scores, -jnp.inf)
    probs_full = jax.nn.softmax(scores, axis=-1)
    probs_low = probs_full.astype(BF)
    attn_out = jnp.einsum("hpt,td->phd", probs_low, value_flat, preferred_element_type=F32)
    row_delta = jnp.sum(grad_attn.astype(F32) * attn_out, axis=-1)
    grad_prob = jnp.einsum("phd,td->hpt", grad_attn, value_flat, preferred_element_type=F32)
    dscore = (probs_full * (grad_prob - jnp.transpose(row_delta)[:, :, None])).astype(BF)
    grad_query = (
        jnp.einsum("hpt,td->phd", dscore, key_flat, preferred_element_type=F32) * inv_root
    ).astype(BF)
    key_grad = jnp.einsum("hpt,phd->td", dscore, queries, preferred_element_type=F32)
    value_grad = jnp.einsum("hpt,phd->td", probs_low, grad_attn, preferred_element_type=F32)
    both = jnp.concatenate([key_grad.astype(BF), value_grad.astype(BF)], axis=1)
    both = gather_sum(both.reshape(exp_size, ctx_size * own, 2 * head_dim), "exp").astype(BF)
    summed = gather_sum(both.reshape(ctx_size, own, 2 * head_dim), "ctx")
    grad_key = (summed[:, :head_dim] * inv_root).astype(BF)[:, None, :]
    grad_value = summed[:, head_dim:].astype(BF)[:, None, :]
    return grad_query, grad_key, grad_value


def experts(moe_input, moe_grad, expert_ids, router_weight, gate_weight, up_weight, down_weight):
    width = moe_input.shape[1]
    exp_size, ctx_size, head_size = (lax.axis_size(a) for a in ("exp", "ctx", "head"))
    half = lax.axis_index("head")
    units = gate_weight.shape[2] // head_size
    columns = width // head_size
    matches = expert_ids[:, :, None] == jnp.arange(exp_size)[None, None, :]
    member = jnp.sum(matches.astype(jnp.int32), axis=1)
    weight_row = jnp.sum(jnp.where(matches, router_weight[:, :, None], 0.0), axis=1)
    slot_rank = jnp.cumsum(member, axis=0) - member
    placed = (member[:, :, None] == 1) & (
        slot_rank[:, :, None] == jnp.arange(CAP)[None, None, :]
    )
    slot_weight = jnp.sum(jnp.where(placed, weight_row[:, :, None], 0.0), axis=0)
    placed_low = placed.astype(BF).reshape(-1, exp_size * CAP)
    rows = jnp.concatenate([moe_input, moe_grad], axis=1)
    picked = jnp.einsum("bs,bd->sd", placed_low, rows, preferred_element_type=F32)
    scaled = picked[:, width:] * slot_weight.reshape(-1, 1)
    sent = jnp.concatenate([picked[:, :width].astype(BF), scaled.astype(BF)], axis=1)
    got = lax.all_to_all(sent.reshape(exp_size, CAP, 2 * width), "exp", 0, 0, tiled=True)
    got = got.reshape(exp_size * CAP, 2 * width)
    input_rows, grad_rows = got[:, :width], got[:, width:]
    gate_mat = lax.dynamic_slice_in_dim(gate_weight[0], half * units, units, 1)
    up_mat = lax.dynamic_slice_in_dim(up_weight[0], half * units, units, 1)
    down_mat = lax.dynamic_slice_in_dim(down_weight[0], half * units, units, 0)
    gate_part = jnp.dot(input_rows, gate_mat, preferred_element_type=F32).astype(BF)
    up_part = jnp.dot(input_rows, up_mat, preferred_element_type=F32).astype(BF)
    back_part = jnp.einsum("rd,fd->rf", grad_rows, down_mat, preferred_element_type=F32).astype(BF)
    parts = jnp.concatenate([gate_part, up_part, back_part], axis=1)
    total = gather_sum(parts.reshape(ctx_size, -1, 3 * units), "ctx")
    hidden, d_gate, d_up = activate(
        total[:, :units], total[:, units : 2 * units], total[:, 2 * units :]
    )
    full = spread(jnp.concatenate([hidden, d_gate, d_up], axis=1), "ctx").reshape(-1, 3 * units)
    hidden, d_gate, d_up = full[:, :units], full[:, units : 2 * units], full[:, 2 * units :]
    contrib = jnp.einsum("rf,df->rd", d_gate, gate_mat, preferred_element_type=F32)
    contrib = contrib + jnp.einsum("rf,df->rd", d_up, up_mat, preferred_element_type=F32)
    mine = lax.dynamic_slice_in_dim(contrib, half * columns, columns, 1)
    other = lax.dynamic_slice_in_dim(contrib, (1 - half) * columns, columns, 1).astype(BF)
    mine = (mine + lax.ppermute(other, "head", [(0, 1), (1, 0)]).astype(F32)).astype(BF)
    back_rows = lax.all_to_all(mine.reshape(exp_size, CAP, columns), "exp", 0, 0, tiled=True)
    grad_input = jnp.dot(
        placed_low, back_rows.reshape(-1, columns), preferred_element_type=F32
    ).astype(BF)
    grad_gate = jnp.einsum("rd,rf->df", input_rows, d_gate, preferred_element_type=F32).astype(BF)
    grad_up = jnp.einsum("rd,rf->df", input_rows, d_up, preferred_element_type=F32).astype(BF)
    grad_down = jnp.einsum("rf,rd->fd", hidden, grad_rows, preferred_element_type=F32).astype(BF)
    return grad_input, grad_gate[None], grad_up[None], grad_down[None]


def shards(
    queries,
    key_rows,
    value_vector_rows,
    grad_attn,
    moe_input,
    moe_grad,
    expert_ids,
    router_weight,
    gate_weight,
    up_weight,
    down_weight,
):
    of_attention = attention(queries, key_rows, value_vector_rows, grad_attn)
    of_experts = experts(
        moe_input, moe_grad, expert_ids, router_weight, gate_weight, up_weight, down_weight
    )
    return of_attention + of_experts


def solution(mesh):
    placed = (
        P("ctx", ("head", "exp"), None),
        P(("ctx", "exp"), "head", None),
        P(("ctx", "exp"), "head", None),
        P("ctx", ("head", "exp"), None),
        P("exp", "ctx"),
        P("exp", "ctx"),
        P("exp", None),
        P("exp", None),
        P("exp", "ctx", None),
        P("exp", "ctx", None),
        P("exp", None, "ctx"),
    )
    return jax.shard_map(
        shards,
        mesh=mesh,
        in_specs=placed,
        out_specs=(
            P("ctx", ("head", "exp"), None),
            P(("ctx", "exp"), "head", None),
            P(("ctx", "exp"), "head", None),
            P("exp", ("ctx", "head")),
            P("exp", "ctx", "head"),
            P("exp", "ctx", "head"),
            P("exp", "head", "ctx"),
        ),
        check_vma=False,
    )
```

```python
import jax
import jax.numpy as jnp
from jax import lax
from jax.sharding import PartitionSpec as P

CAP = 48
X_HI = 2
BF = jnp.bfloat16
F32 = jnp.float32


def activate(gate_val, up_val, back_val):
    sigmoid_gate = jax.nn.sigmoid(gate_val)
    hidden = (gate_val * sigmoid_gate * up_val).astype(BF)
    d_up = (back_val * gate_val * sigmoid_gate).astype(BF)
    d_gate = (back_val * up_val * sigmoid_gate * (1.0 + gate_val * (1.0 - sigmoid_gate))).astype(BF)
    return (hidden, d_gate, d_up)


def spread(block, axis):
    n = lax.axis_size(axis)
    copies = jnp.broadcast_to(block[None], (n,) + block.shape)
    return lax.all_to_all(copies, axis, 0, 0, tiled=True)


def gather_sum(parts, axis):
    return jnp.sum(lax.all_to_all(parts, axis, 0, 0, tiled=True).astype(F32), axis=0)


def z_shift(step):
    n = lax.axis_size("ctx") // X_HI
    return [(h * n + z, h * n + (z + step) % n) for h in range(X_HI) for z in range(n)]


def right(block):
    return lax.ppermute(block, "ctx", z_shift(1))


def left(block):
    return lax.ppermute(block, "ctx", z_shift(-1))


def opposite(block):
    n = lax.axis_size("ctx")
    return lax.ppermute(block, "ctx", [(c, (c + n // X_HI) % n) for c in range(n)])


def after(block, *others):
    return lax.optimization_barrier((block,) + others)[0]


def add_low(a, b):
    return (a.astype(F32) + b.astype(F32)).astype(BF)


def ring_sum(parts, beside):
    n = len(parts)
    far = n // 2
    cut = parts[0].shape[1] // 2
    onward, back = parts[far][:, :cut], parts[far][:, cut:]
    for step in range(far):
        if step in beside:
            onward, back = after(onward, beside[step]), after(back, beside[step])
        onward, back = right(onward), left(back)
        ahead, behind = parts[far - 1 - step], parts[(far + 1 + step) % n]
        if step == 0:
            onward = jnp.concatenate([add_low(onward, ahead[:, :cut]), ahead[:, cut:]], axis=1)
            back = jnp.concatenate([behind[:, :cut], add_low(back, behind[:, cut:])], axis=1)
        elif step < far - 1:
            onward, back = add_low(onward, ahead), add_low(back, behind)
    return onward.astype(F32) + back.astype(F32) + parts[0].astype(F32)


def ring_gather(block, beside=()):
    n = lax.axis_size("ctx") // X_HI
    far = n // 2
    cut = block.shape[1] // 2
    blocks = [block] + [None] * (n - 1)
    onward = back = block
    for step in range(1, far):
        if step in beside:
            onward, back = after(onward, beside[step]), after(back, beside[step])
        onward, back = right(onward), left(back)
        blocks[n - step], blocks[step] = onward, back
    blocks[far] = jnp.concatenate([right(onward[:, :cut]), left(back[:, cut:])], axis=1)
    return blocks


def turn(blocks, places):
    twice = jnp.concatenate([blocks, blocks], axis=0)
    return lax.dynamic_slice_in_dim(twice, places, blocks.shape[0], 0)


def ctx_gather(key_rows, value_vector_rows):
    n = lax.axis_size("ctx") // X_HI
    side = lax.axis_index("ctx") // n
    pair = jnp.concatenate([key_rows[:, 0, :], value_vector_rows[:, 0, :]], axis=1)
    partner = opposite(pair)
    first, second = jnp.where(side == 0, pair, partner), jnp.where(side == 0, partner, pair)
    return jnp.concatenate(ring_gather(jnp.concatenate([first, second], axis=0)), axis=0)


def attention(queries, flat, grad_attn):
    tok_rows = queries.shape[0]
    head_dim = queries.shape[2]
    inv_root = head_dim ** (-0.5)
    ctx_size, exp_size = lax.axis_size("ctx"), lax.axis_size("exp")
    own = flat.shape[0] // (ctx_size * exp_size)
    key_flat, value_flat = flat[:, :head_dim], flat[:, head_dim:]
    ring = ctx_size // X_HI
    at = lax.axis_index("ctx") % ring
    place = jnp.arange(flat.shape[0])
    of_ctx = place // own % X_HI * ring + (place // (own * X_HI) + at) % ring
    key_pos = (of_ctx * exp_size + place // (own * ctx_size)) * own + place % own
    query_pos = lax.axis_index("ctx") * tok_rows + jnp.arange(tok_rows)
    allowed = key_pos[None, :] <= query_pos[:, None]
    scores = (
        jnp.einsum("phd,td->hpt", queries, key_flat, preferred_element_type=F32) * inv_root
    )
    scores = jnp.where(allowed[None], scores, -jnp.inf)
    probs_full = jax.nn.softmax(scores, axis=-1)
    probs_low = probs_full.astype(BF)
    attn_out = jnp.einsum("hpt,td->phd", probs_low, value_flat, preferred_element_type=F32)
    row_delta = jnp.sum(grad_attn.astype(F32) * attn_out, axis=-1)
    grad_prob = jnp.einsum("phd,td->hpt", grad_attn, value_flat, preferred_element_type=F32)
    dscore = (probs_full * (grad_prob - jnp.transpose(row_delta)[:, :, None])).astype(BF)
    grad_query = (
        jnp.einsum("hpt,td->phd", dscore, key_flat, preferred_element_type=F32) * inv_root
    ).astype(BF)
    key_grad = jnp.einsum("hpt,phd->td", dscore, queries, preferred_element_type=F32)
    value_grad = jnp.einsum("hpt,phd->td", probs_low, grad_attn, preferred_element_type=F32)
    both = jnp.concatenate([key_grad.astype(BF), value_grad.astype(BF)], axis=1)
    return both, probs_low, grad_query


def to_owners(both):
    ctx_size = lax.axis_size("ctx")
    ring, head_dim = ctx_size // X_HI, both.shape[1] // 2
    own = both.shape[0] // ctx_size
    at = lax.axis_index("ctx") % ring
    both = turn(both.reshape(ring, X_HI, own, 2 * head_dim), (ring - at) % ring)
    both = jnp.swapaxes(both, 0, 1).reshape(ctx_size, own, 2 * head_dim)
    summed = gather_sum(both, "ctx")
    grad_key = (summed[:, :head_dim] * head_dim ** (-0.5)).astype(BF)[:, None, :]
    grad_value = summed[:, head_dim:].astype(BF)[:, None, :]
    return grad_key, grad_value


def select(moe_input, moe_grad, expert_ids, router_weight):
    width = moe_input.shape[1]
    exp_size = lax.axis_size("exp")
    matches = expert_ids[:, :, None] == jnp.arange(exp_size)[None, None, :]
    member = jnp.sum(matches.astype(jnp.int32), axis=1)
    weight_row = jnp.sum(jnp.where(matches, router_weight[:, :, None], 0.0), axis=1)
    slot_rank = jnp.cumsum(member, axis=0) - member
    placed = (member[:, :, None] == 1) & (
        slot_rank[:, :, None] == jnp.arange(CAP)[None, None, :]
    )
    slot_weight = jnp.sum(jnp.where(placed, weight_row[:, :, None], 0.0), axis=0)
    placed_low = placed.astype(BF).reshape(-1, exp_size * CAP)
    rows = jnp.concatenate([moe_input, moe_grad], axis=1)
    picked = jnp.einsum("bs,bd->sd", placed_low, rows, preferred_element_type=F32)
    scaled = picked[:, width:] * slot_weight.reshape(-1, 1)
    sent = jnp.concatenate([picked[:, :width].astype(BF), scaled.astype(BF)], axis=1)
    got = lax.all_to_all(sent.reshape(exp_size, CAP, 2 * width), "exp", 0, 0, tiled=True)
    return placed_low, got


def project(got, gate_weight, up_weight, down_weight):
    ring = lax.axis_size("ctx") // X_HI
    at = lax.axis_index("ctx") % ring
    half = lax.axis_index("head")
    units = gate_weight.shape[2] // lax.axis_size("head")
    width = got.shape[2] // 2
    got = turn(got.reshape(ring, -1, 2 * width), at).reshape(-1, 2 * width)
    input_rows, grad_rows = got[:, :width], got[:, width:]
    gate_mat = lax.dynamic_slice_in_dim(gate_weight[0], half * units, units, 1)
    up_mat = lax.dynamic_slice_in_dim(up_weight[0], half * units, units, 1)
    down_mat = lax.dynamic_slice_in_dim(down_weight[0], half * units, units, 0)
    gate_part = jnp.dot(input_rows, gate_mat, preferred_element_type=F32).astype(BF)
    up_part = jnp.dot(input_rows, up_mat, preferred_element_type=F32).astype(BF)
    back_part = jnp.einsum("rd,fd->rf", grad_rows, down_mat, preferred_element_type=F32).astype(BF)
    parts = jnp.concatenate([gate_part, up_part, back_part], axis=1).reshape(ring, -1, 3 * units)
    return input_rows, grad_rows, gate_mat, up_mat, [parts[j] for j in range(ring)]


def act_block(total):
    units = total.shape[1] // 3
    total = total + opposite(total.astype(BF)).astype(F32)
    hidden, d_gate, d_up = activate(
        total[:, :units], total[:, units : 2 * units], total[:, 2 * units :]
    )
    return jnp.concatenate([hidden, d_gate, d_up], axis=1)


def finish(full, input_rows, grad_rows, gate_mat, up_mat, placed_low):
    exp_size, head_size = lax.axis_size("exp"), lax.axis_size("head")
    ring = lax.axis_size("ctx") // X_HI
    at = lax.axis_index("ctx") % ring
    half = lax.axis_index("head")
    units = full.shape[1] // 3
    columns = input_rows.shape[1] // head_size
    hidden, d_gate, d_up = full[:, :units], full[:, units : 2 * units], full[:, 2 * units :]
    contrib = jnp.einsum("rf,df->rd", d_gate, gate_mat, preferred_element_type=F32)
    contrib = contrib + jnp.einsum("rf,df->rd", d_up, up_mat, preferred_element_type=F32)
    mine = lax.dynamic_slice_in_dim(contrib, half * columns, columns, 1)
    other = lax.dynamic_slice_in_dim(contrib, (1 - half) * columns, columns, 1).astype(BF)
    mine = (mine + lax.ppermute(other, "head", [(0, 1), (1, 0)]).astype(F32)).astype(BF)
    mine = turn(mine.reshape(ring, -1, columns), (ring - at) % ring).reshape(exp_size, CAP, columns)
    back_rows = lax.all_to_all(mine, "exp", 0, 0, tiled=True)
    grad_input = jnp.dot(
        placed_low, back_rows.reshape(-1, columns), preferred_element_type=F32
    ).astype(BF)
    grad_gate = jnp.einsum("rd,rf->df", input_rows, d_gate, preferred_element_type=F32).astype(BF)
    grad_up = jnp.einsum("rd,rf->df", input_rows, d_up, preferred_element_type=F32).astype(BF)
    grad_down = jnp.einsum("rf,rd->fd", hidden, grad_rows, preferred_element_type=F32).astype(BF)
    return grad_input, grad_gate[None], grad_up[None], grad_down[None]


def shards(
    queries,
    key_rows,
    value_vector_rows,
    grad_attn,
    moe_input,
    moe_grad,
    expert_ids,
    router_weight,
    gate_weight,
    up_weight,
    down_weight,
):
    near = ctx_gather(key_rows, value_vector_rows)
    placed_low, got = select(moe_input, moe_grad, expert_ids, router_weight)
    got, near = lax.optimization_barrier((got, near))
    flat = spread(near, "exp").reshape(-1, near.shape[1])
    input_rows, grad_rows, gate_mat, up_mat, parts = project(
        got, gate_weight, up_weight, down_weight
    )
    both, probs_low, grad_query = attention(queries, flat, grad_attn)
    exp_size = lax.axis_size("exp")
    total = ring_sum(parts, {3: flat})
    block = act_block(total)
    blocks = ring_gather(block, {2: probs_low, 3: both})
    both = gather_sum(both.reshape((exp_size, -1) + both.shape[1:]), "exp").astype(BF)
    full = after(jnp.concatenate(blocks, axis=0), both)
    of_experts = finish(full, input_rows, grad_rows, gate_mat, up_mat, placed_low)
    grad_key, grad_value = to_owners(both)
    return (grad_query, grad_key, grad_value) + of_experts


def solution(mesh):
    placed = (
        P("ctx", ("head", "exp"), None),
        P(("ctx", "exp"), "head", None),
        P(("ctx", "exp"), "head", None),
        P("ctx", ("head", "exp"), None),
        P("exp", "ctx"),
        P("exp", "ctx"),
        P("exp", None),
        P("exp", None),
        P("exp", "ctx", None),
        P("exp", "ctx", None),
        P("exp", None, "ctx"),
    )
    return jax.shard_map(
        shards,
        mesh=mesh,
        in_specs=placed,
        out_specs=(
            P("ctx", ("head", "exp"), None),
            P(("ctx", "exp"), "head", None),
            P(("ctx", "exp"), "head", None),
            P("exp", ("ctx", "head")),
            P("exp", "ctx", "head"),
            P("exp", "ctx", "head"),
            P("exp", "head", "ctx"),
        ),
        check_vma=False,
    )
```

```python
import jax
import jax.numpy as jnp
from jax import lax
from jax.sharding import PartitionSpec as P

CAP = 48
X_HI = 2
MASKS = (4, 2, 8, 1)
BF = jnp.bfloat16
F32 = jnp.float32


def activate(gate_val, up_val, back_val):
    sigmoid_gate = jax.nn.sigmoid(gate_val)
    hidden = (gate_val * sigmoid_gate * up_val).astype(BF)
    d_up = (back_val * gate_val * sigmoid_gate).astype(BF)
    d_gate = (back_val * up_val * sigmoid_gate * (1.0 + gate_val * (1.0 - sigmoid_gate))).astype(BF)
    return (hidden, d_gate, d_up)


def spread(block, axis):
    n = lax.axis_size(axis)
    copies = jnp.broadcast_to(block[None], (n,) + block.shape)
    return lax.all_to_all(copies, axis, 0, 0, tiled=True)


def gather_sum(parts, axis):
    return jnp.sum(lax.all_to_all(parts, axis, 0, 0, tiled=True).astype(F32), axis=0)


def z_shift(step):
    n = lax.axis_size("ctx") // X_HI
    return [(h * n + z, h * n + (z + step) % n) for h in range(X_HI) for z in range(n)]


def right(block):
    return lax.ppermute(block, "ctx", z_shift(1))


def left(block):
    return lax.ppermute(block, "ctx", z_shift(-1))


def opposite(block):
    n = lax.axis_size("ctx")
    return lax.ppermute(block, "ctx", [(c, (c + n // X_HI) % n) for c in range(n)])


def after(block, *others):
    return lax.optimization_barrier((block,) + others)[0]


def add_low(a, b):
    return (a.astype(F32) + b.astype(F32)).astype(BF)


def sum_start(parts):
    far = len(parts) // 2
    cut = parts[0].shape[1] // 2
    return parts[far][:, :cut], parts[far][:, cut:]


def sum_step(parts, step, onward, back):
    n = len(parts)
    far = n // 2
    cut = parts[0].shape[1] // 2
    onward, back = right(onward), left(back)
    ahead, behind = parts[far - 1 - step], parts[(far + 1 + step) % n]
    if step == 0:
        onward = jnp.concatenate([add_low(onward, ahead[:, :cut]), ahead[:, cut:]], axis=1)
        back = jnp.concatenate([behind[:, :cut], add_low(back, behind[:, cut:])], axis=1)
    elif step < far - 1:
        onward, back = add_low(onward, ahead), add_low(back, behind)
    return onward, back


def ring_gather(block, beside):
    n = lax.axis_size("ctx") // X_HI
    far = n // 2
    cut = block.shape[1] // 2
    blocks = [block] + [None] * (n - 1)
    onward = back = block
    for step in range(1, far):
        if step in beside:
            onward, back = after(onward, beside[step]), after(back, beside[step])
        onward, back = right(onward), left(back)
        blocks[n - step], blocks[step] = onward, back
    blocks[far] = jnp.concatenate([right(onward[:, :cut]), left(back[:, cut:])], axis=1)
    return blocks


def turn(blocks, places):
    twice = jnp.concatenate([blocks, blocks], axis=0)
    return lax.dynamic_slice_in_dim(twice, places, blocks.shape[0], 0)


def swap(block, mask):
    return lax.ppermute(block, "ctx", [(c, c ^ mask) for c in range(lax.axis_size("ctx"))])


def ctx_gather(key_rows, value_vector_rows):
    block = jnp.concatenate([key_rows[:, 0, :], value_vector_rows[:, 0, :]], axis=1)
    for mask in MASKS:
        block = jnp.concatenate([block, swap(block, mask)], axis=0)
    return block


def mask_of(index):
    return sum((index >> bit) % 2 * mask for bit, mask in enumerate(MASKS))


def key_places(rows):
    ctx_size, exp_size = lax.axis_size("ctx"), lax.axis_size("exp")
    own = rows // (ctx_size * exp_size)
    place = jnp.arange(rows)
    of_ctx = lax.axis_index("ctx") ^ mask_of(place // own % ctx_size)
    return (of_ctx * exp_size + place // (own * ctx_size)) * own + place % own


def masked_scores(queries, flat):
    tok_rows, _, head_dim = queries.shape
    query_pos = lax.axis_index("ctx") * tok_rows + jnp.arange(tok_rows)
    allowed = key_places(flat.shape[0])[None, :] <= query_pos[:, None]
    scores = jnp.einsum("phd,td->hpt", queries, flat[:, :head_dim], preferred_element_type=F32)
    return jnp.where(allowed[None], scores * head_dim ** (-0.5), -jnp.inf)


def value_side(scores, flat, grad_attn):
    value_flat = flat[:, grad_attn.shape[2] :]
    probs_full = jax.nn.softmax(scores, axis=-1)
    probs_low = probs_full.astype(BF)
    attn_out = jnp.einsum("hpt,td->phd", probs_low, value_flat, preferred_element_type=F32)
    row_delta = jnp.sum(grad_attn.astype(F32) * attn_out, axis=-1)
    value_grad = jnp.einsum("hpt,phd->td", probs_low, grad_attn, preferred_element_type=F32)
    return probs_full, row_delta, value_grad.astype(BF)


def key_side(probs_full, row_delta, queries, flat, grad_attn):
    head_dim = queries.shape[2]
    grad_prob = jnp.einsum(
        "phd,td->hpt", grad_attn, flat[:, head_dim:], preferred_element_type=F32
    )
    dscore = (probs_full * (grad_prob - jnp.transpose(row_delta)[:, :, None])).astype(BF)
    key_grad = jnp.einsum("hpt,phd->td", dscore, queries, preferred_element_type=F32)
    return dscore, key_grad.astype(BF)


def query_side(dscore, flat):
    head_dim = flat.shape[1] // 2
    grad_query = jnp.einsum("hpt,td->phd", dscore, flat[:, :head_dim], preferred_element_type=F32)
    return (grad_query * head_dim ** (-0.5)).astype(BF)


def to_owners(both):
    head_dim = both.shape[1] // 2
    for mask in reversed(MASKS):
        half = both.shape[0] // 2
        sent = both[half:].astype(BF if half >= both.shape[1] // 2 else F32)
        both = both[:half] + swap(sent, mask).astype(F32)
    grad_key = (both[:, :head_dim] * head_dim ** (-0.5)).astype(BF)[:, None, :]
    grad_value = both[:, head_dim:].astype(BF)[:, None, :]
    return grad_key, grad_value


def select(moe_input, moe_grad, expert_ids, router_weight):
    width = moe_input.shape[1]
    exp_size = lax.axis_size("exp")
    matches = expert_ids[:, :, None] == jnp.arange(exp_size)[None, None, :]
    member = jnp.sum(matches.astype(jnp.int32), axis=1)
    weight_row = jnp.sum(jnp.where(matches, router_weight[:, :, None], 0.0), axis=1)
    slot_rank = jnp.cumsum(member, axis=0) - member
    placed = (member[:, :, None] == 1) & (
        slot_rank[:, :, None] == jnp.arange(CAP)[None, None, :]
    )
    slot_weight = jnp.sum(jnp.where(placed, weight_row[:, :, None], 0.0), axis=0)
    placed_low = placed.astype(BF).reshape(-1, exp_size * CAP)
    rows = jnp.concatenate([moe_input, moe_grad], axis=1)
    picked = jnp.einsum("bs,bd->sd", placed_low, rows, preferred_element_type=F32)
    scaled = picked[:, width:] * slot_weight.reshape(-1, 1)
    sent = jnp.concatenate([picked[:, :width].astype(BF), scaled.astype(BF)], axis=1)
    got = lax.all_to_all(sent.reshape(exp_size, CAP, 2 * width), "exp", 0, 0, tiled=True)
    return placed_low, got


def project(got, gate_weight, up_weight, down_weight):
    ring = lax.axis_size("ctx") // X_HI
    at = lax.axis_index("ctx") % ring
    half = lax.axis_index("head")
    units = gate_weight.shape[2] // lax.axis_size("head")
    width = got.shape[2] // 2
    got = turn(got.reshape(ring, -1, 2 * width), at).reshape(-1, 2 * width)
    input_rows, grad_rows = got[:, :width], got[:, width:]
    gate_mat = lax.dynamic_slice_in_dim(gate_weight[0], half * units, units, 1)
    up_mat = lax.dynamic_slice_in_dim(up_weight[0], half * units, units, 1)
    down_mat = lax.dynamic_slice_in_dim(down_weight[0], half * units, units, 0)
    gate_part = jnp.dot(input_rows, gate_mat, preferred_element_type=F32).astype(BF)
    up_part = jnp.dot(input_rows, up_mat, preferred_element_type=F32).astype(BF)
    back_part = jnp.einsum("rd,fd->rf", grad_rows, down_mat, preferred_element_type=F32).astype(BF)
    parts = jnp.concatenate([gate_part, up_part, back_part], axis=1).reshape(ring, -1, 3 * units)
    return input_rows, grad_rows, gate_mat, up_mat, [parts[j] for j in range(ring)]


def act_block(total):
    units = total.shape[1] // 3
    total = total + opposite(total.astype(BF)).astype(F32)
    hidden, d_gate, d_up = activate(
        total[:, :units], total[:, units : 2 * units], total[:, 2 * units :]
    )
    return jnp.concatenate([hidden, d_gate, d_up], axis=1)


def finish(full, input_rows, grad_rows, gate_mat, up_mat, placed_low):
    exp_size, head_size = lax.axis_size("exp"), lax.axis_size("head")
    ring = lax.axis_size("ctx") // X_HI
    at = lax.axis_index("ctx") % ring
    half = lax.axis_index("head")
    units = full.shape[1] // 3
    columns = input_rows.shape[1] // head_size
    hidden, d_gate, d_up = full[:, :units], full[:, units : 2 * units], full[:, 2 * units :]
    contrib = jnp.einsum("rf,df->rd", d_gate, gate_mat, preferred_element_type=F32)
    contrib = contrib + jnp.einsum("rf,df->rd", d_up, up_mat, preferred_element_type=F32)
    mine = lax.dynamic_slice_in_dim(contrib, half * columns, columns, 1)
    other = lax.dynamic_slice_in_dim(contrib, (1 - half) * columns, columns, 1).astype(BF)
    mine = (mine + lax.ppermute(other, "head", [(0, 1), (1, 0)]).astype(F32)).astype(BF)
    mine = turn(mine.reshape(ring, -1, columns), (ring - at) % ring).reshape(exp_size, CAP, columns)
    back_rows = lax.all_to_all(mine, "exp", 0, 0, tiled=True)
    grad_input = jnp.dot(
        placed_low, back_rows.reshape(-1, columns), preferred_element_type=F32
    ).astype(BF)
    grad_gate = jnp.einsum("rd,rf->df", input_rows, d_gate, preferred_element_type=F32).astype(BF)
    grad_up = jnp.einsum("rd,rf->df", input_rows, d_up, preferred_element_type=F32).astype(BF)
    grad_down = jnp.einsum("rf,rd->fd", hidden, grad_rows, preferred_element_type=F32).astype(BF)
    return grad_input, grad_gate[None], grad_up[None], grad_down[None]


def shards(
    queries,
    key_rows,
    value_vector_rows,
    grad_attn,
    moe_input,
    moe_grad,
    expert_ids,
    router_weight,
    gate_weight,
    up_weight,
    down_weight,
):
    exp_size = lax.axis_size("exp")
    near = ctx_gather(key_rows, value_vector_rows)
    placed_low, got = select(moe_input, moe_grad, expert_ids, router_weight)
    flat = spread(after(near, got), "exp").reshape(-1, near.shape[1])
    input_rows, grad_rows, gate_mat, up_mat, parts = project(
        got, gate_weight, up_weight, down_weight
    )
    onward, back = sum_step(parts, 0, *sum_start(parts))
    onward, back = sum_step(parts, 1, onward, back)
    scores = masked_scores(queries, after(flat, onward, back))
    onward, back = sum_step(parts, 2, onward, back)
    probs_full, row_delta, value_grad = value_side(after(scores, onward, back), flat, grad_attn)
    onward, back = sum_step(parts, 3, after(onward, scores), after(back, scores))
    total = onward.astype(F32) + back.astype(F32) + parts[0].astype(F32)
    dscore, key_grad = key_side(
        probs_full, after(row_delta, total), queries, flat, grad_attn
    )
    block = act_block(after(total, value_grad))
    grad_query = query_side(dscore, after(flat, block))
    both = jnp.concatenate([key_grad, value_grad], axis=1)
    blocks = ring_gather(block, {1: both, 2: grad_query})
    both = gather_sum(both.reshape((exp_size, -1) + both.shape[1:]), "exp")
    full = after(jnp.concatenate(blocks, axis=0), both)
    of_experts = finish(full, input_rows, grad_rows, gate_mat, up_mat, placed_low)
    grad_key, grad_value = to_owners(both)
    return (grad_query, grad_key, grad_value) + of_experts


def solution(mesh):
    placed = (
        P("ctx", ("head", "exp"), None),
        P(("ctx", "exp"), "head", None),
        P(("ctx", "exp"), "head", None),
        P("ctx", ("head", "exp"), None),
        P("exp", "ctx"),
        P("exp", "ctx"),
        P("exp", None),
        P("exp", None),
        P("exp", "ctx", None),
        P("exp", "ctx", None),
        P("exp", None, "ctx"),
    )
    return jax.shard_map(
        shards,
        mesh=mesh,
        in_specs=placed,
        out_specs=(
            P("ctx", ("head", "exp"), None),
            P(("ctx", "exp"), "head", None),
            P(("ctx", "exp"), "head", None),
            P("exp", ("ctx", "head")),
            P("exp", "ctx", "head"),
            P("exp", "ctx", "head"),
            P("exp", "head", "ctx"),
        ),
        check_vma=False,
    )
```

```python
import functools

import jax
import jax.numpy as jnp
from jax import lax
from jax.experimental import pallas as pl
from jax.experimental.pallas import tpu as pltpu
from jax.sharding import PartitionSpec as P

CAP = 48
X_HI = 2
MASKS = (4, 2, 8, 1)
BF = jnp.bfloat16
F32 = jnp.float32


def activate(gate_val, up_val, back_val):
    sigmoid_gate = jax.nn.sigmoid(gate_val)
    hidden = (gate_val * sigmoid_gate * up_val).astype(BF)
    d_up = (back_val * gate_val * sigmoid_gate).astype(BF)
    d_gate = (back_val * up_val * sigmoid_gate * (1.0 + gate_val * (1.0 - sigmoid_gate))).astype(BF)
    return (hidden, d_gate, d_up)


def spread(block, axis):
    n = lax.axis_size(axis)
    copies = jnp.broadcast_to(block[None], (n,) + block.shape)
    return lax.all_to_all(copies, axis, 0, 0, tiled=True)


def gather_sum(parts, axis):
    return jnp.sum(lax.all_to_all(parts, axis, 0, 0, tiled=True).astype(F32), axis=0)


def z_shift(step):
    n = lax.axis_size("ctx") // X_HI
    return [(h * n + z, h * n + (z + step) % n) for h in range(X_HI) for z in range(n)]


def right(block):
    return lax.ppermute(block, "ctx", z_shift(1))


def left(block):
    return lax.ppermute(block, "ctx", z_shift(-1))


def opposite(block):
    n = lax.axis_size("ctx")
    return lax.ppermute(block, "ctx", [(c, (c + n // X_HI) % n) for c in range(n)])


def after(block, *others):
    return lax.optimization_barrier((block,) + others)[0]


def add_low(a, b):
    return (a.astype(F32) + b.astype(F32)).astype(BF)


def sum_start(parts):
    far = len(parts) // 2
    cut = parts[0].shape[1] // 2
    return parts[far][:, :cut], parts[far][:, cut:]


def sum_step(parts, step, onward, back):
    n = len(parts)
    far = n // 2
    cut = parts[0].shape[1] // 2
    onward, back = right(onward), left(back)
    ahead, behind = parts[far - 1 - step], parts[(far + 1 + step) % n]
    if step == 0:
        onward = jnp.concatenate([add_low(onward, ahead[:, :cut]), ahead[:, cut:]], axis=1)
        back = jnp.concatenate([behind[:, :cut], add_low(back, behind[:, cut:])], axis=1)
    elif step < far - 1:
        onward, back = add_low(onward, ahead), add_low(back, behind)
    return onward, back


def ring_gather(block, beside):
    n = lax.axis_size("ctx") // X_HI
    far = n // 2
    cut = block.shape[1] // 2
    blocks = [block] + [None] * (n - 1)
    onward = back = block
    for step in range(1, far):
        onward, back = right(onward), left(back)
        blocks[n - step], blocks[step] = onward, back
    onward, back = after(onward, beside), after(back, beside)
    blocks[far] = jnp.concatenate([right(onward[:, :cut]), left(back[:, cut:])], axis=1)
    return blocks


def turn(blocks, places):
    twice = jnp.concatenate([blocks, blocks], axis=0)
    return lax.dynamic_slice_in_dim(twice, places, blocks.shape[0], 0)


def swap(block, mask):
    return lax.ppermute(block, "ctx", [(c, c ^ mask) for c in range(lax.axis_size("ctx"))])


def ctx_gather(block, masks):
    for mask in masks:
        block = jnp.concatenate([block, swap(block, mask)], axis=0)
    return block


def mask_of(index):
    return sum((index >> bit) % 2 * mask for bit, mask in enumerate(MASKS))


def attend_body(own, ctx_size, me_ref, q_ref, g_ref, kv_ref, both_ref, dq_ref, score_ref, dprob_ref):
    size = kv_ref.shape[1] // 2
    lanes = q_ref.shape[0]
    tokens = lanes // 2
    scale = size ** (-0.5)
    chunk = 8 * own
    me = me_ref[0]
    across = (((1,), (1,)), ((), ()))
    ahead = lax.broadcasted_iota(jnp.int32, (own, lanes), 1) % tokens - lax.broadcasted_iota(
        jnp.int32, (own, lanes), 0
    )

    def at(step):
        return pl.ds(pl.multiple_of(step * chunk, chunk), chunk)

    def score(step, top):
        found = lax.dot_general(
            kv_ref[at(step), :size], q_ref[...], across, preferred_element_type=F32
        )
        for part in range(8):
            place = step * 8 + part
            start = (me ^ mask_of(place % ctx_size)) * tokens + place // ctx_size * own
            masked = jnp.where(
                ahead >= start - me * tokens,
                found[part * own : (part + 1) * own] * scale,
                -jnp.inf,
            )
            score_ref[pl.ds(pl.multiple_of(place * own, own), own), :] = masked
            top = jnp.maximum(top, masked)
        return top

    steps = kv_ref.shape[0] // chunk
    top = lax.fori_loop(0, steps, score, jnp.full((own, lanes), -jnp.inf, F32))
    top = jnp.max(top, axis=0, keepdims=True)

    def weigh(step, sums):
        norm, delta = sums
        prob = jnp.exp(score_ref[at(step), :] - top)
        dprob = lax.dot_general(
            kv_ref[at(step), size:], g_ref[...], across, preferred_element_type=F32
        )
        score_ref[at(step), :] = prob
        dprob_ref[at(step), :] = dprob
        norm = norm + jnp.sum(prob.reshape(-1, 8, lanes), axis=0)
        delta = delta + jnp.sum((prob * dprob).reshape(-1, 8, lanes), axis=0)
        return norm, delta

    zero = jnp.zeros((8, lanes), F32)
    norm, delta = lax.fori_loop(0, steps, weigh, (zero, zero))
    inverse = 1.0 / jnp.sum(norm, axis=0, keepdims=True)
    delta = jnp.sum(delta, axis=0, keepdims=True) * inverse

    def back(step, total):
        prob = score_ref[at(step), :] * inverse
        both_ref[at(step), size:] = jnp.dot(
            prob.astype(BF), g_ref[...], preferred_element_type=F32
        ).astype(BF)
        dscore = (prob * (dprob_ref[at(step), :] - delta)).astype(BF)
        both_ref[at(step), :size] = jnp.dot(
            dscore, q_ref[...], preferred_element_type=F32
        ).astype(BF)
        return total + lax.dot_general(
            kv_ref[at(step), :size], dscore, (((0,), (0,)), ((), ())), preferred_element_type=F32
        )

    total = lax.fori_loop(0, steps, back, jnp.zeros((size, lanes), F32))
    dq_ref[...] = (total * scale).T.astype(BF)


def attend(queries, grad_attn, flat):
    tok_rows, heads, size = queries.shape
    lanes = tok_rows * heads
    ctx_size, exp_size = lax.axis_size("ctx"), lax.axis_size("exp")
    keys = flat.shape[0]
    own = keys // (ctx_size * exp_size)
    vmem = pl.BlockSpec(memory_space=pltpu.VMEM)
    both, grad_query = pl.pallas_call(
        functools.partial(attend_body, own, ctx_size),
        out_shape=(
            jax.ShapeDtypeStruct((keys, 2 * size), BF),
            jax.ShapeDtypeStruct((lanes, size), BF),
        ),
        in_specs=[pl.BlockSpec(memory_space=pltpu.SMEM), vmem, vmem, vmem],
        out_specs=(vmem, vmem),
        scratch_shapes=[pltpu.VMEM((keys, lanes), F32), pltpu.VMEM((keys, lanes), F32)],
        compiler_params=pltpu.CompilerParams(vmem_limit_bytes=32 * 2**20),
        cost_estimate=pl.CostEstimate(
            flops=10 * keys * lanes * size,
            bytes_accessed=8 * keys * size,
            transcendentals=keys * lanes,
        ),
        name="attention_backward",
    )(
        lax.axis_index("ctx").astype(jnp.int32).reshape(1),
        jnp.swapaxes(queries, 0, 1).reshape(lanes, size),
        jnp.swapaxes(grad_attn, 0, 1).reshape(lanes, size),
        flat,
    )
    return both, jnp.swapaxes(grad_query.reshape(heads, tok_rows, size), 0, 1)


def ctx_sum(both, masks):
    for mask in reversed(masks):
        half = both.shape[0] // 2
        sent = both[half:].astype(BF if half >= both.shape[1] // 2 else F32)
        both = both[:half] + swap(sent, mask).astype(F32)
    return both


def own_grads(both):
    head_dim = both.shape[1] // 2
    grad_key = (both[:, :head_dim] * head_dim ** (-0.5)).astype(BF)[:, None, :]
    grad_value = both[:, head_dim:].astype(BF)[:, None, :]
    return grad_key, grad_value


def select(moe_input, moe_grad, expert_ids, router_weight, near):
    width = moe_input.shape[1]
    exp_size = lax.axis_size("exp")
    matches = expert_ids[:, :, None] == jnp.arange(exp_size)[None, None, :]
    member = jnp.sum(matches.astype(jnp.int32), axis=1)
    weight_row = jnp.sum(jnp.where(matches, router_weight[:, :, None], 0.0), axis=1)
    slot_rank = jnp.cumsum(member, axis=0) - member
    placed = (member[:, :, None] == 1) & (
        slot_rank[:, :, None] == jnp.arange(CAP)[None, None, :]
    )
    slot_weight = jnp.sum(jnp.where(placed, weight_row[:, :, None], 0.0), axis=0)
    placed_low = placed.astype(BF).reshape(-1, exp_size * CAP)
    rows = jnp.concatenate([moe_input, moe_grad], axis=1)
    picked = jnp.einsum("bs,bd->sd", placed_low, rows, preferred_element_type=F32)
    scaled = picked[:, width:] * slot_weight.reshape(-1, 1)
    sent = jnp.concatenate([picked[:, :width].astype(BF), scaled.astype(BF)], axis=1)
    sent = after(sent, near)
    got = lax.all_to_all(sent.reshape(exp_size, CAP, 2 * width), "exp", 0, 0, tiled=True)
    return placed_low, got


def project(got, gate_weight, up_weight, down_weight):
    ring = lax.axis_size("ctx") // X_HI
    at = lax.axis_index("ctx") % ring
    half = lax.axis_index("head")
    units = gate_weight.shape[2] // lax.axis_size("head")
    width = got.shape[2] // 2
    got = turn(got.reshape(ring, -1, 2 * width), at).reshape(-1, 2 * width)
    input_rows, grad_rows = got[:, :width], got[:, width:]
    gate_mat = lax.dynamic_slice_in_dim(gate_weight[0], half * units, units, 1)
    up_mat = lax.dynamic_slice_in_dim(up_weight[0], half * units, units, 1)
    down_mat = lax.dynamic_slice_in_dim(down_weight[0], half * units, units, 0)
    gate_part = jnp.dot(input_rows, gate_mat, preferred_element_type=F32).astype(BF)
    up_part = jnp.dot(input_rows, up_mat, preferred_element_type=F32).astype(BF)
    back_part = jnp.einsum("rd,fd->rf", grad_rows, down_mat, preferred_element_type=F32).astype(BF)
    parts = jnp.concatenate([gate_part, up_part, back_part], axis=1).reshape(ring, -1, 3 * units)
    return input_rows, grad_rows, gate_mat, up_mat, [parts[j] for j in range(ring)]


def act_block(total):
    units = total.shape[1] // 3
    total = total + opposite(total.astype(BF)).astype(F32)
    hidden, d_gate, d_up = activate(
        total[:, :units], total[:, units : 2 * units], total[:, 2 * units :]
    )
    return jnp.concatenate([hidden, d_gate, d_up], axis=1)


def finish(full, input_rows, grad_rows, gate_mat, up_mat, placed_low):
    exp_size, head_size = lax.axis_size("exp"), lax.axis_size("head")
    ring = lax.axis_size("ctx") // X_HI
    at = lax.axis_index("ctx") % ring
    half = lax.axis_index("head")
    units = full.shape[1] // 3
    columns = input_rows.shape[1] // head_size
    hidden, d_gate, d_up = full[:, :units], full[:, units : 2 * units], full[:, 2 * units :]
    contrib = jnp.einsum("rf,df->rd", d_gate, gate_mat, preferred_element_type=F32)
    contrib = contrib + jnp.einsum("rf,df->rd", d_up, up_mat, preferred_element_type=F32)
    mine = lax.dynamic_slice_in_dim(contrib, half * columns, columns, 1)
    other = lax.dynamic_slice_in_dim(contrib, (1 - half) * columns, columns, 1).astype(BF)
    mine = (mine + lax.ppermute(other, "head", [(0, 1), (1, 0)]).astype(F32)).astype(BF)
    mine = turn(mine.reshape(ring, -1, columns), (ring - at) % ring).reshape(exp_size, CAP, columns)
    back_rows = lax.all_to_all(mine, "exp", 0, 0, tiled=True)
    grad_input = jnp.dot(
        placed_low, back_rows.reshape(-1, columns), preferred_element_type=F32
    ).astype(BF)
    grad_gate = jnp.einsum("rd,rf->df", input_rows, d_gate, preferred_element_type=F32).astype(BF)
    grad_up = jnp.einsum("rd,rf->df", input_rows, d_up, preferred_element_type=F32).astype(BF)
    grad_down = jnp.einsum("rf,rd->fd", hidden, grad_rows, preferred_element_type=F32).astype(BF)
    return grad_input, grad_gate[None], grad_up[None], grad_down[None]


def shards(
    queries,
    key_rows,
    value_vector_rows,
    grad_attn,
    moe_input,
    moe_grad,
    expert_ids,
    router_weight,
    gate_weight,
    up_weight,
    down_weight,
):
    exp_size = lax.axis_size("exp")
    pair = jnp.concatenate([key_rows[:, 0, :], value_vector_rows[:, 0, :]], axis=1)
    near = ctx_gather(pair, MASKS[:2])
    placed_low, got = select(moe_input, moe_grad, expert_ids, router_weight, near)
    near = ctx_gather(near, MASKS[2:])
    flat = spread(after(near, got), "exp").reshape(-1, near.shape[1])
    input_rows, grad_rows, gate_mat, up_mat, parts = project(
        got, gate_weight, up_weight, down_weight
    )
    onward, back = sum_start(parts)
    onward, back = sum_step(parts, 0, after(onward, near), after(back, near))
    onward, back = sum_step(parts, 1, onward, back)
    onward, back = sum_step(parts, 2, onward, back)
    both, grad_query = attend(queries, grad_attn, after(flat, onward, back))
    onward, back = sum_step(parts, 3, after(onward, flat), after(back, flat))
    total = onward.astype(F32) + back.astype(F32) + parts[0].astype(F32)
    block = act_block(after(total, both))
    both = gather_sum(both.reshape((exp_size, -1) + both.shape[1:]), "exp")
    blocks = ring_gather(block, both)
    both = ctx_sum(both, MASKS[3:])
    full = after(jnp.concatenate(blocks, axis=0), both)
    of_experts = finish(full, input_rows, grad_rows, gate_mat, up_mat, placed_low)
    grad_key, grad_value = own_grads(ctx_sum(both, MASKS[:3]))
    return (grad_query, grad_key, grad_value) + of_experts


def solution(mesh):
    placed = (
        P("ctx", ("head", "exp"), None),
        P(("ctx", "exp"), "head", None),
        P(("ctx", "exp"), "head", None),
        P("ctx", ("head", "exp"), None),
        P("exp", "ctx"),
        P("exp", "ctx"),
        P("exp", None),
        P("exp", None),
        P("exp", "ctx", None),
        P("exp", "ctx", None),
        P("exp", None, "ctx"),
    )
    return jax.shard_map(
        shards,
        mesh=mesh,
        in_specs=placed,
        out_specs=(
            P("ctx", ("head", "exp"), None),
            P(("ctx", "exp"), "head", None),
            P(("ctx", "exp"), "head", None),
            P("exp", ("ctx", "head")),
            P("exp", "ctx", "head"),
            P("exp", "ctx", "head"),
            P("exp", "head", "ctx"),
        ),
        check_vma=False,
    )
```

```python
import functools

import jax
import jax.numpy as jnp
from jax import lax
from jax.experimental import pallas as pl
from jax.experimental.pallas import tpu as pltpu
from jax.sharding import PartitionSpec as P

CAP = 48
X_HI = 2
X_LO = 2
MASKED = -1e30
MASKS = (4, 2, 8, 1)
BF = jnp.bfloat16
F32 = jnp.float32


def activate(gate_val, up_val, back_val):
    sigmoid_gate = jax.nn.sigmoid(gate_val)
    hidden = (gate_val * sigmoid_gate * up_val).astype(BF)
    d_up = (back_val * gate_val * sigmoid_gate).astype(BF)
    d_gate = (back_val * up_val * sigmoid_gate * (1.0 + gate_val * (1.0 - sigmoid_gate))).astype(BF)
    return (hidden, d_gate, d_up)


def y_groups():
    n = lax.axis_size("exp")
    return [list(range(x, n, X_LO)) for x in range(X_LO)]


def y_gather(block):
    n = lax.axis_size("exp") // X_LO
    copies = jnp.broadcast_to(block[None], (n,) + block.shape)
    return lax.all_to_all(copies, "exp", 0, 0, tiled=True, axis_index_groups=y_groups())


def y_sum(parts):
    got = lax.all_to_all(parts, "exp", 0, 0, tiled=True, axis_index_groups=y_groups())
    return jnp.sum(got.astype(F32), axis=0)


def beside(block):
    return lax.ppermute(block, "exp", [(e, e ^ 1) for e in range(lax.axis_size("exp"))])


def z_shift(step):
    n = lax.axis_size("ctx") // X_HI
    return [(h * n + z, h * n + (z + step) % n) for h in range(X_HI) for z in range(n)]


def right(block):
    return lax.ppermute(block, "ctx", z_shift(1))


def left(block):
    return lax.ppermute(block, "ctx", z_shift(-1))


def opposite(block):
    n = lax.axis_size("ctx")
    return lax.ppermute(block, "ctx", [(c, (c + n // X_HI) % n) for c in range(n)])


def after(block, *others):
    return lax.optimization_barrier((block,) + others)[0]


def add_low(a, b):
    return (a.astype(F32) + b.astype(F32)).astype(BF)


def sum_start(parts):
    far = len(parts) // 2
    cut = parts[0].shape[1] // 2
    return parts[far][:, :cut], parts[far][:, cut:]


def sum_step(parts, step, onward, back):
    n = len(parts)
    far = n // 2
    cut = parts[0].shape[1] // 2
    onward, back = right(onward), left(back)
    ahead, behind = parts[far - 1 - step], parts[(far + 1 + step) % n]
    if step == 0:
        onward = jnp.concatenate([add_low(onward, ahead[:, :cut]), ahead[:, cut:]], axis=1)
        back = jnp.concatenate([behind[:, :cut], add_low(back, behind[:, cut:])], axis=1)
    elif step < far - 1:
        onward, back = add_low(onward, ahead), add_low(back, behind)
    return onward, back


def ring_gather(block, waits):
    n = lax.axis_size("ctx") // X_HI
    far = n // 2
    cut = block.shape[1] // 2
    blocks = [block] + [None] * (n - 1)
    onward = back = block
    for step in range(1, far):
        if step in waits:
            onward, back = after(onward, waits[step]), after(back, waits[step])
        onward, back = right(onward), left(back)
        blocks[n - step], blocks[step] = onward, back
    if far in waits:
        onward, back = after(onward, waits[far]), after(back, waits[far])
    blocks[far] = jnp.concatenate([right(onward[:, :cut]), left(back[:, cut:])], axis=1)
    return blocks


def turn(blocks, places):
    twice = jnp.concatenate([blocks, blocks], axis=0)
    return lax.dynamic_slice_in_dim(twice, places, blocks.shape[0], 0)


def swap(block, mask):
    return lax.ppermute(block, "ctx", [(c, c ^ mask) for c in range(lax.axis_size("ctx"))])


def ctx_gather(block, masks):
    for mask in masks:
        block = jnp.concatenate([block, swap(block, mask)], axis=0)
    return block


def mask_of(index):
    return sum((index >> bit) % 2 * mask for bit, mask in enumerate(MASKS))


def scores_of(step, own, ctx_size, tokens, here_ref, k, q):
    lanes = q.shape[0]
    found = lax.dot_general(k, q, (((1,), (1,)), ((), ())), preferred_element_type=F32)
    ahead = lax.broadcasted_iota(jnp.int32, (own, lanes), 1) % tokens - lax.broadcasted_iota(
        jnp.int32, (own, lanes), 0
    )
    me, side = here_ref[0], here_ref[1]
    parts = k.shape[0] // own
    masked = []
    for part in range(parts):
        place = step * parts + part
        start = (me ^ mask_of(place % ctx_size)) * tokens + (place // ctx_size * X_LO + side) * own
        masked.append(
            jnp.where(
                ahead >= start - me * tokens,
                found[part * own : (part + 1) * own] * k.shape[1] ** (-0.5),
                MASKED,
            )
        )
    return jnp.concatenate(masked, axis=0)


def stats_body(own, ctx_size, tokens, here_ref, q_ref, g_ref, kv_ref, stats_ref):
    size = kv_ref.shape[1] // 2
    lanes = q_ref.shape[0]
    chunk = 8 * own

    def one(step, held):
        top, norm, delta = held
        rows = pl.ds(pl.multiple_of(step * chunk, chunk), chunk)
        scores = scores_of(step, own, ctx_size, tokens, here_ref, kv_ref[rows, :size], q_ref[...])
        dprob = lax.dot_general(
            kv_ref[rows, size:], g_ref[...], (((1,), (1,)), ((), ())), preferred_element_type=F32
        )
        scores, dprob = scores.reshape(-1, 8, lanes), dprob.reshape(-1, 8, lanes)
        higher = jnp.maximum(top, jnp.max(scores, axis=0))
        shrink = jnp.exp(top - higher)
        prob = jnp.exp(scores - higher[None])
        norm = norm * shrink + jnp.sum(prob, axis=0)
        delta = delta * shrink + jnp.sum(prob * dprob, axis=0)
        return higher, norm, delta

    zero = jnp.zeros((8, lanes), F32)
    top, norm, delta = lax.fori_loop(0, kv_ref.shape[0] // chunk, one, (zero + MASKED, zero, zero))
    highest = jnp.max(top, axis=0, keepdims=True)
    shrink = jnp.exp(top - highest)
    stats_ref[0:1, :] = highest
    stats_ref[1:2, :] = jnp.sum(norm * shrink, axis=0, keepdims=True)
    stats_ref[2:3, :] = jnp.sum(delta * shrink, axis=0, keepdims=True)
    stats_ref[3:, :] = jnp.zeros((5, lanes), F32)


def grads_body(
    own, ctx_size, tokens, here_ref, q_ref, g_ref, kv_ref, stats_ref, far_ref, both_ref, dq_ref
):
    size = kv_ref.shape[1] // 2
    lanes = q_ref.shape[0]
    chunk = 8 * own
    far = jnp.concatenate([far_ref[:, lanes // 2 :], far_ref[:, : lanes // 2]], axis=1)
    near = stats_ref[...]
    top = jnp.maximum(near[0:1], far[0:1])
    shrink_near, shrink_far = jnp.exp(near[0:1] - top), jnp.exp(far[0:1] - top)
    inverse = 1.0 / (near[1:2] * shrink_near + far[1:2] * shrink_far)
    delta = (near[2:3] * shrink_near + far[2:3] * shrink_far) * inverse

    def one(step, total):
        rows = pl.ds(pl.multiple_of(step * chunk, chunk), chunk)
        k = kv_ref[rows, :size]
        scores = scores_of(step, own, ctx_size, tokens, here_ref, k, q_ref[...])
        prob = jnp.exp(scores - top) * inverse
        both_ref[rows, size:] = jnp.dot(
            prob.astype(BF), g_ref[...], preferred_element_type=F32
        ).astype(BF)
        dprob = lax.dot_general(
            kv_ref[rows, size:], g_ref[...], (((1,), (1,)), ((), ())), preferred_element_type=F32
        )
        dscore = (prob * (dprob - delta)).astype(BF)
        both_ref[rows, :size] = jnp.dot(dscore, q_ref[...], preferred_element_type=F32).astype(BF)
        return total + lax.dot_general(
            k, dscore, (((0,), (0,)), ((), ())), preferred_element_type=F32
        )

    total = lax.fori_loop(0, kv_ref.shape[0] // chunk, one, jnp.zeros((size, lanes), F32))
    dq_ref[...] = (total * size ** (-0.5)).T


VMEM = pl.BlockSpec(memory_space=pltpu.VMEM)
SMEM = pl.BlockSpec(memory_space=pltpu.SMEM)


def here():
    return jnp.stack([lax.axis_index("ctx"), lax.axis_index("exp") % X_LO]).astype(jnp.int32)


def attention_stats(own, tokens, queries, grads, flat):
    keys, lanes = flat.shape[0], queries.shape[0]
    return pl.pallas_call(
        functools.partial(stats_body, own, lax.axis_size("ctx"), tokens),
        out_shape=jax.ShapeDtypeStruct((8, lanes), F32),
        in_specs=[SMEM, VMEM, VMEM, VMEM],
        out_specs=VMEM,
        compiler_params=pltpu.CompilerParams(vmem_limit_bytes=24 * 2**20),
        cost_estimate=pl.CostEstimate(
            flops=4 * keys * lanes * flat.shape[1] // 2,
            bytes_accessed=2 * flat.size,
            transcendentals=keys * lanes,
        ),
        name="attention_stats",
    )(here(), queries, grads, flat)


def attention_grads(own, tokens, queries, grads, flat, stats, far):
    keys, lanes = flat.shape[0], queries.shape[0]
    size = flat.shape[1] // 2
    return pl.pallas_call(
        functools.partial(grads_body, own, lax.axis_size("ctx"), tokens),
        out_shape=(
            jax.ShapeDtypeStruct((keys, 2 * size), BF),
            jax.ShapeDtypeStruct((lanes, size), F32),
        ),
        in_specs=[SMEM] + [VMEM] * 5,
        out_specs=(VMEM, VMEM),
        compiler_params=pltpu.CompilerParams(vmem_limit_bytes=24 * 2**20),
        cost_estimate=pl.CostEstimate(
            flops=10 * keys * lanes * size,
            bytes_accessed=4 * flat.size,
            transcendentals=keys * lanes,
        ),
        name="attention_grads",
    )(here(), queries, grads, flat, stats, far)


def by_head(rows):
    return jnp.swapaxes(rows, 0, 1).reshape(-1, rows.shape[2])


def ctx_sum(both, masks):
    for mask in reversed(masks):
        half = both.shape[0] // 2
        sent = both[half:].astype(BF if half >= both.shape[1] // 2 else F32)
        both = both[:half] + swap(sent, mask).astype(F32)
    return both


def own_grads(both):
    head_dim = both.shape[1] // 2
    grad_key = (both[:, :head_dim] * head_dim ** (-0.5)).astype(BF)[:, None, :]
    grad_value = both[:, head_dim:].astype(BF)[:, None, :]
    return grad_key, grad_value


def select(moe_input, moe_grad, expert_ids, router_weight):
    width = moe_input.shape[1]
    exp_size = lax.axis_size("exp")
    matches = expert_ids[:, :, None] == jnp.arange(exp_size)[None, None, :]
    member = jnp.sum(matches.astype(jnp.int32), axis=1)
    weight_row = jnp.sum(jnp.where(matches, router_weight[:, :, None], 0.0), axis=1)
    slot_rank = jnp.cumsum(member, axis=0) - member
    placed = (member[:, :, None] == 1) & (
        slot_rank[:, :, None] == jnp.arange(CAP)[None, None, :]
    )
    slot_weight = jnp.sum(jnp.where(placed, weight_row[:, :, None], 0.0), axis=0)
    placed_low = placed.astype(BF).reshape(-1, exp_size * CAP)
    rows = jnp.concatenate([moe_input, moe_grad], axis=1)
    picked = jnp.einsum("bs,bd->sd", placed_low, rows, preferred_element_type=F32)
    scaled = picked[:, width:] * slot_weight.reshape(-1, 1)
    sent = jnp.concatenate([picked[:, :width].astype(BF), scaled.astype(BF)], axis=1)
    got = lax.all_to_all(sent.reshape(exp_size, CAP, 2 * width), "exp", 0, 0, tiled=True)
    return placed_low, got


def project(got, gate_weight, up_weight, down_weight):
    ring = lax.axis_size("ctx") // X_HI
    at = lax.axis_index("ctx") % ring
    half = lax.axis_index("head")
    units = gate_weight.shape[2] // lax.axis_size("head")
    width = got.shape[2] // 2
    got = turn(got.reshape(ring, -1, 2 * width), at).reshape(-1, 2 * width)
    input_rows, grad_rows = got[:, :width], got[:, width:]
    gate_mat = lax.dynamic_slice_in_dim(gate_weight[0], half * units, units, 1)
    up_mat = lax.dynamic_slice_in_dim(up_weight[0], half * units, units, 1)
    down_mat = lax.dynamic_slice_in_dim(down_weight[0], half * units, units, 0)
    gate_part = jnp.dot(input_rows, gate_mat, preferred_element_type=F32).astype(BF)
    up_part = jnp.dot(input_rows, up_mat, preferred_element_type=F32).astype(BF)
    back_part = jnp.einsum("rd,fd->rf", grad_rows, down_mat, preferred_element_type=F32).astype(BF)
    parts = jnp.concatenate([gate_part, up_part, back_part], axis=1).reshape(ring, -1, 3 * units)
    return input_rows, grad_rows, gate_mat, up_mat, [parts[j] for j in range(ring)]


def act_block(total):
    units = total.shape[1] // 3
    hidden, d_gate, d_up = activate(
        total[:, :units], total[:, units : 2 * units], total[:, 2 * units :]
    )
    return jnp.concatenate([hidden, d_gate, d_up], axis=1)


def finish(full, input_rows, grad_rows, gate_mat, up_mat, placed_low, sums):
    exp_size, head_size = lax.axis_size("exp"), lax.axis_size("head")
    ring = lax.axis_size("ctx") // X_HI
    at = lax.axis_index("ctx") % ring
    half = lax.axis_index("head")
    units = full.shape[1] // 3
    columns = input_rows.shape[1] // head_size
    hidden, d_gate, d_up = full[:, :units], full[:, units : 2 * units], full[:, 2 * units :]
    contrib = jnp.einsum("rf,df->rd", d_gate, gate_mat, preferred_element_type=F32)
    contrib = contrib + jnp.einsum("rf,df->rd", d_up, up_mat, preferred_element_type=F32)
    mine = lax.dynamic_slice_in_dim(contrib, half * columns, columns, 1)
    other = lax.dynamic_slice_in_dim(contrib, (1 - half) * columns, columns, 1).astype(BF)
    mine = (mine + lax.ppermute(other, "head", [(0, 1), (1, 0)]).astype(F32)).astype(BF)
    mine = turn(mine.reshape(ring, -1, columns), (ring - at) % ring).reshape(exp_size, CAP, columns)
    input_rows, grad_rows = after(input_rows, mine), after(grad_rows, mine)
    sums = ctx_sum(after(sums, mine), MASKS[:2])
    back_rows = lax.all_to_all(mine, "exp", 0, 0, tiled=True)
    grad_input = jnp.dot(
        placed_low, back_rows.reshape(-1, columns), preferred_element_type=F32
    ).astype(BF)
    grad_gate = jnp.einsum("rd,rf->df", input_rows, d_gate, preferred_element_type=F32).astype(BF)
    grad_up = jnp.einsum("rd,rf->df", input_rows, d_up, preferred_element_type=F32).astype(BF)
    grad_down = jnp.einsum("rf,rd->fd", hidden, grad_rows, preferred_element_type=F32).astype(BF)
    return grad_input, grad_gate[None], grad_up[None], grad_down[None], sums


def shards(
    queries,
    key_rows,
    value_vector_rows,
    grad_attn,
    moe_input,
    moe_grad,
    expert_ids,
    router_weight,
    gate_weight,
    up_weight,
    down_weight,
):
    tokens, own = queries.shape[0], key_rows.shape[0]
    rows = tokens * queries.shape[1]
    size = queries.shape[2]
    pair = jnp.concatenate([key_rows[:, 0, :], value_vector_rows[:, 0, :]], axis=1)
    near = ctx_gather(pair, MASKS)
    placed_low, got = select(moe_input, moe_grad, expert_ids, router_weight)
    mine = jnp.concatenate([by_head(queries), by_head(grad_attn)], axis=0)
    theirs = beside(mine)
    flat = y_gather(after(near, got, theirs)).reshape(-1, near.shape[1])
    queries = jnp.concatenate([mine[:rows], theirs[:rows]], axis=0)
    grads = jnp.concatenate([mine[rows:], theirs[rows:]], axis=0)
    input_rows, grad_rows, gate_mat, up_mat, parts = project(
        got, gate_weight, up_weight, down_weight
    )
    onward, back = sum_start(parts)
    onward, back = after(onward, near), after(back, near)
    for step in range(len(parts) // 2):
        if step == 3:
            onward, back = after(onward, flat), after(back, flat)
        onward, back = sum_step(parts, step, onward, back)
    total = onward.astype(F32) + back.astype(F32) + parts[0].astype(F32)
    other = opposite(total.astype(BF))
    stats = attention_stats(own, tokens, queries, grads, flat)
    block = act_block(total + after(other, stats).astype(F32))
    both, grad_query = attention_grads(
        own, tokens, queries, grads, flat, stats, beside(stats)
    )
    sums = y_sum(both.reshape((-1,) + near.shape))
    blocks = ring_gather(block, {2: both, 4: sums})
    sums = ctx_sum(sums, MASKS[3:])
    full = after(jnp.concatenate(blocks, axis=0), sums)
    sums = ctx_sum(sums, MASKS[2:3])
    of_experts = finish(full, input_rows, grad_rows, gate_mat, up_mat, placed_low, sums)
    grad_query = grad_query[:rows] + beside(grad_query[rows:].astype(BF)).astype(F32)
    grad_query = jnp.swapaxes(grad_query.astype(BF).reshape(-1, tokens, size), 0, 1)
    grad_key, grad_value = own_grads(of_experts[-1])
    return (grad_query, grad_key, grad_value) + of_experts[:-1]


def solution(mesh):
    placed = (
        P("ctx", ("head", "exp"), None),
        P(("ctx", "exp"), "head", None),
        P(("ctx", "exp"), "head", None),
        P("ctx", ("head", "exp"), None),
        P("exp", "ctx"),
        P("exp", "ctx"),
        P("exp", None),
        P("exp", None),
        P("exp", "ctx", None),
        P("exp", "ctx", None),
        P("exp", None, "ctx"),
    )
    return jax.shard_map(
        shards,
        mesh=mesh,
        in_specs=placed,
        out_specs=(
            P("ctx", ("head", "exp"), None),
            P(("ctx", "exp"), "head", None),
            P(("ctx", "exp"), "head", None),
            P("exp", ("ctx", "head")),
            P("exp", "ctx", "head"),
            P("exp", "ctx", "head"),
            P("exp", "head", "ctx"),
        ),
        check_vma=False,
    )
```

```python
import functools

import jax
import jax.numpy as jnp
from jax import lax
from jax.experimental import pallas as pl
from jax.experimental.pallas import tpu as pltpu
from jax.sharding import PartitionSpec as P

CAP = 48
X_HI = 2
X_LO = 2
MASKED = -1e30
MASKS = (4, 2, 8, 1)
BF = jnp.bfloat16
F32 = jnp.float32


def activate(gate_val, up_val, back_val):
    sigmoid_gate = jax.nn.sigmoid(gate_val)
    hidden = (gate_val * sigmoid_gate * up_val).astype(BF)
    d_up = (back_val * gate_val * sigmoid_gate).astype(BF)
    d_gate = (back_val * up_val * sigmoid_gate * (1.0 + gate_val * (1.0 - sigmoid_gate))).astype(BF)
    return (hidden, d_gate, d_up)


def y_groups():
    n = lax.axis_size("exp")
    return [list(range(x, n, X_LO)) for x in range(X_LO)]


def y_gather(block):
    n = lax.axis_size("exp") // X_LO
    copies = jnp.broadcast_to(block[None], (n,) + block.shape)
    return lax.all_to_all(copies, "exp", 0, 0, tiled=True, axis_index_groups=y_groups())


def y_sum(parts):
    got = lax.all_to_all(parts, "exp", 0, 0, tiled=True, axis_index_groups=y_groups())
    return jnp.sum(got.astype(F32), axis=0)


def beside(block):
    return lax.ppermute(block, "exp", [(e, e ^ 1) for e in range(lax.axis_size("exp"))])


def z_shift(step):
    n = lax.axis_size("ctx") // X_HI
    return [(h * n + z, h * n + (z + step) % n) for h in range(X_HI) for z in range(n)]


def right(block):
    return lax.ppermute(block, "ctx", z_shift(1))


def left(block):
    return lax.ppermute(block, "ctx", z_shift(-1))


def opposite(block):
    n = lax.axis_size("ctx")
    return lax.ppermute(block, "ctx", [(c, (c + n // X_HI) % n) for c in range(n)])


def after(block, *others):
    return lax.optimization_barrier((block,) + others)[0]


def add_low(a, b):
    return (a.astype(F32) + b.astype(F32)).astype(BF)


def sum_start(parts):
    far = len(parts) // 2
    cut = parts[0].shape[1] // 2
    return parts[far][:, :cut], parts[far][:, cut:]


def sum_step(parts, step, onward, back):
    n = len(parts)
    far = n // 2
    cut = parts[0].shape[1] // 2
    onward, back = right(onward), left(back)
    ahead, behind = parts[far - 1 - step], parts[(far + 1 + step) % n]
    if step == 0:
        onward = jnp.concatenate([add_low(onward, ahead[:, :cut]), ahead[:, cut:]], axis=1)
        back = jnp.concatenate([behind[:, :cut], add_low(back, behind[:, cut:])], axis=1)
    elif step < far - 1:
        onward, back = add_low(onward, ahead), add_low(back, behind)
    return onward, back


def ring_gather(block, waits):
    n = lax.axis_size("ctx") // X_HI
    far = n // 2
    cut = block.shape[1] // 2
    blocks = [block] + [None] * (n - 1)
    onward = back = block
    for step in range(1, far):
        if step in waits:
            onward, back = after(onward, waits[step]), after(back, waits[step])
        onward, back = right(onward), left(back)
        blocks[n - step], blocks[step] = onward, back
    if far in waits:
        onward, back = after(onward, waits[far]), after(back, waits[far])
    blocks[far : far + 1] = [right(onward[:, :cut]), left(back[:, cut:])]
    return blocks


def turn(blocks, places):
    twice = jnp.concatenate([blocks, blocks], axis=0)
    return lax.dynamic_slice_in_dim(twice, places, blocks.shape[0], 0)


def swap(block, mask):
    return lax.ppermute(block, "ctx", [(c, c ^ mask) for c in range(lax.axis_size("ctx"))])


def ctx_gather(block, masks):
    for mask in masks:
        block = jnp.concatenate([block, swap(block, mask)], axis=0)
    return block


def mask_of(index):
    return sum((index >> bit) % 2 * mask for bit, mask in enumerate(MASKS))


def scores_of(step, own, ctx_size, tokens, here_ref, k, q):
    lanes = q.shape[0]
    found = lax.dot_general(k, q, (((1,), (1,)), ((), ())), preferred_element_type=F32)
    ahead = lax.broadcasted_iota(jnp.int32, (own, lanes), 1) % tokens - lax.broadcasted_iota(
        jnp.int32, (own, lanes), 0
    )
    me, side = here_ref[0], here_ref[1]
    parts = k.shape[0] // own
    masked = []
    for part in range(parts):
        place = step * parts + part
        start = (me ^ mask_of(place % ctx_size)) * tokens + (place // ctx_size * X_LO + side) * own
        masked.append(
            jnp.where(
                ahead >= start - me * tokens,
                found[part * own : (part + 1) * own] * k.shape[1] ** (-0.5),
                MASKED,
            )
        )
    return jnp.concatenate(masked, axis=0)


def stats_body(own, ctx_size, tokens, here_ref, q_ref, g_ref, kv_ref, stats_ref):
    size = kv_ref.shape[1] // 2
    lanes = q_ref.shape[0]
    chunk = 8 * own

    def one(step, held):
        top, norm, delta = held
        rows = pl.ds(pl.multiple_of(step * chunk, chunk), chunk)
        scores = scores_of(step, own, ctx_size, tokens, here_ref, kv_ref[rows, :size], q_ref[...])
        dprob = lax.dot_general(
            kv_ref[rows, size:], g_ref[...], (((1,), (1,)), ((), ())), preferred_element_type=F32
        )
        scores, dprob = scores.reshape(-1, 8, lanes), dprob.reshape(-1, 8, lanes)
        higher = jnp.maximum(top, jnp.max(scores, axis=0))
        shrink = jnp.exp(top - higher)
        prob = jnp.exp(scores - higher[None])
        norm = norm * shrink + jnp.sum(prob, axis=0)
        delta = delta * shrink + jnp.sum(prob * dprob, axis=0)
        return higher, norm, delta

    zero = jnp.zeros((8, lanes), F32)
    top, norm, delta = lax.fori_loop(0, kv_ref.shape[0] // chunk, one, (zero + MASKED, zero, zero))
    highest = jnp.max(top, axis=0, keepdims=True)
    shrink = jnp.exp(top - highest)
    stats_ref[0:1, :] = highest
    stats_ref[1:2, :] = jnp.sum(norm * shrink, axis=0, keepdims=True)
    stats_ref[2:3, :] = jnp.sum(delta * shrink, axis=0, keepdims=True)
    stats_ref[3:, :] = jnp.zeros((5, lanes), F32)


def grads_body(
    own, ctx_size, tokens, here_ref, q_ref, g_ref, kv_ref, stats_ref, far_ref, both_ref, dq_ref
):
    size = kv_ref.shape[1] // 2
    lanes = q_ref.shape[0]
    chunk = 8 * own
    far = jnp.concatenate([far_ref[:, lanes // 2 :], far_ref[:, : lanes // 2]], axis=1)
    near = stats_ref[...]
    top = jnp.maximum(near[0:1], far[0:1])
    shrink_near, shrink_far = jnp.exp(near[0:1] - top), jnp.exp(far[0:1] - top)
    inverse = 1.0 / (near[1:2] * shrink_near + far[1:2] * shrink_far)
    delta = (near[2:3] * shrink_near + far[2:3] * shrink_far) * inverse

    def one(step, total):
        rows = pl.ds(pl.multiple_of(step * chunk, chunk), chunk)
        k = kv_ref[rows, :size]
        scores = scores_of(step, own, ctx_size, tokens, here_ref, k, q_ref[...])
        prob = jnp.exp(scores - top) * inverse
        both_ref[rows, size:] = jnp.dot(
            prob.astype(BF), g_ref[...], preferred_element_type=F32
        ).astype(BF)
        dprob = lax.dot_general(
            kv_ref[rows, size:], g_ref[...], (((1,), (1,)), ((), ())), preferred_element_type=F32
        )
        dscore = (prob * (dprob - delta)).astype(BF)
        both_ref[rows, :size] = jnp.dot(dscore, q_ref[...], preferred_element_type=F32).astype(BF)
        return total + lax.dot_general(
            k, dscore, (((0,), (0,)), ((), ())), preferred_element_type=F32
        )

    total = lax.fori_loop(0, kv_ref.shape[0] // chunk, one, jnp.zeros((size, lanes), F32))
    dq_ref[...] = (total * size ** (-0.5)).T


VMEM = pl.BlockSpec(memory_space=pltpu.VMEM)
SMEM = pl.BlockSpec(memory_space=pltpu.SMEM)


def here():
    return jnp.stack([lax.axis_index("ctx"), lax.axis_index("exp") % X_LO]).astype(jnp.int32)


def attention_stats(own, tokens, queries, grads, flat):
    keys, lanes = flat.shape[0], queries.shape[0]
    return pl.pallas_call(
        functools.partial(stats_body, own, lax.axis_size("ctx"), tokens),
        out_shape=jax.ShapeDtypeStruct((8, lanes), F32),
        in_specs=[SMEM, VMEM, VMEM, VMEM],
        out_specs=VMEM,
        compiler_params=pltpu.CompilerParams(vmem_limit_bytes=24 * 2**20),
        cost_estimate=pl.CostEstimate(
            flops=4 * keys * lanes * flat.shape[1] // 2,
            bytes_accessed=2 * flat.size,
            transcendentals=keys * lanes,
        ),
        name="attention_stats",
    )(here(), queries, grads, flat)


def attention_grads(own, tokens, queries, grads, flat, stats, far):
    keys, lanes = flat.shape[0], queries.shape[0]
    size = flat.shape[1] // 2
    return pl.pallas_call(
        functools.partial(grads_body, own, lax.axis_size("ctx"), tokens),
        out_shape=(
            jax.ShapeDtypeStruct((keys, 2 * size), BF),
            jax.ShapeDtypeStruct((lanes, size), F32),
        ),
        in_specs=[SMEM] + [VMEM] * 5,
        out_specs=(VMEM, VMEM),
        compiler_params=pltpu.CompilerParams(vmem_limit_bytes=24 * 2**20),
        cost_estimate=pl.CostEstimate(
            flops=10 * keys * lanes * size,
            bytes_accessed=4 * flat.size,
            transcendentals=keys * lanes,
        ),
        name="attention_grads",
    )(here(), queries, grads, flat, stats, far)


def by_head(rows):
    return jnp.swapaxes(rows, 0, 1).reshape(-1, rows.shape[2])


def ctx_sum(both, masks):
    for mask in reversed(masks):
        half = both.shape[0] // 2
        sent = both[half:].astype(BF if half >= both.shape[1] // 2 else F32)
        both = both[:half] + swap(sent, mask).astype(F32)
    return both


def own_grads(both):
    head_dim = both.shape[1] // 2
    grad_key = (both[:, :head_dim] * head_dim ** (-0.5)).astype(BF)[:, None, :]
    grad_value = both[:, head_dim:].astype(BF)[:, None, :]
    return grad_key, grad_value


def select(moe_input, moe_grad, expert_ids, router_weight):
    width = moe_input.shape[1]
    exp_size = lax.axis_size("exp")
    matches = expert_ids[:, :, None] == jnp.arange(exp_size)[None, None, :]
    member = jnp.sum(matches.astype(jnp.int32), axis=1)
    weight_row = jnp.sum(jnp.where(matches, router_weight[:, :, None], 0.0), axis=1)
    slot_rank = jnp.cumsum(member, axis=0) - member
    placed = (member[:, :, None] == 1) & (
        slot_rank[:, :, None] == jnp.arange(CAP)[None, None, :]
    )
    slot_weight = jnp.sum(jnp.where(placed, weight_row[:, :, None], 0.0), axis=0)
    placed_low = placed.astype(BF).reshape(-1, exp_size * CAP)
    rows = jnp.concatenate([moe_input, moe_grad], axis=1)
    picked = jnp.einsum("bs,bd->sd", placed_low, rows, preferred_element_type=F32)
    scaled = picked[:, width:] * slot_weight.reshape(-1, 1)
    sent = jnp.concatenate([picked[:, :width].astype(BF), scaled.astype(BF)], axis=1)
    got = lax.all_to_all(sent.reshape(exp_size, CAP, 2 * width), "exp", 0, 0, tiled=True)
    return placed_low, got


def project(got, gate_weight, up_weight, down_weight):
    ring = lax.axis_size("ctx") // X_HI
    at = lax.axis_index("ctx") % ring
    half = lax.axis_index("head")
    units = gate_weight.shape[2] // lax.axis_size("head")
    width = got.shape[2] // 2
    got = turn(got.reshape(ring, -1, 2 * width), at).reshape(-1, 2 * width)
    input_rows, grad_rows = got[:, :width], got[:, width:]
    gate_mat = lax.dynamic_slice_in_dim(gate_weight[0], half * units, units, 1)
    up_mat = lax.dynamic_slice_in_dim(up_weight[0], half * units, units, 1)
    down_mat = lax.dynamic_slice_in_dim(down_weight[0], half * units, units, 0)
    gate_part = jnp.dot(input_rows, gate_mat, preferred_element_type=F32).astype(BF)
    up_part = jnp.dot(input_rows, up_mat, preferred_element_type=F32).astype(BF)
    back_part = jnp.einsum("rd,fd->rf", grad_rows, down_mat, preferred_element_type=F32).astype(BF)
    parts = jnp.concatenate([gate_part, up_part, back_part], axis=1).reshape(ring, -1, 3 * units)
    return input_rows, grad_rows, gate_mat, up_mat, [parts[j] for j in range(ring)]


def act_block(total):
    units = total.shape[1] // 3
    hidden, d_gate, d_up = activate(
        total[:, :units], total[:, units : 2 * units], total[:, 2 * units :]
    )
    return jnp.concatenate([hidden, d_gate, d_up], axis=1)


def contrib_body(width, half_ref, gate_ref, up_ref, *refs):
    blocks, (mine_ref, other_ref, full_ref) = refs[:-3], refs[-3:]
    height = blocks[0].shape[0]
    units = full_ref.shape[1] // 3
    row = 0
    halves = [block for block in blocks if block.shape[1] < full_ref.shape[1]]
    for block in blocks:
        if block is halves[0]:
            cut = block.shape[1]
            full_ref[row : row + height, :cut] = block[...]
            continue
        if block is halves[1]:
            full_ref[row : row + height, cut:] = block[...]
        else:
            full_ref[row : row + height, :] = block[...]
        row += height
    across = (((1,), (1,)), ((), ()))
    found = lax.dot_general(
        full_ref[:, units : 2 * units], gate_ref[...], across, preferred_element_type=F32
    ) + lax.dot_general(full_ref[:, 2 * units :], up_ref[...], across, preferred_element_type=F32)
    first = half_ref[0] == 0
    mine_ref[...] = jnp.where(first, found[:, :width], found[:, width:])
    other_ref[...] = jnp.where(first, found[:, width:], found[:, :width]).astype(BF)


def weights_body(full_ref, input_ref, grad_ref, gate_ref, up_ref, down_ref):
    units = full_ref.shape[1] // 3
    down = (((0,), (0,)), ((), ()))

    def product(a, b):
        return lax.dot_general(a, b, down, preferred_element_type=F32).astype(BF)

    gate_ref[0] = product(input_ref[...], full_ref[:, units : 2 * units])
    up_ref[0] = product(input_ref[...], full_ref[:, 2 * units :])
    down_ref[0] = product(full_ref[:, :units], grad_ref[...])


def contributions(blocks, gate_mat, up_mat):
    rows = len(blocks) // 2 * 2 * blocks[0].shape[0]
    columns = gate_mat.shape[0] // lax.axis_size("head")
    whole = blocks[0].shape[1]
    return pl.pallas_call(
        functools.partial(contrib_body, columns),
        out_shape=(
            jax.ShapeDtypeStruct((rows, columns), F32),
            jax.ShapeDtypeStruct((rows, columns), BF),
            jax.ShapeDtypeStruct((rows, whole), BF),
        ),
        in_specs=[SMEM] + [VMEM] * (2 + len(blocks)),
        out_specs=(VMEM,) * 3,
        compiler_params=pltpu.CompilerParams(vmem_limit_bytes=24 * 2**20),
        cost_estimate=pl.CostEstimate(
            flops=4 * rows * whole // 3 * gate_mat.shape[0],
            bytes_accessed=4 * rows * whole,
            transcendentals=0,
        ),
        name="expert_contrib",
    )(lax.axis_index("head").astype(jnp.int32).reshape(1), gate_mat, up_mat, *blocks)


def weight_grads(full, input_rows, grad_rows):
    units, width = full.shape[1] // 3, input_rows.shape[1]
    return pl.pallas_call(
        weights_body,
        out_shape=(
            jax.ShapeDtypeStruct((1, width, units), BF),
            jax.ShapeDtypeStruct((1, width, units), BF),
            jax.ShapeDtypeStruct((1, units, width), BF),
        ),
        in_specs=[VMEM] * 3,
        out_specs=(VMEM,) * 3,
        compiler_params=pltpu.CompilerParams(vmem_limit_bytes=24 * 2**20),
        cost_estimate=pl.CostEstimate(
            flops=6 * full.shape[0] * units * width,
            bytes_accessed=4 * full.size,
            transcendentals=0,
        ),
        name="expert_weight_grads",
    )(full, input_rows, grad_rows)


def finish(blocks, input_rows, grad_rows, gate_mat, up_mat, placed_low, sums):
    exp_size = lax.axis_size("exp")
    ring = lax.axis_size("ctx") // X_HI
    at = lax.axis_index("ctx") % ring
    mine, other, full = contributions(blocks, gate_mat, up_mat)
    columns = mine.shape[1]
    mine = (mine + lax.ppermute(other, "head", [(0, 1), (1, 0)]).astype(F32)).astype(BF)
    mine = turn(mine.reshape(ring, -1, columns), (ring - at) % ring).reshape(exp_size, CAP, columns)
    mine = after(mine, sums)
    back_rows = lax.all_to_all(mine, "exp", 0, 0, tiled=True)
    grad_input = jnp.dot(
        placed_low, back_rows.reshape(-1, columns), preferred_element_type=F32
    ).astype(BF)
    sums = ctx_sum(after(sums, mine), MASKS[:1])
    return (grad_input,) + tuple(weight_grads(after(full, mine), input_rows, grad_rows)) + (sums,)


def shards(
    queries,
    key_rows,
    value_vector_rows,
    grad_attn,
    moe_input,
    moe_grad,
    expert_ids,
    router_weight,
    gate_weight,
    up_weight,
    down_weight,
):
    tokens, own = queries.shape[0], key_rows.shape[0]
    rows = tokens * queries.shape[1]
    size = queries.shape[2]
    pair = jnp.concatenate([key_rows[:, 0, :], value_vector_rows[:, 0, :]], axis=1)
    near = ctx_gather(pair, MASKS)
    placed_low, got = select(moe_input, moe_grad, expert_ids, router_weight)
    mine = jnp.concatenate([by_head(queries), by_head(grad_attn)], axis=0)
    theirs = beside(mine)
    flat = y_gather(after(near, got)).reshape(-1, near.shape[1])
    queries = jnp.concatenate([mine[:rows], theirs[:rows]], axis=0)
    grads = jnp.concatenate([mine[rows:], theirs[rows:]], axis=0)
    input_rows, grad_rows, gate_mat, up_mat, parts = project(
        got, gate_weight, up_weight, down_weight
    )
    onward, back = sum_start(parts)
    onward, back = after(onward, near, theirs), after(back, near, theirs)
    onward, back = sum_step(parts, 0, onward, back)
    onward, back = sum_step(parts, 1, onward, back)
    onward, back = after(onward, flat), after(back, flat)
    stats = attention_stats(own, tokens, queries, grads, flat)
    onward, back = sum_step(parts, 2, onward, back)
    onward, back = sum_step(parts, 3, after(onward, stats), after(back, stats))
    total = onward.astype(F32) + back.astype(F32) + parts[0].astype(F32)
    other = opposite(total.astype(BF))
    both, grad_query = attention_grads(
        own, tokens, queries, grads, after(flat, total), stats, beside(stats)
    )
    block = act_block(total + after(other, both).astype(F32))
    sums = y_sum(both.reshape((-1,) + near.shape))
    blocks = ring_gather(block, {3: sums})
    sums = ctx_sum(sums, MASKS[2:])
    blocks[0] = after(block, sums)
    sums = ctx_sum(sums, MASKS[1:2])
    of_experts = finish(blocks, input_rows, grad_rows, gate_mat, up_mat, placed_low, sums)
    grad_query = grad_query[:rows] + beside(grad_query[rows:].astype(BF)).astype(F32)
    grad_query = jnp.swapaxes(grad_query.astype(BF).reshape(-1, tokens, size), 0, 1)
    grad_key, grad_value = own_grads(of_experts[-1])
    return (grad_query, grad_key, grad_value) + of_experts[:-1]


def solution(mesh):
    placed = (
        P("ctx", ("head", "exp"), None),
        P(("ctx", "exp"), "head", None),
        P(("ctx", "exp"), "head", None),
        P("ctx", ("head", "exp"), None),
        P("exp", "ctx"),
        P("exp", "ctx"),
        P("exp", None),
        P("exp", None),
        P("exp", "ctx", None),
        P("exp", "ctx", None),
        P("exp", None, "ctx"),
    )
    return jax.shard_map(
        shards,
        mesh=mesh,
        in_specs=placed,
        out_specs=(
            P("ctx", ("head", "exp"), None),
            P(("ctx", "exp"), "head", None),
            P(("ctx", "exp"), "head", None),
            P("exp", ("ctx", "head")),
            P("exp", "ctx", "head"),
            P("exp", "ctx", "head"),
            P("exp", "head", "ctx"),
        ),
        check_vma=False,
    )
```

```python
import functools

import jax
import jax.numpy as jnp
from jax import lax
from jax.experimental import pallas as pl
from jax.experimental.pallas import tpu as pltpu
from jax.sharding import PartitionSpec as P

CAP = 48
X_HI = 2
X_LO = 2
MASKED = -1e30
MASKS = (4, 2, 8, 1)
BF = jnp.bfloat16
F32 = jnp.float32


def activate(gate_val, up_val, back_val):
    sigmoid_gate = jax.nn.sigmoid(gate_val)
    hidden = (gate_val * sigmoid_gate * up_val).astype(BF)
    d_up = (back_val * gate_val * sigmoid_gate).astype(BF)
    d_gate = (back_val * up_val * sigmoid_gate * (1.0 + gate_val * (1.0 - sigmoid_gate))).astype(BF)
    return (hidden, d_gate, d_up)


VMEM = pl.BlockSpec(memory_space=pltpu.VMEM)
SMEM = pl.BlockSpec(memory_space=pltpu.SMEM)


def stack_body(*refs):
    row = 0
    for ref in refs[:-1]:
        refs[-1][row : row + ref.shape[0], :] = ref[...]
        row += ref.shape[0]


def stacked(*blocks):
    rows = sum(block.shape[0] for block in blocks)
    return pl.pallas_call(
        stack_body,
        out_shape=jax.ShapeDtypeStruct((rows,) + blocks[0].shape[1:], blocks[0].dtype),
        in_specs=[VMEM] * len(blocks),
        out_specs=VMEM,
        cost_estimate=pl.CostEstimate(
            flops=0, bytes_accessed=4 * rows * blocks[0].shape[1], transcendentals=0
        ),
        name="stack_rows",
    )(*blocks)


def beside(block):
    return lax.ppermute(block, "exp", [(e, e ^ 1) for e in range(lax.axis_size("exp"))])


def z_move(block, step):
    n = lax.axis_size("ctx") // X_HI
    pairs = [(h * n + z, h * n + (z + step) % n) for h in range(X_HI) for z in range(n)]
    return lax.ppermute(block, "ctx", pairs)


def y_move(block, step):
    n = lax.axis_size("exp")
    return lax.ppermute(block, "exp", [(e, (e + step * X_LO) % n) for e in range(n)])


def opposite(block):
    n = lax.axis_size("ctx")
    return lax.ppermute(block, "ctx", [(c, (c + n // X_HI) % n) for c in range(n)])


def after(block, *others):
    return lax.optimization_barrier((block,) + others)[0]


def add_low(a, b):
    return (a.astype(F32) + b.astype(F32)).astype(BF)


def sum_start(parts):
    far = len(parts) // 2
    cut = parts[0].shape[1] // 2
    return parts[far][:, :cut], parts[far][:, cut:]


def sum_step(move, parts, step, onward, back):
    n = len(parts)
    far = n // 2
    cut = parts[0].shape[1] // 2
    onward, back = move(onward, 1), move(back, -1)
    ahead, behind = parts[far - 1 - step], parts[(far + 1 + step) % n]
    if step == 0:
        onward = jnp.concatenate([add_low(onward, ahead[:, :cut]), ahead[:, cut:]], axis=1)
        back = jnp.concatenate([behind[:, :cut], add_low(back, behind[:, cut:])], axis=1)
    elif step < far - 1:
        onward, back = add_low(onward, ahead), add_low(back, behind)
    else:
        return onward.astype(F32) + back.astype(F32) + parts[0].astype(F32)
    return onward, back


def ring_step(move, onward, back):
    return move(onward, 1), move(back, -1)


def ring_last(move, onward, back):
    cut = onward.shape[1] // 2
    return move(onward[:, :cut], 1), move(back[:, cut:], -1)


def both_after(onward, back, *others):
    return lax.optimization_barrier((onward, back) + others)[:2]


def turn(blocks, places):
    twice = jnp.concatenate([blocks, blocks], axis=0)
    return lax.dynamic_slice_in_dim(twice, places, blocks.shape[0], 0)


def swap(block, mask):
    return lax.ppermute(block, "ctx", [(c, c ^ mask) for c in range(lax.axis_size("ctx"))])


def fours(masks):
    return ((1, masks[0]), (2, masks[1]), (3, masks[0] ^ masks[1]))


def ctx_gather(block, masks):
    return stacked(block, *[swap(block, mask) for _, mask in fours(masks)])


def ctx_sum(both, masks):
    quarter = both.shape[0] // 4
    wire = BF if quarter >= both.shape[1] // 2 else F32
    total = both[:quarter]
    for place, mask in fours(masks):
        sent = both[place * quarter : (place + 1) * quarter].astype(wire)
        total = total + swap(sent, mask).astype(F32)
    return total


def mask_of(index):
    return sum((index >> bit) % 2 * mask for bit, mask in enumerate(MASKS))


def scores_of(step, own, ctx_size, tokens, here_ref, k, q):
    lanes = q.shape[0]
    found = lax.dot_general(k, q, (((1,), (1,)), ((), ())), preferred_element_type=F32)
    ahead = lax.broadcasted_iota(jnp.int32, (own, lanes), 1) % tokens - lax.broadcasted_iota(
        jnp.int32, (own, lanes), 0
    )
    me, side, row, rows = here_ref[0], here_ref[1], here_ref[2], here_ref[3]
    parts = k.shape[0] // own
    masked = []
    for part in range(parts):
        place = step * parts + part
        at = (row + place // ctx_size) % rows * X_LO + side
        start = (me ^ mask_of(place % ctx_size)) * tokens + at * own
        masked.append(
            jnp.where(
                ahead >= start - me * tokens,
                found[part * own : (part + 1) * own] * k.shape[1] ** (-0.5),
                MASKED,
            )
        )
    return jnp.concatenate(masked, axis=0)


def stats_body(own, ctx_size, tokens, here_ref, q_ref, g_ref, kv_ref, stats_ref):
    size = kv_ref.shape[1] // 2
    lanes = q_ref.shape[0]
    chunk = 8 * own

    def one(step, held):
        top, norm, delta = held
        rows = pl.ds(pl.multiple_of(step * chunk, chunk), chunk)
        scores = scores_of(step, own, ctx_size, tokens, here_ref, kv_ref[rows, :size], q_ref[...])
        dprob = lax.dot_general(
            kv_ref[rows, size:], g_ref[...], (((1,), (1,)), ((), ())), preferred_element_type=F32
        )
        scores, dprob = scores.reshape(-1, 8, lanes), dprob.reshape(-1, 8, lanes)
        higher = jnp.maximum(top, jnp.max(scores, axis=0))
        shrink = jnp.exp(top - higher)
        prob = jnp.exp(scores - higher[None])
        norm = norm * shrink + jnp.sum(prob, axis=0)
        delta = delta * shrink + jnp.sum(prob * dprob, axis=0)
        return higher, norm, delta

    zero = jnp.zeros((8, lanes), F32)
    top, norm, delta = lax.fori_loop(0, kv_ref.shape[0] // chunk, one, (zero + MASKED, zero, zero))
    highest = jnp.max(top, axis=0, keepdims=True)
    shrink = jnp.exp(top - highest)
    stats_ref[0:1, :] = highest
    stats_ref[1:2, :] = jnp.sum(norm * shrink, axis=0, keepdims=True)
    stats_ref[2:3, :] = jnp.sum(delta * shrink, axis=0, keepdims=True)
    stats_ref[3:, :] = jnp.zeros((5, lanes), F32)


def grads_body(
    own, ctx_size, tokens, here_ref, q_ref, g_ref, kv_ref, stats_ref, far_ref, both_ref, dq_ref
):
    size = kv_ref.shape[1] // 2
    lanes = q_ref.shape[0]
    chunk = 8 * own
    far = jnp.concatenate([far_ref[:, lanes // 2 :], far_ref[:, : lanes // 2]], axis=1)
    near = stats_ref[...]
    top = jnp.maximum(near[0:1], far[0:1])
    shrink_near, shrink_far = jnp.exp(near[0:1] - top), jnp.exp(far[0:1] - top)
    inverse = 1.0 / (near[1:2] * shrink_near + far[1:2] * shrink_far)
    delta = (near[2:3] * shrink_near + far[2:3] * shrink_far) * inverse

    def one(step, total):
        rows = pl.ds(pl.multiple_of(step * chunk, chunk), chunk)
        k = kv_ref[rows, :size]
        scores = scores_of(step, own, ctx_size, tokens, here_ref, k, q_ref[...])
        prob = jnp.exp(scores - top) * inverse
        both_ref[rows, size:] = jnp.dot(
            prob.astype(BF), g_ref[...], preferred_element_type=F32
        ).astype(BF)
        dprob = lax.dot_general(
            kv_ref[rows, size:], g_ref[...], (((1,), (1,)), ((), ())), preferred_element_type=F32
        )
        dscore = (prob * (dprob - delta)).astype(BF)
        both_ref[rows, :size] = jnp.dot(dscore, q_ref[...], preferred_element_type=F32).astype(BF)
        return total + lax.dot_general(
            k, dscore, (((0,), (0,)), ((), ())), preferred_element_type=F32
        )

    total = lax.fori_loop(0, kv_ref.shape[0] // chunk, one, jnp.zeros((size, lanes), F32))
    dq_ref[...] = (total * size ** (-0.5)).T


def here():
    exp, n = lax.axis_index("exp"), lax.axis_size("exp")
    return jnp.stack(
        [lax.axis_index("ctx"), exp % X_LO, exp // X_LO, jnp.int32(n // X_LO)]
    ).astype(jnp.int32)


def attention_stats(own, tokens, queries, grads, flat):
    keys, lanes = flat.shape[0], queries.shape[0]
    return pl.pallas_call(
        functools.partial(stats_body, own, lax.axis_size("ctx"), tokens),
        out_shape=jax.ShapeDtypeStruct((8, lanes), F32),
        in_specs=[SMEM, VMEM, VMEM, VMEM],
        out_specs=VMEM,
        compiler_params=pltpu.CompilerParams(vmem_limit_bytes=24 * 2**20),
        cost_estimate=pl.CostEstimate(
            flops=4 * keys * lanes * flat.shape[1] // 2,
            bytes_accessed=2 * flat.size,
            transcendentals=keys * lanes,
        ),
        name="attention_stats",
    )(here(), queries, grads, flat)


def attention_grads(own, tokens, queries, grads, flat, stats, far):
    keys, lanes = flat.shape[0], queries.shape[0]
    size = flat.shape[1] // 2
    return pl.pallas_call(
        functools.partial(grads_body, own, lax.axis_size("ctx"), tokens),
        out_shape=(
            jax.ShapeDtypeStruct((keys, 2 * size), BF),
            jax.ShapeDtypeStruct((lanes, size), F32),
        ),
        in_specs=[SMEM] + [VMEM] * 5,
        out_specs=(VMEM, VMEM),
        compiler_params=pltpu.CompilerParams(vmem_limit_bytes=24 * 2**20),
        cost_estimate=pl.CostEstimate(
            flops=10 * keys * lanes * size,
            bytes_accessed=4 * flat.size,
            transcendentals=keys * lanes,
        ),
        name="attention_grads",
    )(here(), queries, grads, flat, stats, far)


def by_head(rows):
    return jnp.swapaxes(rows, 0, 1).reshape(-1, rows.shape[2])


def own_grads(both):
    head_dim = both.shape[1] // 2
    grad_key = (both[:, :head_dim] * head_dim ** (-0.5)).astype(BF)[:, None, :]
    grad_value = both[:, head_dim:].astype(BF)[:, None, :]
    return grad_key, grad_value


def select(moe_input, moe_grad, expert_ids, router_weight, near):
    width = moe_input.shape[1]
    exp_size = lax.axis_size("exp")
    matches = expert_ids[:, :, None] == jnp.arange(exp_size)[None, None, :]
    member = jnp.sum(matches.astype(jnp.int32), axis=1)
    weight_row = jnp.sum(jnp.where(matches, router_weight[:, :, None], 0.0), axis=1)
    slot_rank = jnp.cumsum(member, axis=0) - member
    placed = (member[:, :, None] == 1) & (
        slot_rank[:, :, None] == jnp.arange(CAP)[None, None, :]
    )
    slot_weight = jnp.sum(jnp.where(placed, weight_row[:, :, None], 0.0), axis=0)
    placed_low = placed.astype(BF).reshape(-1, exp_size * CAP)
    rows = jnp.concatenate([moe_input, moe_grad], axis=1)
    picked = jnp.einsum("bs,bd->sd", placed_low, rows, preferred_element_type=F32)
    scaled = picked[:, width:] * slot_weight.reshape(-1, 1)
    sent = jnp.concatenate([picked[:, :width].astype(BF), scaled.astype(BF)], axis=1)
    sent = after(sent, near)
    got = lax.all_to_all(sent.reshape(exp_size, CAP, 2 * width), "exp", 0, 0, tiled=True)
    return placed_low, got


def project(got, gate_weight, up_weight, down_weight):
    ctx_size = lax.axis_size("ctx")
    half = lax.axis_index("head")
    units = gate_weight.shape[2] // lax.axis_size("head")
    width = got.shape[2] // 2
    got = jnp.swapaxes(got.reshape(ctx_size // X_HI, X_HI, -1, 2 * width), 0, 1)
    got = got.reshape(-1, 2 * width)
    input_rows, grad_rows = got[:, :width], got[:, width:]
    gate_mat = lax.dynamic_slice_in_dim(gate_weight[0], half * units, units, 1)
    up_mat = lax.dynamic_slice_in_dim(up_weight[0], half * units, units, 1)
    down_mat = lax.dynamic_slice_in_dim(down_weight[0], half * units, units, 0)
    gate_part = jnp.dot(input_rows, gate_mat, preferred_element_type=F32).astype(BF)
    up_part = jnp.dot(input_rows, up_mat, preferred_element_type=F32).astype(BF)
    back_part = jnp.einsum("rd,fd->rf", grad_rows, down_mat, preferred_element_type=F32).astype(BF)
    parts = jnp.concatenate([gate_part, up_part, back_part], axis=1)
    return gate_mat, up_mat, parts.reshape(ctx_size, -1, 3 * units)


def act_block(total):
    units = total.shape[1] // 3
    hidden, d_gate, d_up = activate(
        total[:, :units], total[:, units : 2 * units], total[:, 2 * units :]
    )
    return jnp.concatenate([hidden, d_gate, d_up], axis=1)


def contrib_body(width, half_ref, gate_ref, up_ref, *refs):
    blocks, (mine_ref, other_ref, full_ref) = refs[:-3], refs[-3:]
    height = blocks[0].shape[0]
    units = full_ref.shape[1] // 3
    row = 0
    halves = [block for block in blocks if block.shape[1] < full_ref.shape[1]]
    for block in blocks:
        if block is halves[0]:
            cut = block.shape[1]
            full_ref[row : row + height, :cut] = block[...]
            continue
        if block is halves[1]:
            full_ref[row : row + height, cut:] = block[...]
        else:
            full_ref[row : row + height, :] = block[...]
        row += height
    across = (((1,), (1,)), ((), ()))
    found = lax.dot_general(
        full_ref[:, units : 2 * units], gate_ref[...], across, preferred_element_type=F32
    ) + lax.dot_general(full_ref[:, 2 * units :], up_ref[...], across, preferred_element_type=F32)
    first = half_ref[0] == 0
    mine_ref[...] = jnp.where(first, found[:, :width], found[:, width:])
    other_ref[...] = jnp.where(first, found[:, width:], found[:, :width]).astype(BF)


def weights_body(full_ref, input_ref, grad_ref, gate_ref, up_ref, down_ref):
    units = full_ref.shape[1] // 3
    down = (((0,), (0,)), ((), ()))

    def product(a, b):
        return lax.dot_general(a, b, down, preferred_element_type=F32).astype(BF)

    gate_ref[0] = product(input_ref[...], full_ref[:, units : 2 * units])
    up_ref[0] = product(input_ref[...], full_ref[:, 2 * units :])
    down_ref[0] = product(full_ref[:, :units], grad_ref[...])


def contributions(blocks, gate_mat, up_mat):
    rows = len(blocks) // 2 * 2 * blocks[0].shape[0]
    columns = gate_mat.shape[0] // lax.axis_size("head")
    whole = blocks[0].shape[1]
    return pl.pallas_call(
        functools.partial(contrib_body, columns),
        out_shape=(
            jax.ShapeDtypeStruct((rows, columns), F32),
            jax.ShapeDtypeStruct((rows, columns), BF),
            jax.ShapeDtypeStruct((rows, whole), BF),
        ),
        in_specs=[SMEM] + [VMEM] * (2 + len(blocks)),
        out_specs=(VMEM,) * 3,
        compiler_params=pltpu.CompilerParams(vmem_limit_bytes=24 * 2**20),
        cost_estimate=pl.CostEstimate(
            flops=4 * rows * whole // 3 * gate_mat.shape[0],
            bytes_accessed=4 * rows * whole,
            transcendentals=0,
        ),
        name="expert_contrib",
    )(lax.axis_index("head").astype(jnp.int32).reshape(1), gate_mat, up_mat, *blocks)


def weight_grads(full, input_rows, grad_rows):
    units, width = full.shape[1] // 3, input_rows.shape[1]
    return pl.pallas_call(
        weights_body,
        out_shape=(
            jax.ShapeDtypeStruct((1, width, units), BF),
            jax.ShapeDtypeStruct((1, width, units), BF),
            jax.ShapeDtypeStruct((1, units, width), BF),
        ),
        in_specs=[VMEM] * 3,
        out_specs=(VMEM,) * 3,
        compiler_params=pltpu.CompilerParams(vmem_limit_bytes=24 * 2**20),
        cost_estimate=pl.CostEstimate(
            flops=6 * full.shape[0] * units * width,
            bytes_accessed=4 * full.size,
            transcendentals=0,
        ),
        name="expert_weight_grads",
    )(full, input_rows, grad_rows)


def finish(blocks, input_rows, grad_rows, gate_mat, up_mat, placed_low):
    exp_size = lax.axis_size("exp")
    ring = lax.axis_size("ctx") // X_HI
    at = lax.axis_index("ctx") % ring
    mine, other, full = contributions(blocks, gate_mat, up_mat)
    columns = mine.shape[1]
    mine = (mine + lax.ppermute(other, "head", [(0, 1), (1, 0)]).astype(F32)).astype(BF)
    mine = turn(mine.reshape(ring, -1, columns), (ring - at) % ring).reshape(exp_size, CAP, columns)
    back_rows = lax.all_to_all(mine, "exp", 0, 0, tiled=True)
    grad_input = jnp.dot(
        placed_low, back_rows.reshape(-1, columns), preferred_element_type=F32
    ).astype(BF)
    return (grad_input,) + tuple(weight_grads(after(full, mine), input_rows, grad_rows))


def shards(
    queries,
    key_rows,
    value_vector_rows,
    grad_attn,
    moe_input,
    moe_grad,
    expert_ids,
    router_weight,
    gate_weight,
    up_weight,
    down_weight,
):
    tokens, own = queries.shape[0], key_rows.shape[0]
    rows = tokens * queries.shape[1]
    size = queries.shape[2]
    pair = jnp.concatenate([key_rows[:, 0, :], value_vector_rows[:, 0, :]], axis=1)
    near = ctx_gather(pair, MASKS[:2])
    placed_low, got = select(moe_input, moe_grad, expert_ids, router_weight, near)
    near = ctx_gather(near, MASKS[2:])
    mine = jnp.concatenate([by_head(queries), by_head(grad_attn)], axis=0)
    theirs = beside(mine)
    queries = jnp.concatenate([mine[:rows], theirs[:rows]], axis=0)
    grads = jnp.concatenate([mine[rows:], theirs[rows:]], axis=0)
    above, below = ring_step(y_move, near, near)
    gate_mat, up_mat, parts = project(
        after(got, above, below, theirs), gate_weight, up_weight, down_weight
    )
    total = lax.all_to_all(parts, "ctx", 0, 0, tiled=True)
    above, below = both_after(above, below, parts)
    cut = near.shape[0] // 2
    far = stacked(y_move(above[:cut], 1), y_move(below[cut:], -1))
    flat = stacked(near, below, far, above)
    stats = attention_stats(own, tokens, queries, grads, flat)
    both, grad_query = attention_grads(
        own, tokens, queries, grads, flat, stats, beside(stats)
    )
    terms = [both[j * near.shape[0] : (j + 1) * near.shape[0]] for j in range(4)]
    up, down = sum_step(y_move, terms, 0, *sum_start(terms))
    sums = sum_step(y_move, terms, 1, up, down)
    block = act_block(jnp.sum(after(total, sums).astype(F32), axis=0))
    partner = opposite(block)
    first = lax.axis_index("ctx") // (lax.axis_size("ctx") // X_HI) == 0
    block = jnp.concatenate(
        [jnp.where(first, block, partner), jnp.where(first, partner, block)], axis=0
    )
    sums = ctx_sum(sums, MASKS[2:])
    block = after(block, sums)
    blocks = [block] + [None] * 8
    blocks[8], blocks[1] = ring_step(z_move, block, block)
    blocks[7], blocks[2] = ring_step(z_move, blocks[8], blocks[1])
    sums = ctx_sum(sums, MASKS[:2])
    blocks[6], blocks[3] = ring_step(z_move, blocks[7], blocks[2])
    onward, back = both_after(blocks[6], blocks[3], sums)
    blocks[4], blocks[5] = ring_last(z_move, onward, back)
    ring = lax.axis_size("ctx") // X_HI
    width = moe_input.shape[1]
    got = turn(got.reshape(ring, -1, 2 * width), lax.axis_index("ctx") % ring)
    got = got.reshape(-1, 2 * width)
    input_rows, grad_rows = got[:, :width], got[:, width:]
    of_experts = finish(blocks, input_rows, grad_rows, gate_mat, up_mat, placed_low)
    grad_query = grad_query[:rows] + beside(grad_query[rows:].astype(BF)).astype(F32)
    grad_query = jnp.swapaxes(grad_query.astype(BF).reshape(-1, tokens, size), 0, 1)
    return (grad_query,) + own_grads(sums) + of_experts


def solution(mesh):
    placed = (
        P("ctx", ("head", "exp"), None),
        P(("ctx", "exp"), "head", None),
        P(("ctx", "exp"), "head", None),
        P("ctx", ("head", "exp"), None),
        P("exp", "ctx"),
        P("exp", "ctx"),
        P("exp", None),
        P("exp", None),
        P("exp", "ctx", None),
        P("exp", "ctx", None),
        P("exp", None, "ctx"),
    )
    return jax.shard_map(
        shards,
        mesh=mesh,
        in_specs=placed,
        out_specs=(
            P("ctx", ("head", "exp"), None),
            P(("ctx", "exp"), "head", None),
            P(("ctx", "exp"), "head", None),
            P("exp", ("ctx", "head")),
            P("exp", "ctx", "head"),
            P("exp", "ctx", "head"),
            P("exp", "head", "ctx"),
        ),
        check_vma=False,
    )
```

```python
import functools

import jax
import jax.numpy as jnp
from jax import lax
from jax.experimental import pallas as pl
from jax.experimental.pallas import tpu as pltpu
from jax.sharding import PartitionSpec as P

CAP = 48
X_HI = 2
X_LO = 2
MASKED = -1e30
BF = jnp.bfloat16
F32 = jnp.float32


def activate(gate_val, up_val, back_val):
    sigmoid_gate = jax.nn.sigmoid(gate_val)
    hidden = (gate_val * sigmoid_gate * up_val).astype(BF)
    d_up = (back_val * gate_val * sigmoid_gate).astype(BF)
    d_gate = (back_val * up_val * sigmoid_gate * (1.0 + gate_val * (1.0 - sigmoid_gate))).astype(BF)
    return (hidden, d_gate, d_up)


def beside(block):
    return lax.ppermute(block, "exp", [(e, e ^ 1) for e in range(lax.axis_size("exp"))])


def z_move(block, step):
    n = lax.axis_size("ctx") // X_HI
    pairs = [(h * n + z, h * n + (z + step) % n) for h in range(X_HI) for z in range(n)]
    return lax.ppermute(block, "ctx", pairs)


def key_groups():
    exps = lax.axis_size("exp")
    pairs = lax.axis_size("ctx") * exps
    return [[i for i in range(pairs) if i % X_LO == x] for x in range(X_LO)]


def key_gather(block):
    copies = jnp.broadcast_to(block[None], (len(key_groups()[0]),) + block.shape)
    got = lax.all_to_all(
        copies, ("ctx", "exp"), 0, 0, tiled=True, axis_index_groups=key_groups()
    )
    return got.reshape(-1, block.shape[1])


def key_sum(both):
    parts = both.reshape(len(key_groups()[0]), -1, both.shape[1])
    got = lax.all_to_all(parts, ("ctx", "exp"), 0, 0, tiled=True, axis_index_groups=key_groups())
    return jnp.sum(got.astype(F32), axis=0)


def partner(block, mask):
    return lax.ppermute(block, "exp", [(e, e ^ mask) for e in range(lax.axis_size("exp"))])


def exchange(blocks, waits=None):
    shape = blocks.shape
    bits = shape[0].bit_length() - 1
    for bit in range(bits):
        if waits is not None and bit == bits - 1:
            blocks = after(blocks, waits)
        blocks = blocks.reshape((2**bit, 2, -1) + shape[1:])
        got = partner(blocks[:, 1], 2 ** (bits - 1 - bit))
        blocks = jnp.stack([blocks[:, 0], got], axis=1)
    return blocks.reshape(shape)


def opposite(block):
    n = lax.axis_size("ctx")
    return lax.ppermute(block, "ctx", [(c, (c + n // X_HI) % n) for c in range(n)])


def after(block, *others):
    return lax.optimization_barrier((block,) + others)[0]


def add_low(a, b):
    return (a.astype(F32) + b.astype(F32)).astype(BF)


def sum_start(parts):
    far = len(parts) // 2
    cut = parts[0].shape[1] // 2
    return parts[far][:, :cut], parts[far][:, cut:]


def sum_step(move, parts, step, onward, back):
    n = len(parts)
    far = n // 2
    cut = parts[0].shape[1] // 2
    onward, back = move(onward, 1), move(back, -1)
    ahead, behind = parts[far - 1 - step], parts[(far + 1 + step) % n]
    if step == 0:
        onward = jnp.concatenate([add_low(onward, ahead[:, :cut]), ahead[:, cut:]], axis=1)
        back = jnp.concatenate([behind[:, :cut], add_low(back, behind[:, cut:])], axis=1)
    elif step < far - 1:
        onward, back = add_low(onward, ahead), add_low(back, behind)
    else:
        return onward.astype(F32) + back.astype(F32) + parts[0].astype(F32)
    return onward, back


def ring_step(move, onward, back):
    return move(onward, 1), move(back, -1)


def ring_last(move, onward, back):
    cut = onward.shape[1] // 2
    return move(onward[:, :cut], 1), move(back[:, cut:], -1)


def both_after(onward, back, *others):
    return lax.optimization_barrier((onward, back) + others)[:2]


def turn(blocks, places):
    twice = jnp.concatenate([blocks, blocks], axis=0)
    return lax.dynamic_slice_in_dim(twice, places, blocks.shape[0], 0)


def scores_of(step, own, rows, tokens, here_ref, k, q):
    lanes = q.shape[0]
    found = lax.dot_general(k, q, (((1,), (1,)), ((), ())), preferred_element_type=F32)
    ahead = lax.broadcasted_iota(jnp.int32, (own, lanes), 1) % tokens - lax.broadcasted_iota(
        jnp.int32, (own, lanes), 0
    )
    me, side = here_ref[0], here_ref[1]
    parts = k.shape[0] // own
    masked = []
    for part in range(parts):
        place = step * parts + part
        start = place // rows * tokens + (place % rows * X_LO + side) * own
        masked.append(
            jnp.where(
                ahead >= start - me * tokens,
                found[part * own : (part + 1) * own] * k.shape[1] ** (-0.5),
                MASKED,
            )
        )
    return jnp.concatenate(masked, axis=0)


def stats_body(own, rows, tokens, here_ref, q_ref, g_ref, kv_ref, stats_ref):
    size = kv_ref.shape[1] // 2
    lanes = q_ref.shape[0]
    chunk = 8 * own

    def one(step, held):
        top, norm, delta = held
        at = pl.ds(pl.multiple_of(step * chunk, chunk), chunk)
        scores = scores_of(step, own, rows, tokens, here_ref, kv_ref[at, :size], q_ref[...])
        dprob = lax.dot_general(
            kv_ref[at, size:], g_ref[...], (((1,), (1,)), ((), ())), preferred_element_type=F32
        )
        scores, dprob = scores.reshape(-1, 8, lanes), dprob.reshape(-1, 8, lanes)
        higher = jnp.maximum(top, jnp.max(scores, axis=0))
        shrink = jnp.exp(top - higher)
        prob = jnp.exp(scores - higher[None])
        norm = norm * shrink + jnp.sum(prob, axis=0)
        delta = delta * shrink + jnp.sum(prob * dprob, axis=0)
        return higher, norm, delta

    zero = jnp.zeros((8, lanes), F32)
    top, norm, delta = lax.fori_loop(0, kv_ref.shape[0] // chunk, one, (zero + MASKED, zero, zero))
    highest = jnp.max(top, axis=0, keepdims=True)
    shrink = jnp.exp(top - highest)
    stats_ref[0:1, :] = highest
    stats_ref[1:2, :] = jnp.sum(norm * shrink, axis=0, keepdims=True)
    stats_ref[2:3, :] = jnp.sum(delta * shrink, axis=0, keepdims=True)
    stats_ref[3:, :] = jnp.zeros((5, lanes), F32)


def grads_body(
    own, rows, tokens, here_ref, q_ref, g_ref, kv_ref, stats_ref, far_ref, both_ref, dq_ref
):
    size = kv_ref.shape[1] // 2
    lanes = q_ref.shape[0]
    chunk = 8 * own
    far = jnp.concatenate([far_ref[:, lanes // 2 :], far_ref[:, : lanes // 2]], axis=1)
    near = stats_ref[...]
    top = jnp.maximum(near[0:1], far[0:1])
    shrink_near, shrink_far = jnp.exp(near[0:1] - top), jnp.exp(far[0:1] - top)
    inverse = 1.0 / (near[1:2] * shrink_near + far[1:2] * shrink_far)
    delta = (near[2:3] * shrink_near + far[2:3] * shrink_far) * inverse

    def one(step, total):
        at = pl.ds(pl.multiple_of(step * chunk, chunk), chunk)
        k = kv_ref[at, :size]
        scores = scores_of(step, own, rows, tokens, here_ref, k, q_ref[...])
        prob = jnp.exp(scores - top) * inverse
        both_ref[at, size:] = jnp.dot(
            prob.astype(BF), g_ref[...], preferred_element_type=F32
        ).astype(BF)
        dprob = lax.dot_general(
            kv_ref[at, size:], g_ref[...], (((1,), (1,)), ((), ())), preferred_element_type=F32
        )
        dscore = (prob * (dprob - delta)).astype(BF)
        both_ref[at, :size] = jnp.dot(dscore, q_ref[...], preferred_element_type=F32).astype(BF)
        return total + lax.dot_general(
            k, dscore, (((0,), (0,)), ((), ())), preferred_element_type=F32
        )

    total = lax.fori_loop(0, kv_ref.shape[0] // chunk, one, jnp.zeros((size, lanes), F32))
    dq_ref[...] = (total * size ** (-0.5)).T


VMEM = pl.BlockSpec(memory_space=pltpu.VMEM)
SMEM = pl.BlockSpec(memory_space=pltpu.SMEM)


def here():
    return jnp.stack([lax.axis_index("ctx"), lax.axis_index("exp") % X_LO]).astype(jnp.int32)


def attention_stats(own, tokens, queries, grads, flat):
    keys, lanes = flat.shape[0], queries.shape[0]
    return pl.pallas_call(
        functools.partial(stats_body, own, lax.axis_size("exp") // X_LO, tokens),
        out_shape=jax.ShapeDtypeStruct((8, lanes), F32),
        in_specs=[SMEM, VMEM, VMEM, VMEM],
        out_specs=VMEM,
        compiler_params=pltpu.CompilerParams(vmem_limit_bytes=24 * 2**20),
        cost_estimate=pl.CostEstimate(
            flops=4 * keys * lanes * flat.shape[1] // 2,
            bytes_accessed=2 * flat.size,
            transcendentals=keys * lanes,
        ),
        name="attention_stats",
    )(here(), queries, grads, flat)


def attention_grads(own, tokens, queries, grads, flat, stats, far):
    keys, lanes = flat.shape[0], queries.shape[0]
    size = flat.shape[1] // 2
    return pl.pallas_call(
        functools.partial(grads_body, own, lax.axis_size("exp") // X_LO, tokens),
        out_shape=(
            jax.ShapeDtypeStruct((keys, 2 * size), BF),
            jax.ShapeDtypeStruct((lanes, size), F32),
        ),
        in_specs=[SMEM] + [VMEM] * 5,
        out_specs=(VMEM, VMEM),
        compiler_params=pltpu.CompilerParams(vmem_limit_bytes=24 * 2**20),
        cost_estimate=pl.CostEstimate(
            flops=10 * keys * lanes * size,
            bytes_accessed=4 * flat.size,
            transcendentals=keys * lanes,
        ),
        name="attention_grads",
    )(here(), queries, grads, flat, stats, far)


def by_head(rows):
    return jnp.swapaxes(rows, 0, 1).reshape(-1, rows.shape[2])


def own_grads(both):
    head_dim = both.shape[1] // 2
    grad_key = (both[:, :head_dim] * head_dim ** (-0.5)).astype(BF)[:, None, :]
    grad_value = both[:, head_dim:].astype(BF)[:, None, :]
    return grad_key, grad_value


def select(moe_input, moe_grad, expert_ids, router_weight, flat):
    width = moe_input.shape[1]
    exp_size = lax.axis_size("exp")
    labels = lax.axis_index("exp") ^ jnp.arange(exp_size)
    matches = expert_ids[:, :, None] == labels[None, None, :]
    member = jnp.sum(matches.astype(jnp.int32), axis=1)
    weight_row = jnp.sum(jnp.where(matches, router_weight[:, :, None], 0.0), axis=1)
    slot_rank = jnp.cumsum(member, axis=0) - member
    placed = (member[:, :, None] == 1) & (
        slot_rank[:, :, None] == jnp.arange(CAP)[None, None, :]
    )
    slot_weight = jnp.sum(jnp.where(placed, weight_row[:, :, None], 0.0), axis=0)
    placed_low = placed.astype(BF).reshape(-1, exp_size * CAP)
    rows = jnp.concatenate([moe_input, moe_grad], axis=1)
    picked = jnp.einsum("bs,bd->sd", placed_low, rows, preferred_element_type=F32)
    scaled = picked[:, width:] * slot_weight.reshape(-1, 1)
    sent = jnp.concatenate([picked[:, :width].astype(BF), scaled.astype(BF)], axis=1)
    got = exchange(sent.reshape(exp_size, CAP, 2 * width), flat)
    return placed_low, got


def project(got, gate_weight, up_weight, down_weight):
    ring = lax.axis_size("ctx") // X_HI
    at = lax.axis_index("ctx") % ring
    half = lax.axis_index("head")
    units = gate_weight.shape[2] // lax.axis_size("head")
    width = got.shape[2] // 2
    got = turn(got.reshape(ring, -1, 2 * width), at).reshape(-1, 2 * width)
    input_rows, grad_rows = got[:, :width], got[:, width:]
    gate_mat = lax.dynamic_slice_in_dim(gate_weight[0], half * units, units, 1)
    up_mat = lax.dynamic_slice_in_dim(up_weight[0], half * units, units, 1)
    down_mat = lax.dynamic_slice_in_dim(down_weight[0], half * units, units, 0)
    gate_part = jnp.dot(input_rows, gate_mat, preferred_element_type=F32).astype(BF)
    up_part = jnp.dot(input_rows, up_mat, preferred_element_type=F32).astype(BF)
    back_part = jnp.einsum("rd,fd->rf", grad_rows, down_mat, preferred_element_type=F32).astype(BF)
    parts = jnp.concatenate([gate_part, up_part, back_part], axis=1).reshape(ring, -1, 3 * units)
    return input_rows, grad_rows, gate_mat, up_mat, [parts[j] for j in range(ring)]


def act_block(total):
    units = total.shape[1] // 3
    hidden, d_gate, d_up = activate(
        total[:, :units], total[:, units : 2 * units], total[:, 2 * units :]
    )
    return jnp.concatenate([hidden, d_gate, d_up], axis=1)


def contrib_body(width, half_ref, gate_ref, up_ref, *refs):
    blocks, (mine_ref, other_ref, full_ref) = refs[:-3], refs[-3:]
    height = blocks[0].shape[0]
    units = full_ref.shape[1] // 3
    row = 0
    halves = [block for block in blocks if block.shape[1] < full_ref.shape[1]]
    for block in blocks:
        if block is halves[0]:
            cut = block.shape[1]
            full_ref[row : row + height, :cut] = block[...]
            continue
        if block is halves[1]:
            full_ref[row : row + height, cut:] = block[...]
        else:
            full_ref[row : row + height, :] = block[...]
        row += height
    across = (((1,), (1,)), ((), ()))
    found = lax.dot_general(
        full_ref[:, units : 2 * units], gate_ref[...], across, preferred_element_type=F32
    ) + lax.dot_general(full_ref[:, 2 * units :], up_ref[...], across, preferred_element_type=F32)
    first = half_ref[0] == 0
    mine_ref[...] = jnp.where(first, found[:, :width], found[:, width:])
    other_ref[...] = jnp.where(first, found[:, width:], found[:, :width]).astype(BF)


def weights_body(full_ref, input_ref, grad_ref, gate_ref, up_ref, down_ref):
    units = full_ref.shape[1] // 3
    down = (((0,), (0,)), ((), ()))

    def product(a, b):
        return lax.dot_general(a, b, down, preferred_element_type=F32).astype(BF)

    gate_ref[0] = product(input_ref[...], full_ref[:, units : 2 * units])
    up_ref[0] = product(input_ref[...], full_ref[:, 2 * units :])
    down_ref[0] = product(full_ref[:, :units], grad_ref[...])


def contributions(blocks, gate_mat, up_mat):
    rows = len(blocks) // 2 * 2 * blocks[0].shape[0]
    columns = gate_mat.shape[0] // lax.axis_size("head")
    whole = blocks[0].shape[1]
    return pl.pallas_call(
        functools.partial(contrib_body, columns),
        out_shape=(
            jax.ShapeDtypeStruct((rows, columns), F32),
            jax.ShapeDtypeStruct((rows, columns), BF),
            jax.ShapeDtypeStruct((rows, whole), BF),
        ),
        in_specs=[SMEM] + [VMEM] * (2 + len(blocks)),
        out_specs=(VMEM,) * 3,
        compiler_params=pltpu.CompilerParams(vmem_limit_bytes=24 * 2**20),
        cost_estimate=pl.CostEstimate(
            flops=4 * rows * whole // 3 * gate_mat.shape[0],
            bytes_accessed=4 * rows * whole,
            transcendentals=0,
        ),
        name="expert_contrib",
    )(lax.axis_index("head").astype(jnp.int32).reshape(1), gate_mat, up_mat, *blocks)


def weight_grads(full, input_rows, grad_rows):
    units, width = full.shape[1] // 3, input_rows.shape[1]
    return pl.pallas_call(
        weights_body,
        out_shape=(
            jax.ShapeDtypeStruct((1, width, units), BF),
            jax.ShapeDtypeStruct((1, width, units), BF),
            jax.ShapeDtypeStruct((1, units, width), BF),
        ),
        in_specs=[VMEM] * 3,
        out_specs=(VMEM,) * 3,
        compiler_params=pltpu.CompilerParams(vmem_limit_bytes=24 * 2**20),
        cost_estimate=pl.CostEstimate(
            flops=6 * full.shape[0] * units * width,
            bytes_accessed=4 * full.size,
            transcendentals=0,
        ),
        name="expert_weight_grads",
    )(full, input_rows, grad_rows)


def finish(blocks, input_rows, grad_rows, gate_mat, up_mat, placed_low):
    exp_size = lax.axis_size("exp")
    ring = lax.axis_size("ctx") // X_HI
    at = lax.axis_index("ctx") % ring
    mine, other, full = contributions(blocks, gate_mat, up_mat)
    columns = mine.shape[1]
    mine = (mine + lax.ppermute(other, "head", [(0, 1), (1, 0)]).astype(F32)).astype(BF)
    mine = turn(mine.reshape(ring, -1, columns), (ring - at) % ring).reshape(exp_size, CAP, columns)
    back_rows = exchange(mine)
    grad_input = jnp.dot(
        placed_low, back_rows.reshape(-1, columns), preferred_element_type=F32
    ).astype(BF)
    return (grad_input,) + tuple(weight_grads(after(full, mine), input_rows, grad_rows))


def shards(
    queries,
    key_rows,
    value_vector_rows,
    grad_attn,
    moe_input,
    moe_grad,
    expert_ids,
    router_weight,
    gate_weight,
    up_weight,
    down_weight,
):
    tokens, own = queries.shape[0], key_rows.shape[0]
    rows = tokens * queries.shape[1]
    size = queries.shape[2]
    pair = jnp.concatenate([key_rows[:, 0, :], value_vector_rows[:, 0, :]], axis=1)
    flat = key_gather(pair)
    placed_low, got = select(moe_input, moe_grad, expert_ids, router_weight, flat)
    mine = jnp.concatenate([by_head(queries), by_head(grad_attn)], axis=0)
    theirs = beside(mine)
    queries = jnp.concatenate([mine[:rows], theirs[:rows]], axis=0)
    grads = jnp.concatenate([mine[rows:], theirs[rows:]], axis=0)
    input_rows, grad_rows, gate_mat, up_mat, parts = project(
        got, gate_weight, up_weight, down_weight
    )
    onward, back = both_after(*sum_start(parts), theirs)
    stats = attention_stats(own, tokens, queries, grads, after(flat, onward, back))
    onward, back = sum_step(z_move, parts, 0, onward, back)
    onward, back = both_after(onward, back, stats)
    far_stats = beside(stats)
    onward, back = sum_step(z_move, parts, 1, onward, back)
    onward, back = both_after(onward, back, far_stats)
    both, grad_query = attention_grads(
        own, tokens, queries, grads, after(flat, onward, back), stats, far_stats
    )
    onward, back = sum_step(z_move, parts, 2, onward, back)
    onward, back = both_after(onward, back, both)
    total = sum_step(z_move, parts, 3, onward, back)
    sums = key_sum(both)
    other = opposite(total.astype(BF))
    block = act_block(total + other.astype(F32))
    blocks = [block] + [None] * 8
    blocks[8], blocks[1] = ring_step(z_move, block, block)
    blocks[7], blocks[2] = ring_step(z_move, blocks[8], blocks[1])
    blocks[6], blocks[3] = ring_step(z_move, blocks[7], blocks[2])
    onward, back = both_after(blocks[6], blocks[3], sums)
    blocks[4], blocks[5] = ring_last(z_move, onward, back)
    of_experts = finish(blocks, input_rows, grad_rows, gate_mat, up_mat, placed_low)
    grad_query = grad_query[:rows] + beside(grad_query[rows:].astype(BF)).astype(F32)
    grad_query = jnp.swapaxes(grad_query.astype(BF).reshape(-1, tokens, size), 0, 1)
    return (grad_query,) + own_grads(sums) + of_experts


def solution(mesh):
    placed = (
        P("ctx", ("head", "exp"), None),
        P(("ctx", "exp"), "head", None),
        P(("ctx", "exp"), "head", None),
        P("ctx", ("head", "exp"), None),
        P("exp", "ctx"),
        P("exp", "ctx"),
        P("exp", None),
        P("exp", None),
        P("exp", "ctx", None),
        P("exp", "ctx", None),
        P("exp", None, "ctx"),
    )
    return jax.shard_map(
        shards,
        mesh=mesh,
        in_specs=placed,
        out_specs=(
            P("ctx", ("head", "exp"), None),
            P(("ctx", "exp"), "head", None),
            P(("ctx", "exp"), "head", None),
            P("exp", ("ctx", "head")),
            P("exp", "ctx", "head"),
            P("exp", "ctx", "head"),
            P("exp", "head", "ctx"),
        ),
        check_vma=False,
    )
```

```python
import functools

import jax
import jax.numpy as jnp
from jax import lax
from jax.experimental import pallas as pl
from jax.experimental.pallas import tpu as pltpu
from jax.sharding import PartitionSpec as P

CAP = 48
X_HI = 2
X_LO = 2
MASKED = -1e30
MASKS = (4, 2, 8, 1)
BF = jnp.bfloat16
F32 = jnp.float32


def activate(gate_val, up_val, back_val):
    sigmoid_gate = jax.nn.sigmoid(gate_val)
    hidden = (gate_val * sigmoid_gate * up_val).astype(BF)
    d_up = (back_val * gate_val * sigmoid_gate).astype(BF)
    d_gate = (back_val * up_val * sigmoid_gate * (1.0 + gate_val * (1.0 - sigmoid_gate))).astype(BF)
    return (hidden, d_gate, d_up)


def beside(block):
    return lax.ppermute(block, "exp", [(e, e ^ 1) for e in range(lax.axis_size("exp"))])


def z_move(block, step):
    n = lax.axis_size("ctx") // X_HI
    pairs = [(h * n + z, h * n + (z + step) % n) for h in range(X_HI) for z in range(n)]
    return lax.ppermute(block, "ctx", pairs)


def key_groups():
    exps = lax.axis_size("exp")
    pairs = lax.axis_size("ctx") * exps
    return [[i for i in range(pairs) if i % X_LO == x] for x in range(X_LO)]


def key_gather(block):
    copies = jnp.broadcast_to(block[None], (len(key_groups()[0]),) + block.shape)
    got = lax.all_to_all(
        copies, ("ctx", "exp"), 0, 0, tiled=True, axis_index_groups=key_groups()
    )
    return got.reshape(-1, block.shape[1])


def y_parts(both):
    n = lax.axis_size("exp")
    groups = [list(range(x, n, X_LO)) for x in range(X_LO)]
    parts = both.reshape(n // X_LO, -1, both.shape[1])
    return lax.all_to_all(parts, "exp", 0, 0, tiled=True, axis_index_groups=groups)


def ctx_sum(both, masks):
    for mask in reversed(masks):
        half = both.shape[0] // 2
        sent = both[half:].astype(BF if half >= both.shape[1] // 2 else F32)
        pairs = [(c, c ^ mask) for c in range(lax.axis_size("ctx"))]
        both = both[:half] + lax.ppermute(sent, "ctx", pairs).astype(F32)
    return both


def place_of(apart):
    return sum(apart // mask % 2 * 2**bit for bit, mask in enumerate(MASKS))


def partner(block, mask):
    return lax.ppermute(block, "exp", [(e, e ^ mask) for e in range(lax.axis_size("exp"))])


def exchange(blocks):
    shape = blocks.shape
    bits = shape[0].bit_length() - 1
    for bit in range(bits):
        blocks = blocks.reshape((2**bit, 2, -1) + shape[1:])
        got = partner(blocks[:, 1], 2 ** (bits - 1 - bit))
        blocks = jnp.stack([blocks[:, 0], got], axis=1)
    return blocks.reshape(shape)


def opposite(block):
    n = lax.axis_size("ctx")
    return lax.ppermute(block, "ctx", [(c, (c + n // X_HI) % n) for c in range(n)])


def after(block, *others):
    return lax.optimization_barrier((block,) + others)[0]


def add_low(a, b):
    return (a.astype(F32) + b.astype(F32)).astype(BF)


def sum_start(parts):
    far = len(parts) // 2
    cut = parts[0].shape[1] // 2
    return parts[far][:, :cut], parts[far][:, cut:]


def sum_step(move, parts, step, onward, back):
    n = len(parts)
    far = n // 2
    cut = parts[0].shape[1] // 2
    onward, back = move(onward, 1), move(back, -1)
    ahead, behind = parts[far - 1 - step], parts[(far + 1 + step) % n]
    if step == 0:
        onward = jnp.concatenate([add_low(onward, ahead[:, :cut]), ahead[:, cut:]], axis=1)
        back = jnp.concatenate([behind[:, :cut], add_low(back, behind[:, cut:])], axis=1)
    elif step < far - 1:
        onward, back = add_low(onward, ahead), add_low(back, behind)
    else:
        return onward.astype(F32) + back.astype(F32) + parts[0].astype(F32)
    return onward, back


def ring_step(move, onward, back):
    return move(onward, 1), move(back, -1)


def ring_last(move, onward, back):
    cut = onward.shape[1] // 2
    return move(onward[:, :cut], 1), move(back[:, cut:], -1)


def both_after(onward, back, *others):
    return lax.optimization_barrier((onward, back) + others)[:2]


def turn(blocks, places):
    twice = jnp.concatenate([blocks, blocks], axis=0)
    return lax.dynamic_slice_in_dim(twice, places, blocks.shape[0], 0)


def scores_of(step, own, rows, tokens, here_ref, k, q):
    lanes = q.shape[0]
    found = lax.dot_general(k, q, (((1,), (1,)), ((), ())), preferred_element_type=F32)
    ahead = lax.broadcasted_iota(jnp.int32, (own, lanes), 1) % tokens - lax.broadcasted_iota(
        jnp.int32, (own, lanes), 0
    )
    me, side = here_ref[0], here_ref[1]
    parts = k.shape[0] // own
    masked = []
    for part in range(parts):
        place = step * parts + part
        start = (here_ref[2] + place // rows) * tokens + (place % rows * X_LO + side) * own
        masked.append(
            jnp.where(
                ahead >= start - me * tokens,
                found[part * own : (part + 1) * own] * k.shape[1] ** (-0.5),
                MASKED,
            )
        )
    return jnp.concatenate(masked, axis=0)


def stats_body(own, rows, tokens, here_ref, q_ref, g_ref, kv_ref, stats_ref):
    size = kv_ref.shape[1] // 2
    lanes = q_ref.shape[0]
    chunk = 8 * own

    def one(step, held):
        top, norm, delta = held
        at = pl.ds(pl.multiple_of(step * chunk, chunk), chunk)
        scores = scores_of(step, own, rows, tokens, here_ref, kv_ref[at, :size], q_ref[...])
        dprob = lax.dot_general(
            kv_ref[at, size:], g_ref[...], (((1,), (1,)), ((), ())), preferred_element_type=F32
        )
        scores, dprob = scores.reshape(-1, 8, lanes), dprob.reshape(-1, 8, lanes)
        higher = jnp.maximum(top, jnp.max(scores, axis=0))
        shrink = jnp.exp(top - higher)
        prob = jnp.exp(scores - higher[None])
        norm = norm * shrink + jnp.sum(prob, axis=0)
        delta = delta * shrink + jnp.sum(prob * dprob, axis=0)
        return higher, norm, delta

    zero = jnp.zeros((8, lanes), F32)
    top, norm, delta = lax.fori_loop(0, kv_ref.shape[0] // chunk, one, (zero + MASKED, zero, zero))
    highest = jnp.max(top, axis=0, keepdims=True)
    shrink = jnp.exp(top - highest)
    stats_ref[0:1, :] = highest
    stats_ref[1:2, :] = jnp.sum(norm * shrink, axis=0, keepdims=True)
    stats_ref[2:3, :] = jnp.sum(delta * shrink, axis=0, keepdims=True)
    stats_ref[3:, :] = jnp.zeros((5, lanes), F32)


def grads_body(
    own, rows, tokens, here_ref, q_ref, g_ref, kv_ref, stats_ref, far_ref, *refs
):
    before, (both_ref, dq_ref) = refs[:-2], refs[-2:]
    both_ref[...] = before[0][...] if before else jnp.zeros_like(both_ref)
    size = kv_ref.shape[1] // 2
    lanes = q_ref.shape[0]
    chunk = 8 * own
    far = jnp.concatenate([far_ref[:, lanes // 2 :], far_ref[:, : lanes // 2]], axis=1)
    near = stats_ref[...]
    top = jnp.maximum(near[0:1], far[0:1])
    shrink_near, shrink_far = jnp.exp(near[0:1] - top), jnp.exp(far[0:1] - top)
    inverse = 1.0 / (near[1:2] * shrink_near + far[1:2] * shrink_far)
    delta = (near[2:3] * shrink_near + far[2:3] * shrink_far) * inverse

    def one(step, total):
        at = pl.ds(pl.multiple_of(step * chunk, chunk), chunk)
        k = kv_ref[at, :size]
        scores = scores_of(step, own, rows, tokens, here_ref, k, q_ref[...])
        prob = jnp.exp(scores - top) * inverse
        value = jnp.dot(prob.astype(BF), g_ref[...], preferred_element_type=F32).astype(BF)
        dprob = lax.dot_general(
            kv_ref[at, size:], g_ref[...], (((1,), (1,)), ((), ())), preferred_element_type=F32
        )
        dscore = (prob * (dprob - delta)).astype(BF)
        key = jnp.dot(dscore, q_ref[...], preferred_element_type=F32).astype(BF)
        for part in range(8):
            place = step * 8 + part
            i = place_of((here_ref[2] + place // rows) ^ here_ref[0])
            piece = slice(part * own, (part + 1) * own)
            both_ref[place % rows, i, :, :size] = key[piece]
            both_ref[place % rows, i, :, size:] = value[piece]
        return total + lax.dot_general(
            k, dscore, (((0,), (0,)), ((), ())), preferred_element_type=F32
        )

    total = lax.fori_loop(0, kv_ref.shape[0] // chunk, one, jnp.zeros((size, lanes), F32))
    total = (total * size ** (-0.5)).T
    dq_ref[...] = total + before[1][...] if before else total


VMEM = pl.BlockSpec(memory_space=pltpu.VMEM)
SMEM = pl.BlockSpec(memory_space=pltpu.SMEM)


def here(first):
    side = lax.axis_index("exp") % X_LO
    return jnp.stack([lax.axis_index("ctx"), side, jnp.int32(first)]).astype(jnp.int32)


def attention_stats(own, tokens, queries, grads, flat):
    keys, lanes = flat.shape[0], queries.shape[0]
    return pl.pallas_call(
        functools.partial(stats_body, own, lax.axis_size("exp") // X_LO, tokens),
        out_shape=jax.ShapeDtypeStruct((8, lanes), F32),
        in_specs=[SMEM, VMEM, VMEM, VMEM],
        out_specs=VMEM,
        compiler_params=pltpu.CompilerParams(vmem_limit_bytes=24 * 2**20),
        cost_estimate=pl.CostEstimate(
            flops=4 * keys * lanes * flat.shape[1] // 2,
            bytes_accessed=2 * flat.size,
            transcendentals=keys * lanes,
        ),
        name="attention_stats",
    )(here(0), queries, grads, flat)


def attention_grads(own, tokens, first, queries, grads, flat, stats, far, before=()):
    keys, lanes = flat.shape[0], queries.shape[0]
    size = flat.shape[1] // 2
    rows = lax.axis_size("exp") // X_LO
    return pl.pallas_call(
        functools.partial(grads_body, own, rows, tokens),
        out_shape=(
            jax.ShapeDtypeStruct((rows, lax.axis_size("ctx"), own, 2 * size), BF),
            jax.ShapeDtypeStruct((lanes, size), F32),
        ),
        in_specs=[SMEM] + [VMEM] * (5 + len(before)),
        out_specs=(VMEM, VMEM),
        compiler_params=pltpu.CompilerParams(vmem_limit_bytes=24 * 2**20),
        cost_estimate=pl.CostEstimate(
            flops=10 * keys * lanes * size,
            bytes_accessed=4 * flat.size,
            transcendentals=keys * lanes,
        ),
        name="attention_grads",
    )(here(first), queries, grads, flat, stats, far, *before)


def by_head(rows):
    return jnp.swapaxes(rows, 0, 1).reshape(-1, rows.shape[2])


def own_grads(both):
    head_dim = both.shape[1] // 2
    grad_key = (both[:, :head_dim] * head_dim ** (-0.5)).astype(BF)[:, None, :]
    grad_value = both[:, head_dim:].astype(BF)[:, None, :]
    return grad_key, grad_value


def select(moe_input, moe_grad, expert_ids, router_weight):
    width = moe_input.shape[1]
    exp_size = lax.axis_size("exp")
    labels = lax.axis_index("exp") ^ jnp.arange(exp_size)
    matches = expert_ids[:, :, None] == labels[None, None, :]
    member = jnp.sum(matches.astype(jnp.int32), axis=1)
    weight_row = jnp.sum(jnp.where(matches, router_weight[:, :, None], 0.0), axis=1)
    slot_rank = jnp.cumsum(member, axis=0) - member
    placed = (member[:, :, None] == 1) & (
        slot_rank[:, :, None] == jnp.arange(CAP)[None, None, :]
    )
    slot_weight = jnp.sum(jnp.where(placed, weight_row[:, :, None], 0.0), axis=0)
    placed_low = placed.astype(BF).reshape(-1, exp_size * CAP)
    rows = jnp.concatenate([moe_input, moe_grad], axis=1)
    picked = jnp.einsum("bs,bd->sd", placed_low, rows, preferred_element_type=F32)
    scaled = picked[:, width:] * slot_weight.reshape(-1, 1)
    sent = jnp.concatenate([picked[:, :width].astype(BF), scaled.astype(BF)], axis=1)
    got = exchange(sent.reshape(exp_size, CAP, 2 * width))
    return placed_low, got


def project(got, gate_weight, up_weight, down_weight):
    ring = lax.axis_size("ctx") // X_HI
    at = lax.axis_index("ctx") % ring
    half = lax.axis_index("head")
    units = gate_weight.shape[2] // lax.axis_size("head")
    width = got.shape[2] // 2
    got = turn(got.reshape(ring, -1, 2 * width), at).reshape(-1, 2 * width)
    input_rows, grad_rows = got[:, :width], got[:, width:]
    gate_mat = lax.dynamic_slice_in_dim(gate_weight[0], half * units, units, 1)
    up_mat = lax.dynamic_slice_in_dim(up_weight[0], half * units, units, 1)
    down_mat = lax.dynamic_slice_in_dim(down_weight[0], half * units, units, 0)
    gate_part = jnp.dot(input_rows, gate_mat, preferred_element_type=F32).astype(BF)
    up_part = jnp.dot(input_rows, up_mat, preferred_element_type=F32).astype(BF)
    back_part = jnp.einsum("rd,fd->rf", grad_rows, down_mat, preferred_element_type=F32).astype(BF)
    parts = jnp.concatenate([gate_part, up_part, back_part], axis=1).reshape(ring, -1, 3 * units)
    return input_rows, grad_rows, gate_mat, up_mat, [parts[j] for j in range(ring)]


def act_block(total):
    units = total.shape[1] // 3
    hidden, d_gate, d_up = activate(
        total[:, :units], total[:, units : 2 * units], total[:, 2 * units :]
    )
    return jnp.concatenate([hidden, d_gate, d_up], axis=1)


def contrib_body(width, half_ref, gate_ref, up_ref, *refs):
    blocks, (mine_ref, other_ref, full_ref) = refs[:-3], refs[-3:]
    height = blocks[0].shape[0]
    units = full_ref.shape[1] // 3
    row = 0
    halves = [block for block in blocks if block.shape[1] < full_ref.shape[1]]
    for block in blocks:
        if block is halves[0]:
            cut = block.shape[1]
            full_ref[row : row + height, :cut] = block[...]
            continue
        if block is halves[1]:
            full_ref[row : row + height, cut:] = block[...]
        else:
            full_ref[row : row + height, :] = block[...]
        row += height
    across = (((1,), (1,)), ((), ()))
    found = lax.dot_general(
        full_ref[:, units : 2 * units], gate_ref[...], across, preferred_element_type=F32
    ) + lax.dot_general(full_ref[:, 2 * units :], up_ref[...], across, preferred_element_type=F32)
    first = half_ref[0] == 0
    mine_ref[...] = jnp.where(first, found[:, :width], found[:, width:])
    other_ref[...] = jnp.where(first, found[:, width:], found[:, :width]).astype(BF)


def weights_body(full_ref, input_ref, grad_ref, gate_ref, up_ref, down_ref):
    units = full_ref.shape[1] // 3
    down = (((0,), (0,)), ((), ()))

    def product(a, b):
        return lax.dot_general(a, b, down, preferred_element_type=F32).astype(BF)

    gate_ref[0] = product(input_ref[...], full_ref[:, units : 2 * units])
    up_ref[0] = product(input_ref[...], full_ref[:, 2 * units :])
    down_ref[0] = product(full_ref[:, :units], grad_ref[...])


def contributions(blocks, gate_mat, up_mat):
    rows = len(blocks) // 2 * 2 * blocks[0].shape[0]
    columns = gate_mat.shape[0] // lax.axis_size("head")
    whole = blocks[0].shape[1]
    return pl.pallas_call(
        functools.partial(contrib_body, columns),
        out_shape=(
            jax.ShapeDtypeStruct((rows, columns), F32),
            jax.ShapeDtypeStruct((rows, columns), BF),
            jax.ShapeDtypeStruct((rows, whole), BF),
        ),
        in_specs=[SMEM] + [VMEM] * (2 + len(blocks)),
        out_specs=(VMEM,) * 3,
        compiler_params=pltpu.CompilerParams(vmem_limit_bytes=24 * 2**20),
        cost_estimate=pl.CostEstimate(
            flops=4 * rows * whole // 3 * gate_mat.shape[0],
            bytes_accessed=4 * rows * whole,
            transcendentals=0,
        ),
        name="expert_contrib",
    )(lax.axis_index("head").astype(jnp.int32).reshape(1), gate_mat, up_mat, *blocks)


def weight_grads(full, input_rows, grad_rows):
    units, width = full.shape[1] // 3, input_rows.shape[1]
    return pl.pallas_call(
        weights_body,
        out_shape=(
            jax.ShapeDtypeStruct((1, width, units), BF),
            jax.ShapeDtypeStruct((1, width, units), BF),
            jax.ShapeDtypeStruct((1, units, width), BF),
        ),
        in_specs=[VMEM] * 3,
        out_specs=(VMEM,) * 3,
        compiler_params=pltpu.CompilerParams(vmem_limit_bytes=24 * 2**20),
        cost_estimate=pl.CostEstimate(
            flops=6 * full.shape[0] * units * width,
            bytes_accessed=4 * full.size,
            transcendentals=0,
        ),
        name="expert_weight_grads",
    )(full, input_rows, grad_rows)


def finish(blocks, input_rows, grad_rows, gate_mat, up_mat, placed_low):
    exp_size = lax.axis_size("exp")
    ring = lax.axis_size("ctx") // X_HI
    at = lax.axis_index("ctx") % ring
    mine, other, full = contributions(blocks, gate_mat, up_mat)
    columns = mine.shape[1]
    mine = (mine + lax.ppermute(other, "head", [(0, 1), (1, 0)]).astype(F32)).astype(BF)
    mine = turn(mine.reshape(ring, -1, columns), (ring - at) % ring).reshape(exp_size, CAP, columns)
    back_rows = exchange(mine)
    grad_input = jnp.dot(
        placed_low, back_rows.reshape(-1, columns), preferred_element_type=F32
    ).astype(BF)
    return (grad_input,) + tuple(weight_grads(after(full, mine), input_rows, grad_rows))


def shards(
    queries,
    key_rows,
    value_vector_rows,
    grad_attn,
    moe_input,
    moe_grad,
    expert_ids,
    router_weight,
    gate_weight,
    up_weight,
    down_weight,
):
    tokens, own = queries.shape[0], key_rows.shape[0]
    rows = tokens * queries.shape[1]
    size = queries.shape[2]
    pair = jnp.concatenate([key_rows[:, 0, :], value_vector_rows[:, 0, :]], axis=1)
    flat = key_gather(pair)
    placed_low, got = select(moe_input, moe_grad, expert_ids, router_weight)
    mine = jnp.concatenate([by_head(queries), by_head(grad_attn)], axis=0)
    theirs = beside(mine)
    queries = jnp.concatenate([mine[:rows], theirs[:rows]], axis=0)
    grads = jnp.concatenate([mine[rows:], theirs[rows:]], axis=0)
    input_rows, grad_rows, gate_mat, up_mat, parts = project(
        got, gate_weight, up_weight, down_weight
    )
    onward, back = both_after(*sum_start(parts), theirs)
    stats = attention_stats(own, tokens, queries, grads, after(flat, onward, back))
    onward, back = sum_step(z_move, parts, 0, onward, back)
    onward, back = both_after(onward, back, stats)
    far_stats = beside(stats)
    onward, back = sum_step(z_move, parts, 1, onward, back)
    onward, back = both_after(onward, back, far_stats)
    half = flat.shape[0] // 2
    middle = lax.axis_size("ctx") // 2
    lower = attention_grads(
        own, tokens, 0, queries, grads, after(flat[:half], onward, back), stats, far_stats
    )
    onward, back = sum_step(z_move, parts, 2, onward, back)
    onward, back = both_after(onward, back, *lower)
    both, grad_query = attention_grads(
        own, tokens, middle, queries, grads, after(flat[half:], onward, back), stats, far_stats, lower
    )
    total = after(sum_step(z_move, parts, 3, onward, back), both)
    terms = y_parts(both.reshape(-1, pair.shape[1]))
    other = opposite(total.astype(BF))
    block = act_block(total + other.astype(F32))
    far_query = beside(grad_query[rows:].astype(BF))
    grad_query = (grad_query[:rows] + far_query.astype(F32)).astype(BF)
    blocks = [block] + [None] * 8
    blocks[8], blocks[1] = ring_step(z_move, block, block)
    sums = jnp.sum(after(terms, blocks[8], blocks[1]).astype(F32), axis=0)
    onward, back = both_after(blocks[8], blocks[1], far_query)
    blocks[7], blocks[2] = ring_step(z_move, onward, back)
    sums = ctx_sum(sums, MASKS[3:])
    onward, back = both_after(blocks[7], blocks[2], sums)
    blocks[6], blocks[3] = ring_step(z_move, onward, back)
    sums = ctx_sum(sums, MASKS[2:3])
    onward, back = both_after(blocks[6], blocks[3], sums)
    blocks[4], blocks[5] = ring_last(z_move, onward, back)
    sums = ctx_sum(sums, MASKS[1:2])
    blocks[0] = after(block, sums)
    sums = ctx_sum(sums, MASKS[:1])
    of_experts = finish(blocks, input_rows, grad_rows, gate_mat, up_mat, placed_low)
    grad_query = jnp.swapaxes(grad_query.reshape(-1, tokens, size), 0, 1)
    return (grad_query,) + own_grads(sums) + of_experts


def solution(mesh):
    placed = (
        P("ctx", ("head", "exp"), None),
        P(("ctx", "exp"), "head", None),
        P(("ctx", "exp"), "head", None),
        P("ctx", ("head", "exp"), None),
        P("exp", "ctx"),
        P("exp", "ctx"),
        P("exp", None),
        P("exp", None),
        P("exp", "ctx", None),
        P("exp", "ctx", None),
        P("exp", None, "ctx"),
    )
    return jax.shard_map(
        shards,
        mesh=mesh,
        in_specs=placed,
        out_specs=(
            P("ctx", ("head", "exp"), None),
            P(("ctx", "exp"), "head", None),
            P(("ctx", "exp"), "head", None),
            P("exp", ("ctx", "head")),
            P("exp", "ctx", "head"),
            P("exp", "ctx", "head"),
            P("exp", "head", "ctx"),
        ),
        check_vma=False,
    )
```

```python
import functools

import jax
import jax.numpy as jnp
from jax import lax
from jax.experimental import pallas as pl
from jax.experimental.pallas import tpu as pltpu
from jax.sharding import PartitionSpec as P

CAP = 48
X_HI = 2
X_LO = 2
MASKED = -1e30
MASKS = (4, 2, 8, 1)
BF = jnp.bfloat16
F32 = jnp.float32


def activate(gate_val, up_val, back_val):
    sigmoid_gate = jax.nn.sigmoid(gate_val)
    hidden = (gate_val * sigmoid_gate * up_val).astype(BF)
    d_up = (back_val * gate_val * sigmoid_gate).astype(BF)
    d_gate = (back_val * up_val * sigmoid_gate * (1.0 + gate_val * (1.0 - sigmoid_gate))).astype(BF)
    return (hidden, d_gate, d_up)


def beside(block):
    return lax.ppermute(block, "exp", [(e, e ^ 1) for e in range(lax.axis_size("exp"))])


def z_move(block, step):
    n = lax.axis_size("ctx") // X_HI
    pairs = [(h * n + z, h * n + (z + step) % n) for h in range(X_HI) for z in range(n)]
    return lax.ppermute(block, "ctx", pairs)


def y_groups():
    n = lax.axis_size("exp")
    return [list(range(x, n, X_LO)) for x in range(X_LO)]


def ctx_gather(block):
    copies = jnp.broadcast_to(block[None], (lax.axis_size("ctx"),) + block.shape)
    return lax.all_to_all(copies, "ctx", 0, 0, tiled=True)


def y_gather(block):
    copies = jnp.broadcast_to(block[None], (len(y_groups()[0]),) + block.shape)
    got = lax.all_to_all(copies, "exp", 0, 0, tiled=True, axis_index_groups=y_groups())
    return got.reshape(-1, block.shape[-1])


def y_parts(both):
    parts = both.reshape(len(y_groups()[0]), -1, both.shape[1])
    return lax.all_to_all(parts, "exp", 0, 0, tiled=True, axis_index_groups=y_groups())


def ctx_sum(both, masks):
    for mask in reversed(masks):
        half = both.shape[0] // 2
        sent = both[half:].astype(BF if half >= both.shape[1] // 2 else F32)
        pairs = [(c, c ^ mask) for c in range(lax.axis_size("ctx"))]
        both = both[:half] + lax.ppermute(sent, "ctx", pairs).astype(F32)
    return both


def place_of(apart):
    return sum(apart // mask % 2 * 2**bit for bit, mask in enumerate(MASKS))


def partner(block, mask):
    return lax.ppermute(block, "exp", [(e, e ^ mask) for e in range(lax.axis_size("exp"))])


def exchange(blocks, waits):
    shape = blocks.shape
    bits = shape[0].bit_length() - 1
    for bit in range(bits):
        if bit == bits - 1:
            blocks = after(blocks, waits)
        blocks = blocks.reshape((2**bit, 2, -1) + shape[1:])
        got = partner(blocks[:, 1], 2 ** (bits - 1 - bit))
        blocks = jnp.stack([blocks[:, 0], got], axis=1)
    return blocks.reshape(shape)


def opposite(block):
    n = lax.axis_size("ctx")
    return lax.ppermute(block, "ctx", [(c, (c + n // X_HI) % n) for c in range(n)])


def after(block, *others):
    return lax.optimization_barrier((block,) + others)[0]


def add_low(a, b):
    return (a.astype(F32) + b.astype(F32)).astype(BF)


def sum_start(parts):
    far = len(parts) // 2
    cut = parts[0].shape[1] // 2
    return parts[far][:, :cut], parts[far][:, cut:]


def sum_step(move, parts, step, onward, back):
    n = len(parts)
    far = n // 2
    cut = parts[0].shape[1] // 2
    onward, back = move(onward, 1), move(back, -1)
    ahead, behind = parts[far - 1 - step], parts[(far + 1 + step) % n]
    if step == 0:
        onward = jnp.concatenate([add_low(onward, ahead[:, :cut]), ahead[:, cut:]], axis=1)
        back = jnp.concatenate([behind[:, :cut], add_low(back, behind[:, cut:])], axis=1)
    elif step < far - 1:
        onward, back = add_low(onward, ahead), add_low(back, behind)
    else:
        return onward.astype(F32) + back.astype(F32) + parts[0].astype(F32)
    return onward, back


def ring_step(move, onward, back):
    return move(onward, 1), move(back, -1)


def ring_last(move, onward, back):
    cut = onward.shape[1] // 2
    return move(onward[:, :cut], 1), move(back[:, cut:], -1)


def both_after(onward, back, *others):
    return lax.optimization_barrier((onward, back) + others)[:2]


def turn(blocks, places):
    twice = jnp.concatenate([blocks, blocks], axis=0)
    return lax.dynamic_slice_in_dim(twice, places, blocks.shape[0], 0)


def scores_of(step, own, ctx_size, tokens, here_ref, k, q):
    lanes = q.shape[0]
    found = lax.dot_general(k, q, (((1,), (1,)), ((), ())), preferred_element_type=F32)
    ahead = lax.broadcasted_iota(jnp.int32, (own, lanes), 1) % tokens - lax.broadcasted_iota(
        jnp.int32, (own, lanes), 0
    )
    me, side = here_ref[0], here_ref[1]
    parts = k.shape[0] // own
    masked = []
    for part in range(parts):
        place = step * parts + part
        at = (here_ref[2] + place // ctx_size) * X_LO + side
        start = place % ctx_size * tokens + at * own
        masked.append(
            jnp.where(
                ahead >= start - me * tokens,
                found[part * own : (part + 1) * own] * k.shape[1] ** (-0.5),
                MASKED,
            )
        )
    return jnp.concatenate(masked, axis=0)


def stats_body(own, ctx_size, tokens, here_ref, q_ref, g_ref, kv_ref, stats_ref):
    size = kv_ref.shape[1] // 2
    lanes = q_ref.shape[0]
    chunk = 8 * own

    def one(step, held):
        top, norm, delta = held
        at = pl.ds(pl.multiple_of(step * chunk, chunk), chunk)
        scores = scores_of(step, own, ctx_size, tokens, here_ref, kv_ref[at, :size], q_ref[...])
        dprob = lax.dot_general(
            kv_ref[at, size:], g_ref[...], (((1,), (1,)), ((), ())), preferred_element_type=F32
        )
        scores, dprob = scores.reshape(-1, 8, lanes), dprob.reshape(-1, 8, lanes)
        higher = jnp.maximum(top, jnp.max(scores, axis=0))
        shrink = jnp.exp(top - higher)
        prob = jnp.exp(scores - higher[None])
        norm = norm * shrink + jnp.sum(prob, axis=0)
        delta = delta * shrink + jnp.sum(prob * dprob, axis=0)
        return higher, norm, delta

    zero = jnp.zeros((8, lanes), F32)
    top, norm, delta = lax.fori_loop(0, kv_ref.shape[0] // chunk, one, (zero + MASKED, zero, zero))
    highest = jnp.max(top, axis=0, keepdims=True)
    shrink = jnp.exp(top - highest)
    stats_ref[0:1, :] = highest
    stats_ref[1:2, :] = jnp.sum(norm * shrink, axis=0, keepdims=True)
    stats_ref[2:3, :] = jnp.sum(delta * shrink, axis=0, keepdims=True)
    stats_ref[3:, :] = jnp.zeros((5, lanes), F32)


def grads_body(
    own, ctx_size, tokens, here_ref, q_ref, g_ref, kv_ref, stats_ref, far_ref, *refs
):
    before, (both_ref, dq_ref) = refs[:-2], refs[-2:]
    both_ref[...] = before[0][...] if before else jnp.zeros_like(both_ref)
    size = kv_ref.shape[1] // 2
    lanes = q_ref.shape[0]
    chunk = 8 * own
    far = jnp.concatenate([far_ref[:, lanes // 2 :], far_ref[:, : lanes // 2]], axis=1)
    near = stats_ref[...]
    top = jnp.maximum(near[0:1], far[0:1])
    shrink_near, shrink_far = jnp.exp(near[0:1] - top), jnp.exp(far[0:1] - top)
    inverse = 1.0 / (near[1:2] * shrink_near + far[1:2] * shrink_far)
    delta = (near[2:3] * shrink_near + far[2:3] * shrink_far) * inverse

    def one(step, total):
        at = pl.ds(pl.multiple_of(step * chunk, chunk), chunk)
        k = kv_ref[at, :size]
        scores = scores_of(step, own, ctx_size, tokens, here_ref, k, q_ref[...])
        prob = jnp.exp(scores - top) * inverse
        value = jnp.dot(prob.astype(BF), g_ref[...], preferred_element_type=F32).astype(BF)
        dprob = lax.dot_general(
            kv_ref[at, size:], g_ref[...], (((1,), (1,)), ((), ())), preferred_element_type=F32
        )
        dscore = (prob * (dprob - delta)).astype(BF)
        key = jnp.dot(dscore, q_ref[...], preferred_element_type=F32).astype(BF)
        for part in range(8):
            place = step * 8 + part
            y = here_ref[2] + place // ctx_size
            i = place_of(place % ctx_size ^ here_ref[0])
            piece = slice(part * own, (part + 1) * own)
            both_ref[y, i, :, :size] = key[piece]
            both_ref[y, i, :, size:] = value[piece]
        return total + lax.dot_general(
            k, dscore, (((0,), (0,)), ((), ())), preferred_element_type=F32
        )

    total = lax.fori_loop(0, kv_ref.shape[0] // chunk, one, jnp.zeros((size, lanes), F32))
    total = (total * size ** (-0.5)).T
    dq_ref[...] = total + before[1][...] if before else total


VMEM = pl.BlockSpec(memory_space=pltpu.VMEM)
SMEM = pl.BlockSpec(memory_space=pltpu.SMEM)


def here(first):
    side = lax.axis_index("exp") % X_LO
    return jnp.stack([lax.axis_index("ctx"), side, jnp.int32(first)]).astype(jnp.int32)


def attention_stats(own, tokens, queries, grads, flat):
    keys, lanes = flat.shape[0], queries.shape[0]
    return pl.pallas_call(
        functools.partial(stats_body, own, lax.axis_size("ctx"), tokens),
        out_shape=jax.ShapeDtypeStruct((8, lanes), F32),
        in_specs=[SMEM, VMEM, VMEM, VMEM],
        out_specs=VMEM,
        compiler_params=pltpu.CompilerParams(vmem_limit_bytes=24 * 2**20),
        cost_estimate=pl.CostEstimate(
            flops=4 * keys * lanes * flat.shape[1] // 2,
            bytes_accessed=2 * flat.size,
            transcendentals=keys * lanes,
        ),
        name="attention_stats",
    )(here(0), queries, grads, flat)


def attention_grads(own, tokens, first, queries, grads, flat, stats, far, before=()):
    keys, lanes = flat.shape[0], queries.shape[0]
    size = flat.shape[1] // 2
    rows = lax.axis_size("exp") // X_LO
    return pl.pallas_call(
        functools.partial(grads_body, own, lax.axis_size("ctx"), tokens),
        out_shape=(
            jax.ShapeDtypeStruct((rows, lax.axis_size("ctx"), own, 2 * size), BF),
            jax.ShapeDtypeStruct((lanes, size), F32),
        ),
        in_specs=[SMEM] + [VMEM] * (5 + len(before)),
        out_specs=(VMEM, VMEM),
        compiler_params=pltpu.CompilerParams(vmem_limit_bytes=24 * 2**20),
        cost_estimate=pl.CostEstimate(
            flops=10 * keys * lanes * size,
            bytes_accessed=4 * flat.size,
            transcendentals=keys * lanes,
        ),
        name="attention_grads",
    )(here(first), queries, grads, flat, stats, far, *before)


def by_head(rows):
    return jnp.swapaxes(rows, 0, 1).reshape(-1, rows.shape[2])


def own_grads(both):
    head_dim = both.shape[1] // 2
    grad_key = (both[:, :head_dim] * head_dim ** (-0.5)).astype(BF)[:, None, :]
    grad_value = both[:, head_dim:].astype(BF)[:, None, :]
    return grad_key, grad_value


def select(moe_input, moe_grad, expert_ids, router_weight, near):
    width = moe_input.shape[1]
    exp_size = lax.axis_size("exp")
    labels = lax.axis_index("exp") ^ jnp.arange(exp_size)
    matches = expert_ids[:, :, None] == labels[None, None, :]
    member = jnp.sum(matches.astype(jnp.int32), axis=1)
    weight_row = jnp.sum(jnp.where(matches, router_weight[:, :, None], 0.0), axis=1)
    slot_rank = jnp.cumsum(member, axis=0) - member
    placed = (member[:, :, None] == 1) & (
        slot_rank[:, :, None] == jnp.arange(CAP)[None, None, :]
    )
    slot_weight = jnp.sum(jnp.where(placed, weight_row[:, :, None], 0.0), axis=0)
    placed_low = placed.astype(BF).reshape(-1, exp_size * CAP)
    rows = jnp.concatenate([moe_input, moe_grad], axis=1)
    picked = jnp.einsum("bs,bd->sd", placed_low, rows, preferred_element_type=F32)
    scaled = picked[:, width:] * slot_weight.reshape(-1, 1)
    sent = jnp.concatenate([picked[:, :width].astype(BF), scaled.astype(BF)], axis=1)
    got = exchange(sent.reshape(exp_size, CAP, 2 * width), near)
    return placed_low, got


def project(got, gate_weight, up_weight, down_weight):
    ring = lax.axis_size("ctx") // X_HI
    at = lax.axis_index("ctx") % ring
    half = lax.axis_index("head")
    units = gate_weight.shape[2] // lax.axis_size("head")
    width = got.shape[2] // 2
    got = turn(got.reshape(ring, -1, 2 * width), at).reshape(-1, 2 * width)
    input_rows, grad_rows = got[:, :width], got[:, width:]
    gate_mat = lax.dynamic_slice_in_dim(gate_weight[0], half * units, units, 1)
    up_mat = lax.dynamic_slice_in_dim(up_weight[0], half * units, units, 1)
    down_mat = lax.dynamic_slice_in_dim(down_weight[0], half * units, units, 0)
    gate_part = jnp.dot(input_rows, gate_mat, preferred_element_type=F32).astype(BF)
    up_part = jnp.dot(input_rows, up_mat, preferred_element_type=F32).astype(BF)
    back_part = jnp.einsum("rd,fd->rf", grad_rows, down_mat, preferred_element_type=F32).astype(BF)
    parts = jnp.concatenate([gate_part, up_part, back_part], axis=1).reshape(ring, -1, 3 * units)
    return input_rows, grad_rows, gate_mat, up_mat, [parts[j] for j in range(ring)]


def act_block(total):
    units = total.shape[1] // 3
    hidden, d_gate, d_up = activate(
        total[:, :units], total[:, units : 2 * units], total[:, 2 * units :]
    )
    return jnp.concatenate([hidden, d_gate, d_up], axis=1)


def contrib_body(width, here_ref, gate_ref, up_ref, *refs):
    blocks, (mine_ref, other_ref, full_ref) = refs[:-3], refs[-3:]
    height = blocks[0].shape[0]
    units = full_ref.shape[1] // 3
    row = 0
    halves = [block for block in blocks if block.shape[1] < full_ref.shape[1]]
    for block in blocks:
        if block is halves[0]:
            cut = block.shape[1]
            full_ref[row : row + height, :cut] = block[...]
            continue
        if block is halves[1]:
            full_ref[row : row + height, cut:] = block[...]
        else:
            full_ref[row : row + height, :] = block[...]
        row += height
    across = (((1,), (1,)), ((), ()))
    found = lax.dot_general(
        full_ref[:, units : 2 * units], gate_ref[...], across, preferred_element_type=F32
    ) + lax.dot_general(full_ref[:, 2 * units :], up_ref[...], across, preferred_element_type=F32)
    first = here_ref[0] == 0
    mine = jnp.where(first, found[:, :width], found[:, width:])
    other = jnp.where(first, found[:, width:], found[:, :width]).astype(BF)
    count = mine_ref.shape[0]
    for j in range(count):
        to = (j + here_ref[1]) % count ^ here_ref[2]
        mine_ref[to] = mine[j * height : (j + 1) * height]
        other_ref[to] = other[j * height : (j + 1) * height]


def order_body(here_ref, back_ref, rows_ref):
    count, height, _ = back_ref.shape
    for j in range(count):
        rows_ref[j * height : (j + 1) * height, :] = back_ref[j ^ here_ref[0]]


def ordered(back_rows):
    count, height, columns = back_rows.shape
    return pl.pallas_call(
        order_body,
        out_shape=jax.ShapeDtypeStruct((count * height, columns), BF),
        in_specs=[SMEM, VMEM],
        out_specs=VMEM,
        cost_estimate=pl.CostEstimate(
            flops=0, bytes_accessed=4 * back_rows.size, transcendentals=0
        ),
        name="order_rows",
    )(lax.axis_index("exp").astype(jnp.int32).reshape(1), back_rows)


def weights_body(full_ref, input_ref, grad_ref, gate_ref, up_ref, down_ref):
    units = full_ref.shape[1] // 3
    down = (((0,), (0,)), ((), ()))

    def product(a, b):
        return lax.dot_general(a, b, down, preferred_element_type=F32).astype(BF)

    gate_ref[0] = product(input_ref[...], full_ref[:, units : 2 * units])
    up_ref[0] = product(input_ref[...], full_ref[:, 2 * units :])
    down_ref[0] = product(full_ref[:, :units], grad_ref[...])


def contributions(blocks, gate_mat, up_mat):
    rows = len(blocks) // 2 * 2 * blocks[0].shape[0]
    columns = gate_mat.shape[0] // lax.axis_size("head")
    whole = blocks[0].shape[1]
    count = len(blocks) // 2 * 2
    at = lax.axis_index("ctx") % (lax.axis_size("ctx") // X_HI)
    here = jnp.stack([lax.axis_index("head"), at, lax.axis_index("exp")])
    return pl.pallas_call(
        functools.partial(contrib_body, columns),
        out_shape=(
            jax.ShapeDtypeStruct((count, rows // count, columns), F32),
            jax.ShapeDtypeStruct((count, rows // count, columns), BF),
            jax.ShapeDtypeStruct((rows, whole), BF),
        ),
        in_specs=[SMEM] + [VMEM] * (2 + len(blocks)),
        out_specs=(VMEM,) * 3,
        compiler_params=pltpu.CompilerParams(vmem_limit_bytes=24 * 2**20),
        cost_estimate=pl.CostEstimate(
            flops=4 * rows * whole // 3 * gate_mat.shape[0],
            bytes_accessed=4 * rows * whole,
            transcendentals=0,
        ),
        name="expert_contrib",
    )(here.astype(jnp.int32), gate_mat, up_mat, *blocks)


def weight_grads(full, input_rows, grad_rows):
    units, width = full.shape[1] // 3, input_rows.shape[1]
    return pl.pallas_call(
        weights_body,
        out_shape=(
            jax.ShapeDtypeStruct((1, width, units), BF),
            jax.ShapeDtypeStruct((1, width, units), BF),
            jax.ShapeDtypeStruct((1, units, width), BF),
        ),
        in_specs=[VMEM] * 3,
        out_specs=(VMEM,) * 3,
        compiler_params=pltpu.CompilerParams(vmem_limit_bytes=24 * 2**20),
        cost_estimate=pl.CostEstimate(
            flops=6 * full.shape[0] * units * width,
            bytes_accessed=4 * full.size,
            transcendentals=0,
        ),
        name="expert_weight_grads",
    )(full, input_rows, grad_rows)


def finish(blocks, input_rows, grad_rows, gate_mat, up_mat, placed_low):
    mine, other, full = contributions(blocks, gate_mat, up_mat)
    mine = (mine + lax.ppermute(other, "head", [(0, 1), (1, 0)]).astype(F32)).astype(BF)
    back_rows = lax.all_to_all(mine, "exp", 0, 0, tiled=True)
    grad_input = jnp.dot(placed_low, ordered(back_rows), preferred_element_type=F32).astype(BF)
    return (grad_input,) + tuple(weight_grads(after(full, mine), input_rows, grad_rows))


def shards(
    queries,
    key_rows,
    value_vector_rows,
    grad_attn,
    moe_input,
    moe_grad,
    expert_ids,
    router_weight,
    gate_weight,
    up_weight,
    down_weight,
):
    tokens, own = queries.shape[0], key_rows.shape[0]
    rows = tokens * queries.shape[1]
    size = queries.shape[2]
    pair = jnp.concatenate([key_rows[:, 0, :], value_vector_rows[:, 0, :]], axis=1)
    near = ctx_gather(pair)
    placed_low, got = select(moe_input, moe_grad, expert_ids, router_weight, near)
    flat = y_gather(near)
    mine = jnp.concatenate([by_head(queries), by_head(grad_attn)], axis=0)
    theirs = beside(mine)
    queries = jnp.concatenate([mine[:rows], theirs[:rows]], axis=0)
    grads = jnp.concatenate([mine[rows:], theirs[rows:]], axis=0)
    input_rows, grad_rows, gate_mat, up_mat, parts = project(
        got, gate_weight, up_weight, down_weight
    )
    onward, back = both_after(*sum_start(parts), theirs)
    onward, back = sum_step(z_move, parts, 0, onward, back)
    onward, back = both_after(onward, back, flat)
    stats = attention_stats(own, tokens, queries, grads, after(flat, onward, back))
    onward, back = sum_step(z_move, parts, 1, onward, back)
    onward, back = both_after(onward, back, stats)
    far_stats = beside(stats)
    half = flat.shape[0] // 2
    middle = lax.axis_size("exp") // X_LO // 2
    lower = attention_grads(
        own, tokens, 0, queries, grads, flat[:half], after(stats, onward, back), far_stats
    )
    onward, back = sum_step(z_move, parts, 2, onward, back)
    onward, back = both_after(onward, back, *lower)
    both, grad_query = attention_grads(
        own, tokens, middle, queries, grads, after(flat[half:], onward, back), stats, far_stats, lower
    )
    total = after(sum_step(z_move, parts, 3, onward, back), both)
    terms = y_parts(both.reshape(-1, pair.shape[1]))
    other = opposite(total.astype(BF))
    block = act_block(total + other.astype(F32))
    far_query = beside(grad_query[rows:].astype(BF))
    grad_query = (grad_query[:rows] + far_query.astype(F32)).astype(BF)
    blocks = [block] + [None] * 8
    blocks[8], blocks[1] = ring_step(z_move, block, block)
    sums = jnp.sum(after(terms, blocks[8], blocks[1]).astype(F32), axis=0)
    onward, back = both_after(blocks[8], blocks[1], far_query)
    blocks[7], blocks[2] = ring_step(z_move, onward, back)
    sums = ctx_sum(sums, MASKS[3:])
    onward, back = both_after(blocks[7], blocks[2], sums)
    blocks[6], blocks[3] = ring_step(z_move, onward, back)
    sums = ctx_sum(sums, MASKS[2:3])
    onward, back = both_after(blocks[6], blocks[3], sums)
    blocks[4], blocks[5] = ring_last(z_move, onward, back)
    sums = ctx_sum(sums, MASKS[1:2])
    blocks[0] = after(block, sums)
    sums = ctx_sum(sums, MASKS[:1])
    of_experts = finish(blocks, input_rows, grad_rows, gate_mat, up_mat, placed_low)
    grad_query = jnp.swapaxes(grad_query.reshape(-1, tokens, size), 0, 1)
    return (grad_query,) + own_grads(sums) + of_experts


def solution(mesh):
    placed = (
        P("ctx", ("head", "exp"), None),
        P(("ctx", "exp"), "head", None),
        P(("ctx", "exp"), "head", None),
        P("ctx", ("head", "exp"), None),
        P("exp", "ctx"),
        P("exp", "ctx"),
        P("exp", None),
        P("exp", None),
        P("exp", "ctx", None),
        P("exp", "ctx", None),
        P("exp", None, "ctx"),
    )
    return jax.shard_map(
        shards,
        mesh=mesh,
        in_specs=placed,
        out_specs=(
            P("ctx", ("head", "exp"), None),
            P(("ctx", "exp"), "head", None),
            P(("ctx", "exp"), "head", None),
            P("exp", ("ctx", "head")),
            P("exp", "ctx", "head"),
            P("exp", "ctx", "head"),
            P("exp", "head", "ctx"),
        ),
        check_vma=False,
    )
```

```python
import functools

import jax
import jax.numpy as jnp
from jax import lax
from jax.experimental import pallas as pl
from jax.experimental.pallas import tpu as pltpu
from jax.sharding import PartitionSpec as P

CAP = 48
X_HI = 2
X_LO = 2
MASKED = -1e30
MASKS = (4, 2, 8, 1)
BF = jnp.bfloat16
F32 = jnp.float32


def activate(gate_val, up_val, back_val):
    sigmoid_gate = jax.nn.sigmoid(gate_val)
    hidden = (gate_val * sigmoid_gate * up_val).astype(BF)
    d_up = (back_val * gate_val * sigmoid_gate).astype(BF)
    d_gate = (back_val * up_val * sigmoid_gate * (1.0 + gate_val * (1.0 - sigmoid_gate))).astype(BF)
    return (hidden, d_gate, d_up)


def beside(block):
    return lax.ppermute(block, "exp", [(e, e ^ 1) for e in range(lax.axis_size("exp"))])


def z_move(block, step):
    n = lax.axis_size("ctx") // X_HI
    pairs = [(h * n + z, h * n + (z + step) % n) for h in range(X_HI) for z in range(n)]
    return lax.ppermute(block, "ctx", pairs)


def y_groups():
    n = lax.axis_size("exp")
    return [list(range(x, n, X_LO)) for x in range(X_LO)]


def key_gather(block):
    exps, ctxs = lax.axis_size("exp"), lax.axis_size("ctx")
    groups = [
        [c * exps + y * X_LO + x for y in range(exps // X_LO) for c in range(ctxs)]
        for x in range(X_LO)
    ]
    copies = jnp.broadcast_to(block[None], (len(groups[0]),) + block.shape)
    got = lax.all_to_all(copies, ("ctx", "exp"), 0, 0, tiled=True, axis_index_groups=groups)
    return got.reshape(-1, block.shape[1])


def y_parts(both):
    parts = both.reshape(len(y_groups()[0]), -1, both.shape[1])
    return lax.all_to_all(parts, "exp", 0, 0, tiled=True, axis_index_groups=y_groups())


def ctx_sum(both, masks):
    for mask in reversed(masks):
        half = both.shape[0] // 2
        sent = both[half:].astype(BF if half >= both.shape[1] // 2 else F32)
        pairs = [(c, c ^ mask) for c in range(lax.axis_size("ctx"))]
        both = both[:half] + lax.ppermute(sent, "ctx", pairs).astype(F32)
    return both


def place_of(apart):
    return sum(apart // mask % 2 * 2**bit for bit, mask in enumerate(MASKS))


def partner(block, mask):
    return lax.ppermute(block, "exp", [(e, e ^ mask) for e in range(lax.axis_size("exp"))])


def exchange(blocks):
    shape = blocks.shape
    bits = shape[0].bit_length() - 1
    for bit in range(bits):
        blocks = blocks.reshape((2**bit, 2, -1) + shape[1:])
        got = partner(blocks[:, 1], 2 ** (bits - 1 - bit))
        blocks = jnp.stack([blocks[:, 0], got], axis=1)
    return blocks.reshape(shape)


def opposite(block):
    n = lax.axis_size("ctx")
    return lax.ppermute(block, "ctx", [(c, (c + n // X_HI) % n) for c in range(n)])


def after(block, *others):
    return lax.optimization_barrier((block,) + others)[0]


def add_low(a, b):
    return (a.astype(F32) + b.astype(F32)).astype(BF)


def sum_start(parts):
    far = len(parts) // 2
    cut = parts[0].shape[1] // 2
    return parts[far][:, :cut], parts[far][:, cut:]


def sum_step(move, parts, step, onward, back, waits=()):
    n = len(parts)
    far = n // 2
    cut = parts[0].shape[1] // 2
    onward, back = move(onward, 1), move(back, -1)
    onward, back = both_after(onward, back, *waits)
    ahead, behind = parts[far - 1 - step], parts[(far + 1 + step) % n]
    if step == 0:
        onward = jnp.concatenate([add_low(onward, ahead[:, :cut]), ahead[:, cut:]], axis=1)
        back = jnp.concatenate([behind[:, :cut], add_low(back, behind[:, cut:])], axis=1)
    elif step < far - 1:
        onward, back = add_low(onward, ahead), add_low(back, behind)
    else:
        return onward.astype(F32) + back.astype(F32) + parts[0].astype(F32)
    return onward, back


def ring_step(move, onward, back):
    return move(onward, 1), move(back, -1)


def ring_last(move, onward, back):
    cut = onward.shape[1] // 2
    return move(onward[:, :cut], 1), move(back[:, cut:], -1)


def both_after(onward, back, *others):
    return lax.optimization_barrier((onward, back) + others)[:2]


def turn(blocks, places):
    twice = jnp.concatenate([blocks, blocks], axis=0)
    return lax.dynamic_slice_in_dim(twice, places, blocks.shape[0], 0)


def scores_of(step, own, ctx_size, tokens, here_ref, k, q):
    lanes = q.shape[0]
    found = lax.dot_general(k, q, (((1,), (1,)), ((), ())), preferred_element_type=F32)
    ahead = lax.broadcasted_iota(jnp.int32, (own, lanes), 1) % tokens - lax.broadcasted_iota(
        jnp.int32, (own, lanes), 0
    )
    me, side = here_ref[0], here_ref[1]
    parts = k.shape[0] // own
    masked = []
    for part in range(parts):
        place = step * parts + part
        at = (here_ref[2] + place // ctx_size) * X_LO + side
        start = place % ctx_size * tokens + at * own
        masked.append(
            jnp.where(
                ahead >= start - me * tokens,
                found[part * own : (part + 1) * own] * k.shape[1] ** (-0.5),
                MASKED,
            )
        )
    return jnp.concatenate(masked, axis=0)


def stats_body(own, ctx_size, tokens, here_ref, q_ref, g_ref, kv_ref, stats_ref):
    size = kv_ref.shape[1] // 2
    lanes = q_ref.shape[0]
    chunk = 8 * own

    def one(step, held):
        top, norm, delta = held
        at = pl.ds(pl.multiple_of(step * chunk, chunk), chunk)
        scores = scores_of(step, own, ctx_size, tokens, here_ref, kv_ref[at, :size], q_ref[...])
        dprob = lax.dot_general(
            kv_ref[at, size:], g_ref[...], (((1,), (1,)), ((), ())), preferred_element_type=F32
        )
        scores, dprob = scores.reshape(-1, 8, lanes), dprob.reshape(-1, 8, lanes)
        higher = jnp.maximum(top, jnp.max(scores, axis=0))
        shrink = jnp.exp(top - higher)
        prob = jnp.exp(scores - higher[None])
        norm = norm * shrink + jnp.sum(prob, axis=0)
        delta = delta * shrink + jnp.sum(prob * dprob, axis=0)
        return higher, norm, delta

    zero = jnp.zeros((8, lanes), F32)
    top, norm, delta = lax.fori_loop(0, kv_ref.shape[0] // chunk, one, (zero + MASKED, zero, zero))
    highest = jnp.max(top, axis=0, keepdims=True)
    shrink = jnp.exp(top - highest)
    stats_ref[0:1, :] = highest
    stats_ref[1:2, :] = jnp.sum(norm * shrink, axis=0, keepdims=True)
    stats_ref[2:3, :] = jnp.sum(delta * shrink, axis=0, keepdims=True)
    stats_ref[3:, :] = jnp.zeros((5, lanes), F32)


def grads_body(
    own, ctx_size, tokens, here_ref, q_ref, g_ref, kv_ref, stats_ref, far_ref, *refs
):
    before, (both_ref, dq_ref) = refs[:-2], refs[-2:]
    both_ref[...] = before[0][...] if before else jnp.zeros_like(both_ref)
    size = kv_ref.shape[1] // 2
    lanes = q_ref.shape[0]
    chunk = 8 * own
    far = jnp.concatenate([far_ref[:, lanes // 2 :], far_ref[:, : lanes // 2]], axis=1)
    near = stats_ref[...]
    top = jnp.maximum(near[0:1], far[0:1])
    shrink_near, shrink_far = jnp.exp(near[0:1] - top), jnp.exp(far[0:1] - top)
    inverse = 1.0 / (near[1:2] * shrink_near + far[1:2] * shrink_far)
    delta = (near[2:3] * shrink_near + far[2:3] * shrink_far) * inverse

    def one(step, total):
        at = pl.ds(pl.multiple_of(step * chunk, chunk), chunk)
        k = kv_ref[at, :size]
        scores = scores_of(step, own, ctx_size, tokens, here_ref, k, q_ref[...])
        prob = jnp.exp(scores - top) * inverse
        value = jnp.dot(prob.astype(BF), g_ref[...], preferred_element_type=F32).astype(BF)
        dprob = lax.dot_general(
            kv_ref[at, size:], g_ref[...], (((1,), (1,)), ((), ())), preferred_element_type=F32
        )
        dscore = (prob * (dprob - delta)).astype(BF)
        key = jnp.dot(dscore, q_ref[...], preferred_element_type=F32).astype(BF)
        for part in range(8):
            place = step * 8 + part
            y = here_ref[2] + place // ctx_size
            i = place_of(place % ctx_size ^ here_ref[0])
            piece = slice(part * own, (part + 1) * own)
            both_ref[y, i, :, :size] = key[piece]
            both_ref[y, i, :, size:] = value[piece]
        return total + lax.dot_general(
            k, dscore, (((0,), (0,)), ((), ())), preferred_element_type=F32
        )

    total = lax.fori_loop(0, kv_ref.shape[0] // chunk, one, jnp.zeros((size, lanes), F32))
    total = (total * size ** (-0.5)).T
    dq_ref[...] = total + before[1][...] if before else total


VMEM = pl.BlockSpec(memory_space=pltpu.VMEM)
SMEM = pl.BlockSpec(memory_space=pltpu.SMEM)


def here(first):
    side = lax.axis_index("exp") % X_LO
    return jnp.stack([lax.axis_index("ctx"), side, jnp.int32(first)]).astype(jnp.int32)


def attention_stats(own, tokens, queries, grads, flat):
    keys, lanes = flat.shape[0], queries.shape[0]
    return pl.pallas_call(
        functools.partial(stats_body, own, lax.axis_size("ctx"), tokens),
        out_shape=jax.ShapeDtypeStruct((8, lanes), F32),
        in_specs=[SMEM, VMEM, VMEM, VMEM],
        out_specs=VMEM,
        compiler_params=pltpu.CompilerParams(vmem_limit_bytes=24 * 2**20),
        cost_estimate=pl.CostEstimate(
            flops=4 * keys * lanes * flat.shape[1] // 2,
            bytes_accessed=2 * flat.size,
            transcendentals=keys * lanes,
        ),
        name="attention_stats",
    )(here(0), queries, grads, flat)


def attention_grads(own, tokens, first, queries, grads, flat, stats, far, before=()):
    keys, lanes = flat.shape[0], queries.shape[0]
    size = flat.shape[1] // 2
    rows = lax.axis_size("exp") // X_LO
    return pl.pallas_call(
        functools.partial(grads_body, own, lax.axis_size("ctx"), tokens),
        out_shape=(
            jax.ShapeDtypeStruct((rows, lax.axis_size("ctx"), own, 2 * size), BF),
            jax.ShapeDtypeStruct((lanes, size), F32),
        ),
        in_specs=[SMEM] + [VMEM] * (5 + len(before)),
        out_specs=(VMEM, VMEM),
        compiler_params=pltpu.CompilerParams(vmem_limit_bytes=24 * 2**20),
        cost_estimate=pl.CostEstimate(
            flops=10 * keys * lanes * size,
            bytes_accessed=4 * flat.size,
            transcendentals=keys * lanes,
        ),
        name="attention_grads",
    )(here(first), queries, grads, flat, stats, far, *before)


def by_head(rows):
    return jnp.swapaxes(rows, 0, 1).reshape(-1, rows.shape[2])


def own_grads(both):
    head_dim = both.shape[1] // 2
    grad_key = (both[:, :head_dim] * head_dim ** (-0.5)).astype(BF)[:, None, :]
    grad_value = both[:, head_dim:].astype(BF)[:, None, :]
    return grad_key, grad_value


def select(moe_input, moe_grad, expert_ids, router_weight):
    width = moe_input.shape[1]
    exp_size = lax.axis_size("exp")
    labels = lax.axis_index("exp") ^ jnp.arange(exp_size)
    matches = expert_ids[:, :, None] == labels[None, None, :]
    member = jnp.sum(matches.astype(jnp.int32), axis=1)
    weight_row = jnp.sum(jnp.where(matches, router_weight[:, :, None], 0.0), axis=1)
    slot_rank = jnp.cumsum(member, axis=0) - member
    placed = (member[:, :, None] == 1) & (
        slot_rank[:, :, None] == jnp.arange(CAP)[None, None, :]
    )
    slot_weight = jnp.sum(jnp.where(placed, weight_row[:, :, None], 0.0), axis=0)
    placed_low = placed.astype(BF).reshape(-1, exp_size * CAP)
    rows = jnp.concatenate([moe_input, moe_grad], axis=1)
    picked = jnp.einsum("bs,bd->sd", placed_low, rows, preferred_element_type=F32)
    scaled = picked[:, width:] * slot_weight.reshape(-1, 1)
    sent = jnp.concatenate([picked[:, :width].astype(BF), scaled.astype(BF)], axis=1)
    got = exchange(sent.reshape(exp_size, CAP, 2 * width))
    return placed_low, got


def project(got, gate_weight, up_weight, down_weight):
    ring = lax.axis_size("ctx") // X_HI
    at = lax.axis_index("ctx") % ring
    half = lax.axis_index("head")
    units = gate_weight.shape[2] // lax.axis_size("head")
    width = got.shape[2] // 2
    got = turn(got.reshape(ring, -1, 2 * width), at).reshape(-1, 2 * width)
    input_rows, grad_rows = got[:, :width], got[:, width:]
    gate_mat = lax.dynamic_slice_in_dim(gate_weight[0], half * units, units, 1)
    up_mat = lax.dynamic_slice_in_dim(up_weight[0], half * units, units, 1)
    down_mat = lax.dynamic_slice_in_dim(down_weight[0], half * units, units, 0)
    gate_part = jnp.dot(input_rows, gate_mat, preferred_element_type=F32).astype(BF)
    up_part = jnp.dot(input_rows, up_mat, preferred_element_type=F32).astype(BF)
    back_part = jnp.einsum("rd,fd->rf", grad_rows, down_mat, preferred_element_type=F32).astype(BF)
    parts = jnp.concatenate([gate_part, up_part, back_part], axis=1).reshape(ring, -1, 3 * units)
    return input_rows, grad_rows, gate_mat, up_mat, [parts[j] for j in range(ring)]


def act_block(total):
    units = total.shape[1] // 3
    hidden, d_gate, d_up = activate(
        total[:, :units], total[:, units : 2 * units], total[:, 2 * units :]
    )
    return jnp.concatenate([hidden, d_gate, d_up], axis=1)


def contrib_body(width, here_ref, gate_ref, up_ref, *refs):
    blocks, (mine_ref, other_ref, full_ref) = refs[:-3], refs[-3:]
    height = blocks[0].shape[0]
    units = full_ref.shape[1] // 3
    row = 0
    halves = [block for block in blocks if block.shape[1] < full_ref.shape[1]]
    for block in blocks:
        if block is halves[0]:
            cut = block.shape[1]
            full_ref[row : row + height, :cut] = block[...]
            continue
        if block is halves[1]:
            full_ref[row : row + height, cut:] = block[...]
        else:
            full_ref[row : row + height, :] = block[...]
        row += height
    across = (((1,), (1,)), ((), ()))
    found = lax.dot_general(
        full_ref[:, units : 2 * units], gate_ref[...], across, preferred_element_type=F32
    ) + lax.dot_general(full_ref[:, 2 * units :], up_ref[...], across, preferred_element_type=F32)
    first = here_ref[0] == 0
    mine = jnp.where(first, found[:, :width], found[:, width:])
    other = jnp.where(first, found[:, width:], found[:, :width]).astype(BF)
    count = mine_ref.shape[0]
    for j in range(count):
        to = (j + here_ref[1]) % count ^ here_ref[2]
        mine_ref[to] = mine[j * height : (j + 1) * height]
        other_ref[to] = other[j * height : (j + 1) * height]


def order_body(here_ref, back_ref, rows_ref):
    count, height, _ = back_ref.shape
    for j in range(count):
        rows_ref[j * height : (j + 1) * height, :] = back_ref[j ^ here_ref[0]]


def ordered(back_rows):
    count, height, columns = back_rows.shape
    return pl.pallas_call(
        order_body,
        out_shape=jax.ShapeDtypeStruct((count * height, columns), BF),
        in_specs=[SMEM, VMEM],
        out_specs=VMEM,
        cost_estimate=pl.CostEstimate(
            flops=0, bytes_accessed=4 * back_rows.size, transcendentals=0
        ),
        name="order_rows",
    )(lax.axis_index("exp").astype(jnp.int32).reshape(1), back_rows)


def weights_body(full_ref, input_ref, grad_ref, gate_ref, up_ref, down_ref):
    units = full_ref.shape[1] // 3
    down = (((0,), (0,)), ((), ()))

    def product(a, b):
        return lax.dot_general(a, b, down, preferred_element_type=F32).astype(BF)

    gate_ref[0] = product(input_ref[...], full_ref[:, units : 2 * units])
    up_ref[0] = product(input_ref[...], full_ref[:, 2 * units :])
    down_ref[0] = product(full_ref[:, :units], grad_ref[...])


def contributions(blocks, gate_mat, up_mat):
    rows = len(blocks) // 2 * 2 * blocks[0].shape[0]
    columns = gate_mat.shape[0] // lax.axis_size("head")
    whole = blocks[0].shape[1]
    count = len(blocks) // 2 * 2
    at = lax.axis_index("ctx") % (lax.axis_size("ctx") // X_HI)
    here = jnp.stack([lax.axis_index("head"), at, lax.axis_index("exp")])
    return pl.pallas_call(
        functools.partial(contrib_body, columns),
        out_shape=(
            jax.ShapeDtypeStruct((count, rows // count, columns), F32),
            jax.ShapeDtypeStruct((count, rows // count, columns), BF),
            jax.ShapeDtypeStruct((rows, whole), BF),
        ),
        in_specs=[SMEM] + [VMEM] * (2 + len(blocks)),
        out_specs=(VMEM,) * 3,
        compiler_params=pltpu.CompilerParams(vmem_limit_bytes=24 * 2**20),
        cost_estimate=pl.CostEstimate(
            flops=4 * rows * whole // 3 * gate_mat.shape[0],
            bytes_accessed=4 * rows * whole,
            transcendentals=0,
        ),
        name="expert_contrib",
    )(here.astype(jnp.int32), gate_mat, up_mat, *blocks)


def weight_grads(full, input_rows, grad_rows):
    units, width = full.shape[1] // 3, input_rows.shape[1]
    return pl.pallas_call(
        weights_body,
        out_shape=(
            jax.ShapeDtypeStruct((1, width, units), BF),
            jax.ShapeDtypeStruct((1, width, units), BF),
            jax.ShapeDtypeStruct((1, units, width), BF),
        ),
        in_specs=[VMEM] * 3,
        out_specs=(VMEM,) * 3,
        compiler_params=pltpu.CompilerParams(vmem_limit_bytes=24 * 2**20),
        cost_estimate=pl.CostEstimate(
            flops=6 * full.shape[0] * units * width,
            bytes_accessed=4 * full.size,
            transcendentals=0,
        ),
        name="expert_weight_grads",
    )(full, input_rows, grad_rows)


def finish(blocks, input_rows, grad_rows, gate_mat, up_mat, placed_low):
    mine, other, full = contributions(blocks, gate_mat, up_mat)
    mine = (mine + lax.ppermute(other, "head", [(0, 1), (1, 0)]).astype(F32)).astype(BF)
    back_rows = lax.all_to_all(mine, "exp", 0, 0, tiled=True)
    grad_input = jnp.dot(placed_low, ordered(back_rows), preferred_element_type=F32).astype(BF)
    return (grad_input,) + tuple(weight_grads(after(full, mine), input_rows, grad_rows))


def shards(
    queries,
    key_rows,
    value_vector_rows,
    grad_attn,
    moe_input,
    moe_grad,
    expert_ids,
    router_weight,
    gate_weight,
    up_weight,
    down_weight,
):
    tokens, own = queries.shape[0], key_rows.shape[0]
    rows = tokens * queries.shape[1]
    size = queries.shape[2]
    pair = jnp.concatenate([key_rows[:, 0, :], value_vector_rows[:, 0, :]], axis=1)
    flat = key_gather(pair)
    placed_low, got = select(moe_input, moe_grad, expert_ids, router_weight)
    mine = jnp.concatenate([by_head(queries), by_head(grad_attn)], axis=0)
    theirs = beside(mine)
    queries = jnp.concatenate([mine[:rows], theirs[:rows]], axis=0)
    grads = jnp.concatenate([mine[rows:], theirs[rows:]], axis=0)
    input_rows, grad_rows, gate_mat, up_mat, parts = project(
        got, gate_weight, up_weight, down_weight
    )
    onward, back = both_after(*sum_start(parts), theirs)
    stats = attention_stats(own, tokens, queries, grads, after(flat, onward, back))
    onward, back = sum_step(z_move, parts, 0, onward, back, (stats,))
    far_stats = beside(stats)
    onward, back = sum_step(z_move, parts, 1, onward, back)
    onward, back = both_after(onward, back, far_stats)
    half = flat.shape[0] // 2
    middle = lax.axis_size("exp") // X_LO // 2
    lower = attention_grads(
        own, tokens, 0, queries, grads, flat[:half], after(stats, onward, back), far_stats
    )
    onward, back = sum_step(z_move, parts, 2, onward, back)
    onward, back = both_after(onward, back, *lower)
    both, grad_query = attention_grads(
        own, tokens, middle, queries, grads, after(flat[half:], onward, back), stats, far_stats, lower
    )
    total = after(sum_step(z_move, parts, 3, onward, back), both)
    terms = y_parts(both.reshape(-1, pair.shape[1]))
    other = opposite(total.astype(BF))
    block = act_block(total + other.astype(F32))
    far_query = beside(grad_query[rows:].astype(BF))
    grad_query = (grad_query[:rows] + far_query.astype(F32)).astype(BF)
    blocks = [block] + [None] * 8
    blocks[8], blocks[1] = ring_step(z_move, block, block)
    sums = jnp.sum(after(terms, blocks[8], blocks[1]).astype(F32), axis=0)
    onward, back = both_after(blocks[8], blocks[1], far_query)
    blocks[7], blocks[2] = ring_step(z_move, onward, back)
    sums = ctx_sum(sums, MASKS[3:])
    onward, back = both_after(blocks[7], blocks[2], sums)
    blocks[6], blocks[3] = ring_step(z_move, onward, back)
    sums = ctx_sum(sums, MASKS[2:3])
    onward, back = both_after(blocks[6], blocks[3], sums)
    blocks[4], blocks[5] = ring_last(z_move, onward, back)
    sums = ctx_sum(sums, MASKS[1:2])
    blocks[0] = after(block, sums)
    sums = ctx_sum(sums, MASKS[:1])
    of_experts = finish(blocks, input_rows, grad_rows, gate_mat, up_mat, placed_low)
    grad_query = jnp.swapaxes(grad_query.reshape(-1, tokens, size), 0, 1)
    return (grad_query,) + own_grads(sums) + of_experts


def solution(mesh):
    placed = (
        P("ctx", ("head", "exp"), None),
        P(("ctx", "exp"), "head", None),
        P(("ctx", "exp"), "head", None),
        P("ctx", ("head", "exp"), None),
        P("exp", "ctx"),
        P("exp", "ctx"),
        P("exp", None),
        P("exp", None),
        P("exp", "ctx", None),
        P("exp", "ctx", None),
        P("exp", None, "ctx"),
    )
    return jax.shard_map(
        shards,
        mesh=mesh,
        in_specs=placed,
        out_specs=(
            P("ctx", ("head", "exp"), None),
            P(("ctx", "exp"), "head", None),
            P(("ctx", "exp"), "head", None),
            P("exp", ("ctx", "head")),
            P("exp", "ctx", "head"),
            P("exp", "ctx", "head"),
            P("exp", "head", "ctx"),
        ),
        check_vma=False,
    )
```

```python
import functools

import jax
import jax.numpy as jnp
from jax import lax
from jax.experimental import pallas as pl
from jax.experimental.pallas import tpu as pltpu
from jax.sharding import PartitionSpec as P

CAP = 48
X_HI = 2
X_LO = 2
MASKED = -1e30
MASKS = (4, 2, 8, 1)
BF = jnp.bfloat16
F32 = jnp.float32


def activate(gate_val, up_val, back_val):
    sigmoid_gate = jax.nn.sigmoid(gate_val)
    hidden = (gate_val * sigmoid_gate * up_val).astype(BF)
    d_up = (back_val * gate_val * sigmoid_gate).astype(BF)
    d_gate = (back_val * up_val * sigmoid_gate * (1.0 + gate_val * (1.0 - sigmoid_gate))).astype(BF)
    return (hidden, d_gate, d_up)


def beside(block):
    return lax.ppermute(block, "exp", [(e, e ^ 1) for e in range(lax.axis_size("exp"))])


def z_move(block, step):
    n = lax.axis_size("ctx") // X_HI
    pairs = [(h * n + z, h * n + (z + step) % n) for h in range(X_HI) for z in range(n)]
    return lax.ppermute(block, "ctx", pairs)


def key_groups():
    exps = lax.axis_size("exp")
    pairs = lax.axis_size("ctx") * exps
    return [[i for i in range(pairs) if i % X_LO == x] for x in range(X_LO)]


def key_gather(block):
    copies = jnp.broadcast_to(block[None], (len(key_groups()[0]),) + block.shape)
    got = lax.all_to_all(
        copies, ("ctx", "exp"), 0, 0, tiled=True, axis_index_groups=key_groups()
    )
    return got.reshape(-1, block.shape[1])


def y_parts(both):
    n = lax.axis_size("exp")
    groups = [list(range(x, n, X_LO)) for x in range(X_LO)]
    parts = both.reshape(n // X_LO, -1, both.shape[1])
    return lax.all_to_all(parts, "exp", 0, 0, tiled=True, axis_index_groups=groups)


def ctx_sum(both, masks):
    for mask in reversed(masks):
        half = both.shape[0] // 2
        sent = both[half:].astype(BF if half >= both.shape[1] // 2 else F32)
        pairs = [(c, c ^ mask) for c in range(lax.axis_size("ctx"))]
        both = both[:half] + lax.ppermute(sent, "ctx", pairs).astype(F32)
    return both


def place_of(apart):
    return sum(apart // mask % 2 * 2**bit for bit, mask in enumerate(MASKS))


def partner(block, mask):
    return lax.ppermute(block, "exp", [(e, e ^ mask) for e in range(lax.axis_size("exp"))])


def exchange(blocks):
    shape = blocks.shape
    bits = shape[0].bit_length() - 1
    for bit in range(bits):
        middle = blocks
        blocks = blocks.reshape((2**bit, 2, -1) + shape[1:])
        got = partner(blocks[:, 1], 2 ** (bits - 1 - bit))
        blocks = jnp.stack([blocks[:, 0], got], axis=1)
    return blocks.reshape(shape), middle


def opposite(block):
    n = lax.axis_size("ctx")
    return lax.ppermute(block, "ctx", [(c, (c + n // X_HI) % n) for c in range(n)])


def after(block, *others):
    return lax.optimization_barrier((block,) + others)[0]


def add_low(a, b):
    return (a.astype(F32) + b.astype(F32)).astype(BF)


def sum_start(parts):
    far = len(parts) // 2
    cut = parts[0].shape[1] // 2
    return parts[far][:, :cut], parts[far][:, cut:]


def sum_step(move, parts, step, onward, back, waits=()):
    n = len(parts)
    far = n // 2
    cut = parts[0].shape[1] // 2
    onward, back = move(onward, 1), move(back, -1)
    onward, back = both_after(onward, back, *waits)
    ahead, behind = parts[far - 1 - step], parts[(far + 1 + step) % n]
    if step == 0:
        onward = jnp.concatenate([add_low(onward, ahead[:, :cut]), ahead[:, cut:]], axis=1)
        back = jnp.concatenate([behind[:, :cut], add_low(back, behind[:, cut:])], axis=1)
    elif step < far - 1:
        onward, back = add_low(onward, ahead), add_low(back, behind)
    else:
        return onward.astype(F32) + back.astype(F32) + parts[0].astype(F32)
    return onward, back


def ring_step(move, onward, back):
    return move(onward, 1), move(back, -1)


def ring_last(move, onward, back):
    cut = onward.shape[1] // 2
    return move(onward[:, :cut], 1), move(back[:, cut:], -1)


def both_after(onward, back, *others):
    return lax.optimization_barrier((onward, back) + others)[:2]


def turn(blocks, places):
    twice = jnp.concatenate([blocks, blocks], axis=0)
    return lax.dynamic_slice_in_dim(twice, places, blocks.shape[0], 0)


def scores_of(step, own, rows, tokens, here_ref, k, q):
    lanes = q.shape[0]
    found = lax.dot_general(k, q, (((1,), (1,)), ((), ())), preferred_element_type=F32)
    ahead = lax.broadcasted_iota(jnp.int32, (own, lanes), 1) % tokens - lax.broadcasted_iota(
        jnp.int32, (own, lanes), 0
    )
    me, side = here_ref[0], here_ref[1]
    parts = k.shape[0] // own
    masked = []
    for part in range(parts):
        place = step * parts + part
        start = (here_ref[2] + place // rows) * tokens + (place % rows * X_LO + side) * own
        masked.append(
            jnp.where(
                ahead >= start - me * tokens,
                found[part * own : (part + 1) * own] * k.shape[1] ** (-0.5),
                MASKED,
            )
        )
    return jnp.concatenate(masked, axis=0)


def stats_body(own, rows, tokens, here_ref, q_ref, g_ref, kv_ref, stats_ref):
    size = kv_ref.shape[1] // 2
    lanes = q_ref.shape[0]
    chunk = 8 * own

    def one(step, held):
        top, norm, delta = held
        at = pl.ds(pl.multiple_of(step * chunk, chunk), chunk)
        scores = scores_of(step, own, rows, tokens, here_ref, kv_ref[at, :size], q_ref[...])
        dprob = lax.dot_general(
            kv_ref[at, size:], g_ref[...], (((1,), (1,)), ((), ())), preferred_element_type=F32
        )
        scores, dprob = scores.reshape(-1, 8, lanes), dprob.reshape(-1, 8, lanes)
        higher = jnp.maximum(top, jnp.max(scores, axis=0))
        shrink = jnp.exp(top - higher)
        prob = jnp.exp(scores - higher[None])
        norm = norm * shrink + jnp.sum(prob, axis=0)
        delta = delta * shrink + jnp.sum(prob * dprob, axis=0)
        return higher, norm, delta

    zero = jnp.zeros((8, lanes), F32)
    top, norm, delta = lax.fori_loop(0, kv_ref.shape[0] // chunk, one, (zero + MASKED, zero, zero))
    highest = jnp.max(top, axis=0, keepdims=True)
    shrink = jnp.exp(top - highest)
    stats_ref[0:1, :] = highest
    stats_ref[1:2, :] = jnp.sum(norm * shrink, axis=0, keepdims=True)
    stats_ref[2:3, :] = jnp.sum(delta * shrink, axis=0, keepdims=True)
    stats_ref[3:, :] = jnp.zeros((5, lanes), F32)


def grads_body(
    own, rows, tokens, here_ref, q_ref, g_ref, kv_ref, stats_ref, far_ref, *refs
):
    before, (both_ref, dq_ref) = refs[:-2], refs[-2:]
    both_ref[...] = before[0][...] if before else jnp.zeros_like(both_ref)
    size = kv_ref.shape[1] // 2
    lanes = q_ref.shape[0]
    chunk = 8 * own
    far = jnp.concatenate([far_ref[:, lanes // 2 :], far_ref[:, : lanes // 2]], axis=1)
    near = stats_ref[...]
    top = jnp.maximum(near[0:1], far[0:1])
    shrink_near, shrink_far = jnp.exp(near[0:1] - top), jnp.exp(far[0:1] - top)
    inverse = 1.0 / (near[1:2] * shrink_near + far[1:2] * shrink_far)
    delta = (near[2:3] * shrink_near + far[2:3] * shrink_far) * inverse

    def one(step, total):
        at = pl.ds(pl.multiple_of(step * chunk, chunk), chunk)
        k = kv_ref[at, :size]
        scores = scores_of(step, own, rows, tokens, here_ref, k, q_ref[...])
        prob = jnp.exp(scores - top) * inverse
        value = jnp.dot(prob.astype(BF), g_ref[...], preferred_element_type=F32).astype(BF)
        dprob = lax.dot_general(
            kv_ref[at, size:], g_ref[...], (((1,), (1,)), ((), ())), preferred_element_type=F32
        )
        dscore = (prob * (dprob - delta)).astype(BF)
        key = jnp.dot(dscore, q_ref[...], preferred_element_type=F32).astype(BF)
        for part in range(8):
            place = step * 8 + part
            i = place_of((here_ref[2] + place // rows) ^ here_ref[0])
            piece = slice(part * own, (part + 1) * own)
            both_ref[place % rows, i, :, :size] = key[piece]
            both_ref[place % rows, i, :, size:] = value[piece]
        return total + lax.dot_general(
            k, dscore, (((0,), (0,)), ((), ())), preferred_element_type=F32
        )

    total = lax.fori_loop(0, kv_ref.shape[0] // chunk, one, jnp.zeros((size, lanes), F32))
    total = (total * size ** (-0.5)).T
    dq_ref[...] = total + before[1][...] if before else total


VMEM = pl.BlockSpec(memory_space=pltpu.VMEM)
SMEM = pl.BlockSpec(memory_space=pltpu.SMEM)


def here(first):
    side = lax.axis_index("exp") % X_LO
    return jnp.stack([lax.axis_index("ctx"), side, jnp.int32(first)]).astype(jnp.int32)


def attention_stats(own, tokens, queries, grads, flat):
    keys, lanes = flat.shape[0], queries.shape[0]
    return pl.pallas_call(
        functools.partial(stats_body, own, lax.axis_size("exp") // X_LO, tokens),
        out_shape=jax.ShapeDtypeStruct((8, lanes), F32),
        in_specs=[SMEM, VMEM, VMEM, VMEM],
        out_specs=VMEM,
        compiler_params=pltpu.CompilerParams(vmem_limit_bytes=24 * 2**20),
        cost_estimate=pl.CostEstimate(
            flops=4 * keys * lanes * flat.shape[1] // 2,
            bytes_accessed=2 * flat.size,
            transcendentals=keys * lanes,
        ),
        name="attention_stats",
    )(here(0), queries, grads, flat)


def attention_grads(own, tokens, first, queries, grads, flat, stats, far, before=()):
    keys, lanes = flat.shape[0], queries.shape[0]
    size = flat.shape[1] // 2
    rows = lax.axis_size("exp") // X_LO
    return pl.pallas_call(
        functools.partial(grads_body, own, rows, tokens),
        out_shape=(
            jax.ShapeDtypeStruct((rows, lax.axis_size("ctx"), own, 2 * size), BF),
            jax.ShapeDtypeStruct((lanes, size), F32),
        ),
        in_specs=[SMEM] + [VMEM] * (5 + len(before)),
        out_specs=(VMEM, VMEM),
        compiler_params=pltpu.CompilerParams(vmem_limit_bytes=24 * 2**20),
        cost_estimate=pl.CostEstimate(
            flops=10 * keys * lanes * size,
            bytes_accessed=4 * flat.size,
            transcendentals=keys * lanes,
        ),
        name="attention_grads",
    )(here(first), queries, grads, flat, stats, far, *before)


def by_head(rows):
    return jnp.swapaxes(rows, 0, 1).reshape(-1, rows.shape[2])


def own_grads(both):
    head_dim = both.shape[1] // 2
    grad_key = (both[:, :head_dim] * head_dim ** (-0.5)).astype(BF)[:, None, :]
    grad_value = both[:, head_dim:].astype(BF)[:, None, :]
    return grad_key, grad_value


def select(moe_input, moe_grad, expert_ids, router_weight):
    width = moe_input.shape[1]
    exp_size = lax.axis_size("exp")
    labels = lax.axis_index("exp") ^ jnp.arange(exp_size)
    matches = expert_ids[:, :, None] == labels[None, None, :]
    member = jnp.sum(matches.astype(jnp.int32), axis=1)
    weight_row = jnp.sum(jnp.where(matches, router_weight[:, :, None], 0.0), axis=1)
    slot_rank = jnp.cumsum(member, axis=0) - member
    placed = (member[:, :, None] == 1) & (
        slot_rank[:, :, None] == jnp.arange(CAP)[None, None, :]
    )
    slot_weight = jnp.sum(jnp.where(placed, weight_row[:, :, None], 0.0), axis=0)
    placed_low = placed.astype(BF).reshape(-1, exp_size * CAP)
    rows = jnp.concatenate([moe_input, moe_grad], axis=1)
    picked = jnp.einsum("bs,bd->sd", placed_low, rows, preferred_element_type=F32)
    scaled = picked[:, width:] * slot_weight.reshape(-1, 1)
    sent = jnp.concatenate([picked[:, :width].astype(BF), scaled.astype(BF)], axis=1)
    got, middle = exchange(sent.reshape(exp_size, CAP, 2 * width))
    return placed_low, got, middle


def project(got, gate_weight, up_weight, down_weight):
    ring = lax.axis_size("ctx") // X_HI
    at = lax.axis_index("ctx") % ring
    half = lax.axis_index("head")
    units = gate_weight.shape[2] // lax.axis_size("head")
    width = got.shape[2] // 2
    got = turn(got.reshape(ring, -1, 2 * width), at).reshape(-1, 2 * width)
    input_rows, grad_rows = got[:, :width], got[:, width:]
    gate_mat = lax.dynamic_slice_in_dim(gate_weight[0], half * units, units, 1)
    up_mat = lax.dynamic_slice_in_dim(up_weight[0], half * units, units, 1)
    down_mat = lax.dynamic_slice_in_dim(down_weight[0], half * units, units, 0)
    gate_part = jnp.dot(input_rows, gate_mat, preferred_element_type=F32).astype(BF)
    up_part = jnp.dot(input_rows, up_mat, preferred_element_type=F32).astype(BF)
    back_part = jnp.einsum("rd,fd->rf", grad_rows, down_mat, preferred_element_type=F32).astype(BF)
    parts = jnp.concatenate([gate_part, up_part, back_part], axis=1).reshape(ring, -1, 3 * units)
    return input_rows, grad_rows, gate_mat, up_mat, [parts[j] for j in range(ring)]


def act_block(total):
    units = total.shape[1] // 3
    hidden, d_gate, d_up = activate(
        total[:, :units], total[:, units : 2 * units], total[:, 2 * units :]
    )
    return jnp.concatenate([hidden, d_gate, d_up], axis=1)


def contrib_body(width, half_ref, gate_ref, up_ref, *refs):
    blocks, (mine_ref, other_ref, full_ref) = refs[:-3], refs[-3:]
    height = blocks[0].shape[0]
    units = full_ref.shape[1] // 3
    row = 0
    halves = [block for block in blocks if block.shape[1] < full_ref.shape[1]]
    for block in blocks:
        if block is halves[0]:
            cut = block.shape[1]
            full_ref[row : row + height, :cut] = block[...]
            continue
        if block is halves[1]:
            full_ref[row : row + height, cut:] = block[...]
        else:
            full_ref[row : row + height, :] = block[...]
        row += height
    across = (((1,), (1,)), ((), ()))
    found = lax.dot_general(
        full_ref[:, units : 2 * units], gate_ref[...], across, preferred_element_type=F32
    ) + lax.dot_general(full_ref[:, 2 * units :], up_ref[...], across, preferred_element_type=F32)
    first = half_ref[0] == 0
    mine_ref[...] = jnp.where(first, found[:, :width], found[:, width:])
    other_ref[...] = jnp.where(first, found[:, width:], found[:, :width]).astype(BF)


def weights_body(full_ref, input_ref, grad_ref, gate_ref, up_ref, down_ref):
    units = full_ref.shape[1] // 3
    down = (((0,), (0,)), ((), ()))

    def product(a, b):
        return lax.dot_general(a, b, down, preferred_element_type=F32).astype(BF)

    gate_ref[0] = product(input_ref[...], full_ref[:, units : 2 * units])
    up_ref[0] = product(input_ref[...], full_ref[:, 2 * units :])
    down_ref[0] = product(full_ref[:, :units], grad_ref[...])


def contributions(blocks, gate_mat, up_mat):
    rows = len(blocks) // 2 * 2 * blocks[0].shape[0]
    columns = gate_mat.shape[0] // lax.axis_size("head")
    whole = blocks[0].shape[1]
    return pl.pallas_call(
        functools.partial(contrib_body, columns),
        out_shape=(
            jax.ShapeDtypeStruct((rows, columns), F32),
            jax.ShapeDtypeStruct((rows, columns), BF),
            jax.ShapeDtypeStruct((rows, whole), BF),
        ),
        in_specs=[SMEM] + [VMEM] * (2 + len(blocks)),
        out_specs=(VMEM,) * 3,
        compiler_params=pltpu.CompilerParams(vmem_limit_bytes=24 * 2**20),
        cost_estimate=pl.CostEstimate(
            flops=4 * rows * whole // 3 * gate_mat.shape[0],
            bytes_accessed=4 * rows * whole,
            transcendentals=0,
        ),
        name="expert_contrib",
    )(lax.axis_index("head").astype(jnp.int32).reshape(1), gate_mat, up_mat, *blocks)


def weight_grads(full, input_rows, grad_rows):
    units, width = full.shape[1] // 3, input_rows.shape[1]
    return pl.pallas_call(
        weights_body,
        out_shape=(
            jax.ShapeDtypeStruct((1, width, units), BF),
            jax.ShapeDtypeStruct((1, width, units), BF),
            jax.ShapeDtypeStruct((1, units, width), BF),
        ),
        in_specs=[VMEM] * 3,
        out_specs=(VMEM,) * 3,
        compiler_params=pltpu.CompilerParams(vmem_limit_bytes=24 * 2**20),
        cost_estimate=pl.CostEstimate(
            flops=6 * full.shape[0] * units * width,
            bytes_accessed=4 * full.size,
            transcendentals=0,
        ),
        name="expert_weight_grads",
    )(full, input_rows, grad_rows)


def finish(blocks, input_rows, grad_rows, gate_mat, up_mat, placed_low):
    exp_size = lax.axis_size("exp")
    ring = lax.axis_size("ctx") // X_HI
    at = lax.axis_index("ctx") % ring
    mine, other, full = contributions(blocks, gate_mat, up_mat)
    columns = mine.shape[1]
    mine = (mine + lax.ppermute(other, "head", [(0, 1), (1, 0)]).astype(F32)).astype(BF)
    mine = turn(mine.reshape(ring, -1, columns), (ring - at) % ring).reshape(exp_size, CAP, columns)
    back_rows, _ = exchange(mine)
    grad_input = jnp.dot(
        placed_low, back_rows.reshape(-1, columns), preferred_element_type=F32
    ).astype(BF)
    return (grad_input,) + tuple(weight_grads(after(full, mine), input_rows, grad_rows))


def shards(
    queries,
    key_rows,
    value_vector_rows,
    grad_attn,
    moe_input,
    moe_grad,
    expert_ids,
    router_weight,
    gate_weight,
    up_weight,
    down_weight,
):
    tokens, own = queries.shape[0], key_rows.shape[0]
    rows = tokens * queries.shape[1]
    size = queries.shape[2]
    pair = jnp.concatenate([key_rows[:, 0, :], value_vector_rows[:, 0, :]], axis=1)
    placed_low, got, middle = select(moe_input, moe_grad, expert_ids, router_weight)
    flat = key_gather(after(pair, middle))
    mine = jnp.concatenate([by_head(queries), by_head(grad_attn)], axis=0)
    theirs = beside(mine)
    queries = jnp.concatenate([mine[:rows], theirs[:rows]], axis=0)
    grads = jnp.concatenate([mine[rows:], theirs[rows:]], axis=0)
    input_rows, grad_rows, gate_mat, up_mat, parts = project(
        got, gate_weight, up_weight, down_weight
    )
    onward, back = both_after(*sum_start(parts), theirs)
    onward, back = sum_step(z_move, parts, 0, onward, back)
    stats = attention_stats(own, tokens, queries, grads, after(flat, onward, back))
    onward, back = sum_step(z_move, parts, 1, onward, back, (stats,))
    far_stats = beside(stats)
    half = flat.shape[0] // 2
    middle = lax.axis_size("ctx") // 2
    lower = attention_grads(
        own, tokens, 0, queries, grads, flat[:half], after(stats, onward, back), far_stats
    )
    onward, back = sum_step(z_move, parts, 2, onward, back)
    onward, back = both_after(onward, back, *lower)
    both, grad_query = attention_grads(
        own, tokens, middle, queries, grads, after(flat[half:], onward, back), stats, far_stats, lower
    )
    total = after(sum_step(z_move, parts, 3, onward, back), both)
    terms = y_parts(both.reshape(-1, pair.shape[1]))
    other = opposite(total.astype(BF))
    block = act_block(total + other.astype(F32))
    far_query = beside(grad_query[rows:].astype(BF))
    grad_query = (grad_query[:rows] + far_query.astype(F32)).astype(BF)
    blocks = [block] + [None] * 8
    blocks[8], blocks[1] = ring_step(z_move, block, block)
    sums = jnp.sum(after(terms, blocks[8], blocks[1]).astype(F32), axis=0)
    onward, back = both_after(blocks[8], blocks[1], far_query)
    blocks[7], blocks[2] = ring_step(z_move, onward, back)
    sums = ctx_sum(sums, MASKS[3:])
    onward, back = both_after(blocks[7], blocks[2], sums)
    blocks[6], blocks[3] = ring_step(z_move, onward, back)
    sums = ctx_sum(sums, MASKS[2:3])
    onward, back = both_after(blocks[6], blocks[3], sums)
    blocks[4], blocks[5] = ring_last(z_move, onward, back)
    sums = ctx_sum(sums, MASKS[1:2])
    blocks[0] = after(block, sums)
    sums = ctx_sum(sums, MASKS[:1])
    of_experts = finish(blocks, input_rows, grad_rows, gate_mat, up_mat, placed_low)
    grad_query = jnp.swapaxes(grad_query.reshape(-1, tokens, size), 0, 1)
    return (grad_query,) + own_grads(sums) + of_experts


def solution(mesh):
    placed = (
        P("ctx", ("head", "exp"), None),
        P(("ctx", "exp"), "head", None),
        P(("ctx", "exp"), "head", None),
        P("ctx", ("head", "exp"), None),
        P("exp", "ctx"),
        P("exp", "ctx"),
        P("exp", None),
        P("exp", None),
        P("exp", "ctx", None),
        P("exp", "ctx", None),
        P("exp", None, "ctx"),
    )
    return jax.shard_map(
        shards,
        mesh=mesh,
        in_specs=placed,
        out_specs=(
            P("ctx", ("head", "exp"), None),
            P(("ctx", "exp"), "head", None),
            P(("ctx", "exp"), "head", None),
            P("exp", ("ctx", "head")),
            P("exp", "ctx", "head"),
            P("exp", "ctx", "head"),
            P("exp", "head", "ctx"),
        ),
        check_vma=False,
    )
```
